32 devices in a mesh: wide: 8 (over z, y), narrow: 4 (over x, core).
Axes of the slice: x: 2, y: 2, z: 4, core: 2. Of those that a mesh axis runs over, the one named last changes fastest.
Arguments:
- charges: float32 [2, 2097152], P(None, ('wide', 'narrow')), may hold values from -6 to 6
- source_order: int32 [2097152], P(('wide', 'narrow')), may hold values from 0 to 7, as said below
- velocity: bfloat16 [262144], P(('wide', 'narrow')), may hold values from 0.5 to 4
- leaf_weight: bfloat16 [16, 128], replicated, may hold values from -1.5 to 1.5
- mixing: bfloat16 [8, 2, 2, 128, 128], replicated, may hold values from -0.375 to 0.375
- eval_weight: bfloat16 [128, 16], replicated, may hold values from -0.5 to 0.5
- target_order: int32 [2097152], P(('wide', 'narrow')), may hold values from 0 to 7, as said below
Outputs:
- potentials: float32 [2, 2097152], P(None, ('wide', 'narrow'))
The draws below stay inside these ranges and needn't reach their ends.
Inputs may be any that keep to these rules, and one draw needn't show every extreme that they name: `source_order`: each aligned block of 8 entries is a permutation of 0 .. 7. `target_order`: each aligned block of 8 entries is a permutation of 0 .. 7.
All inputs are finite; a program needn't handle non-finite values.
Results may differ from the reference program's by a relative error of at most 0.02.
Values may be sent and summed in bfloat16 or wider, within the bound.
No kernel may reach another device: no remote copies, remote signals or barrier semaphores. Data moves between devices by JAX's collectives and lax.ppermute only.
A program may use at most 128 MiB of HBM per device.

```python
import math
import jax
import jax.numpy as jnp

WIDTH = 128
LEAF = 8
BOX = 8192
LOCAL_LEVELS = 3
LEVELS = 8
NBOX = 262144
NSRC = 2097152


def block_permutation(seed_key, blocks, length):
    scores = jax.random.randint(seed_key, (blocks, length), 0, 1 << 20, dtype=jnp.int32)
    scores = scores * length + jnp.arange(length, dtype=jnp.int32)[None, :]
    return jnp.argsort(scores, axis=1, stable=True).reshape(-1).astype(jnp.int32)


def draw_source_order(key, part):
    return block_permutation(jax.random.fold_in(key, 11), NSRC // LEAF, LEAF)


def draw_target_order(key, part):
    return block_permutation(jax.random.fold_in(key, 29), NSRC // LEAF, LEAF)


def levels(own_key, shape, split, low, largest):
    factor_of = 1.0
    for position, shards_of in split:
        steps = jax.random.uniform(jax.random.fold_in(jax.random.fold_in(own_key, 6), position), (shards_of,), jnp.float32, low / len(split), largest / len(split))
        factor_of = factor_of * jnp.repeat(jnp.exp(steps), shape[position] // shards_of).reshape((-1,) + (1,) * (len(shape) - 1 - position))
    return factor_of


def centred(own_key, shape, spread, limit, cuts=(), kind=jnp.bfloat16):
    factor_of = levels(own_key, shape, cuts, -0.22, 0.18) if cuts else 1.0
    result = jax.random.normal(own_key, shape, jnp.float32) * spread * factor_of
    return jnp.minimum(jnp.maximum(result, -limit), limit).astype(kind)


def setup_inputs(seed: int = 0) -> dict:
    streams_of = jax.random.split(jax.random.key(seed), 8)
    charges = centred(streams_of[0], (2, NSRC), 1.0, 6.0, ((1, 32),), jnp.float32)
    source_order = draw_source_order(jax.random.fold_in(streams_of[7], 71), 0)
    velocity = jnp.clip(jnp.exp(math.log(4.0) - 2.0794415 * jax.random.uniform(streams_of[2], (NBOX,), jnp.float32) ** levels(streams_of[2], (NBOX,), ((0, 32),), -0.2, 0.2)), 0.5, 4.0).astype(jnp.bfloat16)
    leaf_weight = centred(streams_of[3], (2 * LEAF, WIDTH), (2 * LEAF) ** -0.5, 1.5)
    mixing = centred(streams_of[4], (LEVELS, 2, 2, WIDTH, WIDTH), (2 * WIDTH) ** -0.5, 0.375)
    eval_weight = centred(streams_of[5], (WIDTH, 2 * LEAF), WIDTH ** -0.5, 0.5)
    target_order = draw_target_order(jax.random.fold_in(streams_of[7], 71), 0)
    return dict(charges=charges, source_order=source_order, velocity=velocity, leaf_weight=leaf_weight, mixing=mixing, eval_weight=eval_weight, target_order=target_order)


def rotate(pre, speeds, section_no):
    rank = pre.shape[1] // 2
    nodes = jnp.cos(math.pi * (jnp.arange(rank, dtype=jnp.float32) + 0.5) / rank)
    theta = (math.pi * (section_no + 1)) * speeds.astype(jnp.float32)[:, None] * nodes[None, :]
    cosine = jnp.cos(theta)
    sine = jnp.sin(theta)
    real_part = pre[:, :rank]
    imag_part = pre[:, rank:]
    return jnp.concatenate([real_part * cosine - imag_part * sine, real_part * sine + imag_part * cosine], axis=1).astype(jnp.bfloat16)


def butterfly_section(state, speeds, mixing, section_no, stride):
    total, width = state.shape
    blocks = state.reshape(total // (2 * stride), 2, stride, width)
    first = blocks[:, 0].reshape(-1, width)
    second = blocks[:, 1].reshape(-1, width)
    results = []
    for target in range(2):
        pre = jnp.dot(first, mixing[section_no, target, 0], preferred_element_type=jnp.float32)
        pre = pre + jnp.dot(second, mixing[section_no, target, 1], preferred_element_type=jnp.float32)
        results.append(pre.reshape(total // (2 * stride), stride, width))
    pre = jnp.stack(results, axis=1).reshape(total, width)
    return rotate(pre, speeds, section_no)


def reference(charges, source_order, velocity, leaf_weight, mixing, eval_weight, target_order):
    offsets = (jnp.arange(NSRC, dtype=jnp.int32) // LEAF) * LEAF
    ordered = jnp.take(charges, source_order.astype(jnp.int32) + offsets, axis=1)
    leaf_in = ordered.reshape(2, NBOX, LEAF).transpose(1, 0, 2).reshape(NBOX, 2 * LEAF).astype(jnp.bfloat16)
    state = jnp.dot(leaf_in, leaf_weight, preferred_element_type=jnp.float32).astype(jnp.bfloat16)
    box_bits = int(BOX).bit_length() - 1
    for section_no in range(LEVELS):
        if section_no < LOCAL_LEVELS:
            bit_no = section_no
        else:
            bit_no = box_bits + section_no - LOCAL_LEVELS
        state = butterfly_section(state, velocity, mixing, section_no, 2 ** bit_no)
    values = jnp.dot(state, eval_weight, preferred_element_type=jnp.float32)
    field = values.reshape(NBOX, 2, LEAF).transpose(1, 0, 2).reshape(2, NSRC)
    return jnp.take(field, target_order.astype(jnp.int32) + offsets, axis=1)
```

```python
import functools
import math

import jax
import jax.numpy as jnp
import numpy as np
from jax import lax
from jax.experimental import pallas as pl
from jax.experimental.pallas import tpu as pltpu
from jax.sharding import PartitionSpec as P

LANES = 128
AXES = ("wide", "narrow")


def lane_index(shape):
    return lax.broadcasted_iota(jnp.int32, shape, len(shape) - 1)


def row_index(shape):
    return lax.broadcasted_iota(jnp.int32, shape, len(shape) - 2)


def pick(rows, order, leaf):
    lanes = lane_index(order.shape)
    return jnp.take_along_axis(rows, order + lanes // leaf * leaf, axis=1)


def pack_kernel(leaf, charges_ref, order_ref, velocity_ref, out_ref):
    rows = order_ref.shape[0]
    step = min(rows, 64)

    @pl.loop(0, rows // step)
    def _(block):
        here = pl.ds(pl.multiple_of(block * step, step), step)
        order = order_ref[here, :]
        for part in range(2):
            values = charges_ref[pl.ds(block * (2 * step) + part, step, stride=2), :]
            out_ref[here, part * LANES : (part + 1) * LANES] = pick(values, order, leaf).astype(
                jnp.bfloat16
            )
        speeds = velocity_ref[pl.ds(block * (step // leaf), step // leaf), :]
        speeds = jnp.broadcast_to(speeds[:, None, :], (step // leaf, leaf, LANES))
        speeds = speeds.reshape(step, LANES)
        shape = (step, LANES)
        own = lane_index(shape) // (LANES // leaf) == row_index(shape) % leaf
        out_ref[here, 2 * LANES :] = jnp.where(own, speeds, 0.0).astype(jnp.bfloat16)


def unpack_kernel(leaf, values_ref, order_ref, out_ref):
    rows = order_ref.shape[0]
    step = min(rows, 64)

    @pl.loop(0, rows // step)
    def _(block):
        here = pl.ds(pl.multiple_of(block * step, step), step)
        order = order_ref[here, :]
        for part in range(2):
            values = values_ref[here, part * LANES : (part + 1) * LANES].astype(jnp.float32)
            out_ref[pl.ds(block * (2 * step) + part, step, stride=2), :] = pick(
                values, order, leaf
            )


def sine_cosine(turns):
    u = turns - jnp.round(turns)
    w = u * u
    sin_terms = [(-1) ** i * math.pi ** (2 * i + 1) / math.factorial(2 * i + 1) for i in range(8)]
    cos_terms = [(-1) ** i * math.pi ** (2 * i) / math.factorial(2 * i) for i in range(8)]
    half_sin = jnp.full_like(w, sin_terms[-1])
    for term in sin_terms[-2::-1]:
        half_sin = half_sin * w + term
    half_sin = half_sin * u
    half_cos = jnp.full_like(w, cos_terms[-1])
    for term in cos_terms[-2::-1]:
        half_cos = half_cos * w + term
    twice = half_sin + half_sin
    return twice * half_cos, 1.0 - twice * half_sin


def butterfly_kernel(
    levels, local_levels, rows_per, leaf,
    packed_ref, nodes_ref, leaf_ref, mixing_ref, eval_ref, out_ref,
    state, maps, leaf_maps, eval_maps, node_maps, twice_ref, cos_ref, sin_ref,
):
    rows = packed_ref.shape[0]
    half = LANES // 2
    pairs = state.shape[0]
    group = 2 * pairs
    f32, b16 = jnp.float32, jnp.bfloat16

    def swapped(x):
        return pltpu.roll(x, half, 1)

    low64 = lane_index((half, LANES)) < half

    @pl.loop(0, levels)
    def _(level):
        for target in range(2):
            for source in range(2):
                for part in range(2):
                    own = mixing_ref[
                        level, target, source, part * half : (part + 1) * half, :
                    ].astype(f32)
                    far = swapped(own)
                    top, bottom = 2 * part * half, (2 * part + 1) * half
                    place = maps.at[level, target, source]
                    place[top : top + half, :LANES] = jnp.where(low64, own, 0.0).astype(b16)
                    place[top : top + half, LANES:] = jnp.where(low64, far, 0.0).astype(b16)
                    place[bottom : bottom + half, :LANES] = jnp.where(low64, 0.0, far).astype(b16)
                    place[bottom : bottom + half, LANES:] = jnp.where(low64, 0.0, own).astype(b16)

    leaf_rows = leaf_ref[...].astype(f32)
    low = lane_index((LANES, LANES)) < half
    box_of_row = row_index((LANES, LANES)) // leaf
    box_of_lane = lane_index((half, LANES)) // leaf
    slot = lane_index((2 * leaf, 2 * LANES))
    spread = (slot // LANES * leaf + slot % leaf == row_index((2 * leaf, 2 * LANES))).astype(b16)
    eval_rows = jnp.dot(eval_ref[...], spread, preferred_element_type=f32)
    node_box = row_index((LANES, LANES)) % group
    for part in range(2):
        tiled = jnp.broadcast_to(
            leaf_rows[part * leaf : (part + 1) * leaf][None], (group, leaf, LANES)
        ).reshape(LANES, LANES)
        far = swapped(tiled)
        for pair in range(pairs):
            first, second = box_of_row == pair, box_of_row == pair + pairs
            here = slice(part * LANES, (part + 1) * LANES)
            leaf_maps[pair, here, :LANES] = jnp.where(
                low, jnp.where(first, tiled, 0.0), jnp.where(second, far, 0.0)
            ).astype(b16)
            leaf_maps[pair, here, LANES:] = jnp.where(
                low, jnp.where(first, far, 0.0), jnp.where(second, tiled, 0.0)
            ).astype(b16)
    for pair in range(pairs):
        for part in range(2):
            for number in range(2):
                top = (2 * part + number) * half
                for side in range(2):
                    block = eval_rows[
                        part * half : (part + 1) * half, side * LANES : (side + 1) * LANES
                    ]
                    eval_maps[pair, top : top + half, side * LANES : (side + 1) * LANES] = (
                        jnp.where(box_of_lane == pair + number * pairs, block, 0.0).astype(b16)
                    )
        for piece in range(3):
            nodes = nodes_ref[piece : piece + 1, :]
            mine = node_box == jnp.where(low, pair, pair + pairs)
            node_maps[pair, piece * LANES : (piece + 1) * LANES, :] = jnp.where(
                mine, nodes, 0.0
            ).astype(b16)

    step = min(rows, 128)

    @pl.loop(0, pairs * (rows // step))
    def _(item):
        pair, block = item // (rows // step), item % (rows // step)
        here = pl.ds(pl.multiple_of(block * step, step), step)
        charges = packed_ref[here, : 2 * LANES]
        state[pair, here, :] = jnp.dot(
            charges, leaf_maps[pair], preferred_element_type=f32
        ).astype(b16)
        speeds = packed_ref[here, 2 * LANES :]
        turns = jnp.dot(
            jnp.concatenate([speeds] * 3, axis=1), node_maps[pair], preferred_element_type=f32
        )
        sine, cosine = sine_cosine(turns)
        twice_ref[pair, here, :] = cosine + cosine
        cos_ref[0, pair, here, :] = cosine
        sin_ref[0, pair, here, :] = sine
        cos_ref[1, pair, here, :] = jnp.ones_like(cosine)
        sin_ref[1, pair, here, :] = jnp.zeros_like(sine)

    def turn(level, pre, index):
        now, other = level % 2, 1 - level % 2
        cosine, sine = cos_ref[(now, *index)], sin_ref[(now, *index)]
        real, imag = pre[:, :LANES], pre[:, LANES:]
        shape = cosine.shape
        cosine, sine = cosine.reshape(real.shape), sine.reshape(real.shape)
        turned = jnp.concatenate(
            [real * cosine - imag * sine, real * sine + imag * cosine], axis=1
        ).astype(b16)
        if level + 1 < levels:
            twice = twice_ref[index].reshape(real.shape)
            cos_ref[(other, *index)] = (
                twice * cosine - cos_ref[(other, *index)].reshape(real.shape)
            ).reshape(shape)
            sin_ref[(other, *index)] = (
                twice * sine - sin_ref[(other, *index)].reshape(real.shape)
            ).reshape(shape)
        return turned

    def mixed(level, target, first, second):
        return jnp.dot(first, maps[level, target, 0], preferred_element_type=f32) + jnp.dot(
            second, maps[level, target, 1], preferred_element_type=f32
        )

    for level in range(levels):
        if level < local_levels:
            blocks = rows // step
            stride = 1 << level

            @pl.loop(0, pairs // 2 * blocks)
            def _(item):
                which, block = item // blocks, item % blocks
                low_pair = which // stride * (2 * stride) + which % stride
                here = pl.ds(pl.multiple_of(block * step, step), step)
                first = state[low_pair, here, :]
                second = state[low_pair + stride, here, :]
                for target in range(2):
                    pair = low_pair + target * stride
                    pre = mixed(level, target, first, second)
                    state[pair, here, :] = turn(level, pre, (pair, here))

            continue
        stride = rows_per << (level - local_levels)
        if stride % 16 == 0:
            span = max(2 * step, 2 * stride)
            blocks = rows // span
            tops = span // (2 * stride)

            @pl.loop(0, pairs * blocks)
            def _(item):
                pair, block = item // blocks, item % blocks
                for start in range(0, stride, step):
                    count = min(step, stride)
                    for_targets = []
                    for source in range(2):
                        parts = []
                        for top in range(tops):
                            at = block * span + (2 * top + source) * stride + start
                            parts.append(state[pair, pl.ds(pl.multiple_of(at, 16), count), :])
                        for_targets.append(
                            parts[0] if tops == 1 else jnp.concatenate(parts, axis=0)
                        )
                    for target in range(2):
                        pre = mixed(level, target, *for_targets)
                        for top in range(tops):
                            at = block * span + (2 * top + target) * stride + start
                            here = pl.ds(pl.multiple_of(at, 16), count)
                            state[pair, here, :] = turn(
                                level, pre[top * count : (top + 1) * count], (pair, here)
                            )

        else:
            blocks = rows // step

            @pl.loop(0, pairs * blocks)
            def _(item):
                pair, block = item // blocks, item % blocks
                here = pl.ds(pl.multiple_of(block * step, step), step)
                own = state[pair, here, :].astype(f32)
                upper = row_index(own.shape) // stride % 2 == 1
                first = jnp.where(upper, pltpu.roll(own, stride, 0), own).astype(b16)
                second = jnp.where(upper, own, pltpu.roll(own, step - stride, 0)).astype(b16)
                pre = jnp.where(
                    upper, mixed(level, 1, first, second), mixed(level, 0, first, second)
                )
                state[pair, here, :] = turn(level, pre, (pair, here))

    @pl.loop(0, rows // step)
    def _(block):
        here = pl.ds(pl.multiple_of(block * step, step), step)
        total = jnp.dot(state[0, here, :], eval_maps[0], preferred_element_type=f32)
        for pair in range(1, pairs):
            total = total + jnp.dot(
                state[pair, here, :], eval_maps[pair], preferred_element_type=f32
            )
        out_ref[here, :] = total.astype(b16)


def split_nodes(rank):
    nodes = np.cos(np.pi * (np.arange(rank) + 0.5) / rank) / 2
    pieces = []
    rest = np.tile(nodes, LANES // rank)
    for _ in range(3):
        piece = rest.astype(jnp.bfloat16)
        pieces.append(piece.astype(np.float32))
        rest = rest - piece.astype(np.float64)
    return np.stack(pieces)


def on_device(charges, source_order, velocity, leaf_weight, mixing, eval_weight, target_order):
    leaf = leaf_weight.shape[0] // 2
    width = leaf_weight.shape[1]
    boxes = charges.shape[1] // leaf
    group = LANES // leaf
    rows = boxes // group
    devices = lax.axis_size("wide") * lax.axis_size("narrow")
    rows_per = rows // devices
    levels = mixing.shape[0]
    local_levels = levels - (devices.bit_length() - 1)
    pairs = group // 2
    vmem = pltpu.CompilerParams(vmem_limit_bytes=48 * 2**20)

    charge_rows = charges.reshape(2, rows, LANES).transpose(1, 0, 2).reshape(2 * rows, LANES)
    speed_rows = velocity.astype(jnp.float32).reshape(boxes // LANES, LANES)
    packed = pl.pallas_call(
        functools.partial(pack_kernel, leaf),
        out_shape=jax.ShapeDtypeStruct((rows, 3 * LANES), jnp.bfloat16),
        compiler_params=vmem,
        name="pack",
    )(charge_rows, source_order.reshape(rows, LANES), speed_rows)

    packed = lax.all_to_all(
        packed.reshape(devices, rows_per, 3 * LANES), AXES, 0, 0, tiled=True
    ).reshape(rows, 3 * LANES)

    nodes = jnp.asarray(split_nodes(width // 2))
    table = pltpu.VMEM((pairs, rows, LANES), jnp.float32)
    values = pl.pallas_call(
        functools.partial(butterfly_kernel, levels, local_levels, rows_per, leaf),
        out_shape=jax.ShapeDtypeStruct((rows, 2 * LANES), jnp.bfloat16),
        scratch_shapes=[
            pltpu.VMEM((pairs, rows, 2 * LANES), jnp.bfloat16),
            pltpu.VMEM((levels, 2, 2, 2 * LANES, 2 * LANES), jnp.bfloat16),
            pltpu.VMEM((pairs, 2 * LANES, 2 * LANES), jnp.bfloat16),
            pltpu.VMEM((pairs, 2 * LANES, 2 * LANES), jnp.bfloat16),
            pltpu.VMEM((pairs, 3 * LANES, LANES), jnp.bfloat16),
            table,
            pltpu.VMEM((2, pairs, rows, LANES), jnp.float32),
            pltpu.VMEM((2, pairs, rows, LANES), jnp.float32),
        ],
        compiler_params=vmem,
        name="butterfly",
    )(packed, nodes, leaf_weight, mixing, eval_weight)

    values = lax.all_to_all(
        values.reshape(devices, rows_per, 2 * LANES), AXES, 0, 0, tiled=True
    ).reshape(rows, 2 * LANES)

    out = pl.pallas_call(
        functools.partial(unpack_kernel, leaf),
        out_shape=jax.ShapeDtypeStruct((2 * rows, LANES), jnp.float32),
        compiler_params=vmem,
        name="unpack",
    )(values, target_order.reshape(rows, LANES))
    return out.reshape(rows, 2, LANES).transpose(1, 0, 2).reshape(2, rows * LANES)


def solution(mesh):
    return jax.shard_map(
        on_device,
        mesh=mesh,
        in_specs=(
            P(None, AXES),
            P(AXES),
            P(AXES),
            P(),
            P(),
            P(),
            P(AXES),
        ),
        out_specs=P(None, AXES),
        check_vma=False,
    )
```

```python
import functools
import math

import jax
import jax.numpy as jnp
import numpy as np
from jax import lax
from jax.experimental import pallas as pl
from jax.experimental.pallas import tpu as pltpu
from jax.sharding import PartitionSpec as P

LANES = 128
HALF = LANES // 2
TILE = 16
AXES = ("wide", "narrow")
F32, B16 = jnp.float32, jnp.bfloat16
UNITS = 32
VMEM = pltpu.CompilerParams(vmem_limit_bytes=56 * 2**20)


def lane_index(shape):
    return lax.broadcasted_iota(jnp.int32, shape, len(shape) - 1)


def row_index(shape):
    return lax.broadcasted_iota(jnp.int32, shape, len(shape) - 2)


def swapped(x):
    return pltpu.roll(x, HALF, 1)


def odd_bits(number):
    for shift in (16, 8, 4, 2, 1):
        number = number ^ lax.shift_right_logical(number, shift)
    return number & 1


def device_number():
    return lax.axis_index("wide") * lax.axis_size("narrow") + lax.axis_index("narrow")


def pack_kernel(leaf, charges_ref, order_ref, velocity_ref, out_ref):
    rows = order_ref.shape[0]
    odd = odd_bits(device_number()) == 1
    step = min(rows, 64)
    lanes = lane_index((step, LANES))
    group = LANES // leaf

    @pl.loop(0, rows // step)
    def _(block):
        here = pl.ds(pl.multiple_of(block * step, step), step)
        index = order_ref[here, :] + lanes // leaf * leaf
        for part in range(2):
            values = charges_ref[pl.ds(block * (2 * step) + part, step, stride=2), :]
            values = jnp.take_along_axis(values, index, axis=1)
            values = jnp.where(odd, swapped(values), values)
            out_ref[here, part * LANES : (part + 1) * LANES] = values.astype(B16)

    speeds = velocity_ref[...].astype(F32)
    lanes = lane_index(speeds.shape)
    speeds = jnp.take_along_axis(speeds, lanes ^ jnp.where(odd, group // 2, 0), axis=1)
    count = speeds.shape[0]
    speeds = jnp.broadcast_to(speeds[:, None, :], (count, leaf, LANES)).reshape(rows, LANES)
    own = lane_index(speeds.shape) // group == row_index(speeds.shape) % leaf
    speeds = jnp.where(own, speeds, 0.0)
    shift = group
    while shift < LANES:
        speeds = speeds + pltpu.roll(speeds, shift, 1)
        shift *= 2
    out_ref[:, 2 * LANES :] = speeds.astype(B16)


def unpack_kernel(leaf, values_ref, order_ref, out_ref):
    rows = order_ref.shape[0]
    odd = odd_bits(device_number()) == 1
    step = min(rows, 64)
    base = lane_index((step, LANES)) // leaf * leaf ^ jnp.where(odd, HALF, 0)

    @pl.loop(0, rows // step)
    def _(block):
        here = pl.ds(pl.multiple_of(block * step, step), step)
        index = order_ref[here, :] + base
        for part in range(2):
            values = values_ref[here, part * LANES : (part + 1) * LANES].astype(F32)
            out_ref[pl.ds(block * (2 * step) + part, step, stride=2), :] = jnp.take_along_axis(
                values, index, axis=1
            )


def odd_pair(pair):
    return bin(pair).count("1") % 2 == 1


def maps_kernel(leaf, leaf_ref, mixing_ref, eval_ref, nodes_ref, maps, leaf_maps, eval_maps, node_maps):
    levels = mixing_ref.shape[0]
    pairs = leaf_maps.shape[0]
    group = 2 * pairs
    low = lane_index((HALF, LANES)) < HALF

    @pl.loop(0, levels)
    def _(level):
        for source in range(2):
            for part in range(2):
                rows = slice(part * HALF, (part + 1) * HALF)
                to_first = mixing_ref[level, 0, source, rows, :].astype(F32)
                to_second = mixing_ref[level, 1, source, rows, :].astype(F32)
                first_far, second_far = swapped(to_first), swapped(to_second)
                for order in range(2):
                    top = part * LANES + (source ^ order) * HALF
                    place = maps.at[level, order, top : top + HALF]
                    if order == 0:
                        real = jnp.where(low, to_first, second_far)
                        imag = jnp.where(low, first_far, to_second)
                    else:
                        real = jnp.where(low, to_second, first_far)
                        imag = jnp.where(low, second_far, to_first)
                    place[:, :LANES] = real.astype(B16)
                    place[:, LANES:] = imag.astype(B16)

    leaf_rows = leaf_ref[...].astype(F32)
    low = lane_index((LANES, LANES)) < HALF
    box_of_row = row_index((LANES, LANES)) // leaf
    box_of_lane = lane_index((HALF, LANES)) // leaf
    slot = lane_index((2 * leaf, 2 * LANES))
    spread = (slot // LANES * leaf + slot % leaf == row_index((2 * leaf, 2 * LANES))).astype(B16)
    eval_rows = jnp.dot(eval_ref[...], spread, preferred_element_type=F32)
    node_row = row_index((LANES, LANES))
    nodes = jnp.zeros((LANES, LANES), F32)
    for piece in range(3):
        nodes = jnp.where(node_row // group == piece, nodes_ref[piece : piece + 1, :], nodes)
    node_maps[...] = jnp.zeros(node_maps.shape, B16)
    for pair in range(pairs):
        left, right = (pair + pairs, pair) if odd_pair(pair) else (pair, pair + pairs)
        for part in range(2):
            tiled = jnp.broadcast_to(
                leaf_rows[part * leaf : (part + 1) * leaf][None], (group, leaf, LANES)
            ).reshape(LANES, LANES)
            far = swapped(tiled)
            first, second = box_of_row == left, box_of_row == right
            here = slice(part * LANES, (part + 1) * LANES)
            leaf_maps[pair, here, :LANES] = jnp.where(
                low, jnp.where(first, tiled, 0.0), jnp.where(second, far, 0.0)
            ).astype(B16)
            leaf_maps[pair, here, LANES:] = jnp.where(
                low, jnp.where(first, far, 0.0), jnp.where(second, tiled, 0.0)
            ).astype(B16)
            for number, box in enumerate((left, right)):
                top = (2 * part + number) * HALF
                for side in range(2):
                    lanes = slice(side * LANES, (side + 1) * LANES)
                    block = eval_rows[part * HALF : (part + 1) * HALF, lanes]
                    eval_maps[pair, top : top + HALF, lanes] = jnp.where(
                        box_of_lane == box, block, 0.0
                    ).astype(B16)
        lanes = slice(pair % 2 * LANES, (pair % 2 + 1) * LANES)
        mine = node_row % group == jnp.where(low, left, right)
        node_maps[pair // 2, :LANES, lanes] = jnp.where(mine, nodes, 0.0).astype(B16)


def sine_cosine(turns):
    u = turns - jnp.round(turns)
    w = u * u
    sin_terms = [(-1) ** i * math.pi ** (2 * i + 1) / math.factorial(2 * i + 1) for i in range(7)]
    cos_terms = [(-1) ** i * math.pi ** (2 * i) / math.factorial(2 * i) for i in range(7)]
    half_sin = jnp.full_like(w, sin_terms[-1])
    for term in sin_terms[-2::-1]:
        half_sin = half_sin * w + term
    half_sin = half_sin * u
    half_cos = jnp.full_like(w, cos_terms[-1])
    for term in cos_terms[-2::-1]:
        half_cos = half_cos * w + term
    twice = half_sin + half_sin
    return twice * half_cos, 1.0 - twice * half_sin


def butterfly_kernel(
    plan, packed_ref, maps, leaf_maps, eval_maps, node_maps, out_ref,
    state_a, state_b, twice_ref, *tables,
):
    rows = packed_ref.shape[0]
    pairs = leaf_maps.shape[0]
    levels = len(plan)
    states = (state_a, state_b)
    cosines, sines = tables[:3], tables[3:]
    low = lane_index((TILE, LANES)) < HALF
    low16 = lax.broadcasted_iota(jnp.int16, (TILE, LANES), 1) < jnp.int16(HALF)

    def merged(mask, first, second):
        return jnp.concatenate(
            [
                jnp.where(mask, first[:, :LANES], second[:, :LANES]),
                jnp.where(mask, first[:, LANES:], second[:, LANES:]),
            ],
            axis=1,
        )

    def turned(level, tile, real, imag):
        now, last, coming = level % 3, (level - 1) % 3, (level + 1) % 3
        cosine, sine = cosines[now][tile], sines[now][tile]
        target = states[1 - level % 2]
        target[tile, :, :LANES] = (real * cosine - imag * sine).astype(B16)
        target[tile, :, LANES:] = (real * sine + imag * cosine).astype(B16)
        if level + 1 < levels:
            twice = twice_ref[tile]
            last_cosine = cosines[last][tile] if level else 1.0
            cosines[coming][tile] = twice * cosine - last_cosine
            sines[coming][tile] = twice * sine - sines[last][tile] if level else twice * sine

    half_tiles = state_a.shape[0] // 2
    units = min(UNITS, half_tiles)
    blocks = half_tiles // units

    def tiles_of(level, block, unit):
        bit = plan[level][1]
        stride = 1 << bit
        if stride >= units:
            start = block * units
            base = lax.shift_left(lax.shift_right_logical(start, bit), bit + 1) | (
                start & (stride - 1)
            )
            tile = base + unit
        else:
            tile = block * (2 * units) + (unit >> bit << (bit + 1) | unit & (stride - 1))
        return tile, tile + stride

    def run(*accumulators):
        def load_maps(level):
            for order in range(2):
                pltpu.matmul_push_rhs(maps[level, order], 0, order)

        def send(level, block, unit, fresh):
            source = states[level % 2]
            first, second = (source[tile] for tile in tiles_of(level, block, unit))
            for order in range(2):
                pltpu.matmul_acc_lhs(
                    accumulators[2 * unit + order],
                    merged(low16, *((second, first) if order else (first, second))),
                    load_staged_rhs=0 if fresh and unit == 0 else None,
                )

        def finish(level, block, unit):
            one, other = (pltpu.matmul_pop(accumulators[2 * unit + order]) for order in range(2))
            for target, tile in enumerate(tiles_of(level, block, unit)):
                left, right = (other, one) if target else (one, other)
                turned(
                    level, tile,
                    jnp.where(low, left[:, :LANES], right[:, :LANES]),
                    jnp.where(low, left[:, LANES:], right[:, LANES:]),
                )

        def within_tiles(level):
            stride = plan[level][1]
            upper = row_index((TILE, 2 * LANES)) // stride % 2 == 1
            mask = (lane_index((TILE, 2 * LANES)) % LANES < HALF) != upper

            def one_tile(tile, fresh):
                own = states[level % 2][tile].astype(F32)
                far = jnp.where(
                    upper, pltpu.roll(own, stride, 0), pltpu.roll(own, TILE - stride, 0)
                )
                pre = []
                for order in range(2):
                    lhs = jnp.where(mask, far, own) if order else jnp.where(mask, own, far)
                    pltpu.matmul_acc_lhs(
                        accumulators[order], lhs.astype(B16), load_staged_rhs=0 if fresh else None
                    )
                    pre.append(pltpu.matmul_pop(accumulators[order]))
                mixed = jnp.where(mask, *pre)
                turned(level, tile, mixed[:, :LANES], mixed[:, LANES:])

            one_tile(0, True)

            @pl.loop(1, 2 * half_tiles)
            def _(tile):
                one_tile(tile, False)

        row_tiles = rows // TILE
        few = min(TILE, row_tiles)

        @pl.loop(0, pairs // 2 * (row_tiles // few))
        def _(item):
            duo, start = item // (row_tiles // few), item % (row_tiles // few) * few
            for order in range(2):
                pltpu.matmul_push_rhs(node_maps[duo], 0, order)
                pltpu.matmul_push_rhs(leaf_maps[2 * duo + order], 1, order)
            strips = [pl.ds(pl.multiple_of((start + i) * TILE, TILE), TILE) for i in range(few)]
            for i, strip in enumerate(strips):
                speeds = packed_ref[strip, 2 * LANES :]
                pltpu.matmul_acc_lhs(
                    accumulators[2 * few + i],
                    jnp.concatenate([speeds, speeds], axis=1),
                    load_staged_rhs=0 if i < 2 else None,
                )
            for i, strip in enumerate(strips):
                for order in range(2):
                    pltpu.matmul_acc_lhs(
                        accumulators[2 * i + order],
                        packed_ref[strip, : 2 * LANES],
                        load_staged_rhs=1 if i == 0 else None,
                    )
            for i in range(few):
                turns = pltpu.matmul_pop(accumulators[2 * few + i])
                for order in range(2):
                    tile = (start + i) * pairs + 2 * duo + order
                    sine, cosine = sine_cosine(turns[:, order * LANES : (order + 1) * LANES])
                    twice_ref[tile] = cosine + cosine
                    cosines[0][tile] = cosine
                    sines[0][tile] = sine
                    state_a[tile] = pltpu.matmul_pop(accumulators[2 * i + order]).astype(B16)

        flowing = False
        for level in range(levels):
            if not flowing:
                load_maps(level)
            if plan[level][0] == "rows":
                within_tiles(level)
                continue
            if not flowing:
                for unit in range(units):
                    send(level, 0, unit, True)

            @pl.loop(0, blocks - 1)
            def _(block):
                for unit in range(units):
                    finish(level, block, unit)
                    send(level, block + 1, unit, False)

            flowing = blocks > 2 and level + 1 < levels and plan[level + 1][0] == "tiles"
            if flowing:
                load_maps(level + 1)
            for unit in range(units):
                finish(level, blocks - 1, unit)
                if flowing:
                    send(level + 1, 0, unit, True)

        final = states[levels % 2]
        share = row_tiles // 2
        for pair in range(pairs):
            for order in range(2):
                pltpu.matmul_push_rhs(eval_maps[pair], pair % 2, order)
            for i in range(share):
                for order in range(2):
                    pltpu.matmul_acc_lhs(
                        accumulators[2 * i + order],
                        final[(order * share + i) * pairs + pair],
                        load_staged_rhs=pair % 2 if i == 0 else None,
                    )
        for i in range(share):
            for order in range(2):
                top = (order * share + i) * TILE
                out_ref[top : top + TILE, :] = pltpu.matmul_pop(
                    accumulators[2 * i + order]
                ).astype(B16)

    pl.run_scoped(
        run, *[pltpu.ACC(order)((TILE, 2 * LANES), F32) for _ in range(units) for order in range(2)]
    )


def split_nodes(rank):
    nodes = np.cos(np.pi * (np.arange(rank) + 0.5) / rank) / 2
    pieces = []
    rest = np.tile(nodes, LANES // rank)
    for _ in range(3):
        piece = rest.astype(B16)
        pieces.append(piece.astype(np.float32))
        rest = rest - piece.astype(np.float64)
    return np.stack(pieces)


def level_plan(levels, local_levels, rows_per):
    plan = [("tiles", level) for level in range(local_levels)]
    stride = rows_per
    for _ in range(levels - local_levels):
        if stride < TILE:
            plan.append(("rows", stride))
        else:
            plan.append(("tiles", local_levels + (stride // TILE).bit_length() - 1))
        stride *= 2
    return tuple(plan)


def on_device(charges, source_order, velocity, leaf_weight, mixing, eval_weight, target_order):
    leaf = leaf_weight.shape[0] // 2
    width = leaf_weight.shape[1]
    boxes = charges.shape[1] // leaf
    group = LANES // leaf
    pairs = group // 2
    rows = boxes // group
    devices = lax.axis_size("wide") * lax.axis_size("narrow")
    rows_per = rows // devices
    levels = mixing.shape[0]
    local_levels = levels - (devices.bit_length() - 1)
    assert width == LANES and 1 << local_levels == pairs

    charge_rows = charges.reshape(2, rows, LANES).transpose(1, 0, 2).reshape(2 * rows, LANES)
    packed = pl.pallas_call(
        functools.partial(pack_kernel, leaf),
        out_shape=jax.ShapeDtypeStruct((rows, 3 * LANES), B16),
        compiler_params=VMEM,
        name="pack",
    )(charge_rows, source_order.reshape(rows, LANES), velocity.reshape(boxes // LANES, LANES))

    packed = lax.all_to_all(
        packed.reshape(devices, rows_per, 3 * LANES), AXES, 0, 0, tiled=True
    ).reshape(rows, 3 * LANES)

    square = (2 * LANES, 2 * LANES)
    weights = pl.pallas_call(
        functools.partial(maps_kernel, leaf),
        out_shape=[
            jax.ShapeDtypeStruct((levels, 2, *square), B16),
            jax.ShapeDtypeStruct((pairs, *square), B16),
            jax.ShapeDtypeStruct((pairs, *square), B16),
            jax.ShapeDtypeStruct((pairs // 2, *square), B16),
        ],
        compiler_params=VMEM,
        cost_estimate=pl.CostEstimate(flops=10**9, bytes_accessed=10**7, transcendentals=0),
        name="maps",
    )(leaf_weight, mixing, eval_weight, jnp.asarray(split_nodes(width // 2)))

    tiles = rows // TILE * pairs
    state = pltpu.VMEM((tiles, TILE, 2 * LANES), B16)
    table = pltpu.VMEM((tiles, TILE, LANES), F32)
    values = pl.pallas_call(
        functools.partial(butterfly_kernel, level_plan(levels, local_levels, rows_per)),
        out_shape=jax.ShapeDtypeStruct((rows, 2 * LANES), B16),
        scratch_shapes=[state, state] + [table] * 7,
        compiler_params=VMEM,
        name="butterfly",
    )(packed, *weights)

    values = lax.all_to_all(
        values.reshape(devices, rows_per, 2 * LANES), AXES, 0, 0, tiled=True
    ).reshape(rows, 2 * LANES)

    out = pl.pallas_call(
        functools.partial(unpack_kernel, leaf),
        out_shape=jax.ShapeDtypeStruct((2 * rows, LANES), F32),
        compiler_params=VMEM,
        name="unpack",
    )(values, target_order.reshape(rows, LANES))
    return out.reshape(rows, 2, LANES).transpose(1, 0, 2).reshape(2, rows * LANES)


def solution(mesh):
    mapped = jax.shard_map(
        on_device,
        mesh=mesh,
        in_specs=(
            P(None, AXES),
            P(AXES),
            P(AXES),
            P(),
            P(),
            P(),
            P(AXES),
        ),
        out_specs=P(None, AXES),
        check_vma=False,
    )

    def program(*arrays):
        with jax.sharding.use_abstract_mesh(mesh.abstract_mesh):
            return mapped(*arrays)

    return program
```

```python
import functools
import math

import jax
import jax.numpy as jnp
import numpy as np
from jax import lax
from jax.experimental import pallas as pl
from jax.experimental.pallas import tpu as pltpu
from jax.sharding import PartitionSpec as P

LANES = 128
HALF = LANES // 2
TILE = 16
AXES = ("wide", "narrow")
F32, B16 = jnp.float32, jnp.bfloat16
UNITS = 32
def vmem(mebibytes):
    return pltpu.CompilerParams(vmem_limit_bytes=mebibytes * 2**20)


def lane_index(shape):
    return lax.broadcasted_iota(jnp.int32, shape, len(shape) - 1)


def row_index(shape):
    return lax.broadcasted_iota(jnp.int32, shape, len(shape) - 2)


def swapped(x):
    return pltpu.roll(x, HALF, 1)


def odd_bits(number):
    for shift in (16, 8, 4, 2, 1):
        number = number ^ lax.shift_right_logical(number, shift)
    return number & 1


def device_number():
    return lax.axis_index("wide") * lax.axis_size("narrow") + lax.axis_index("narrow")


def pack_kernel(leaf, charges_ref, order_ref, velocity_ref, out_ref):
    rows = order_ref.shape[0]
    odd = odd_bits(device_number()) == 1
    step = min(rows, 64)
    lanes = lane_index((step, LANES))
    group = LANES // leaf

    @pl.loop(0, rows // step)
    def _(block):
        here = pl.ds(pl.multiple_of(block * step, step), step)
        index = order_ref[here, :] + lanes // leaf * leaf
        for part in range(2):
            values = charges_ref[pl.ds(block * (2 * step) + part, step, stride=2), :]
            values = jnp.take_along_axis(values, index, axis=1)
            values = jnp.where(odd, swapped(values), values)
            out_ref[here, part * LANES : (part + 1) * LANES] = values.astype(B16)

    speeds = velocity_ref[...].astype(F32)
    lanes = lane_index(speeds.shape)
    speeds = jnp.take_along_axis(speeds, lanes ^ jnp.where(odd, group // 2, 0), axis=1)
    count = speeds.shape[0]
    speeds = jnp.broadcast_to(speeds[:, None, :], (count, leaf, LANES)).reshape(rows, LANES)
    own = lane_index(speeds.shape) // group == row_index(speeds.shape) % leaf
    speeds = jnp.where(own, speeds, 0.0)
    shift = group
    while shift < LANES:
        speeds = speeds + pltpu.roll(speeds, shift, 1)
        shift *= 2
    out_ref[:, 2 * LANES :] = speeds.astype(B16)


def unpack_kernel(leaf, values_ref, order_ref, out_ref):
    rows = order_ref.shape[0]
    odd = odd_bits(device_number()) == 1
    step = min(rows, 64)
    base = lane_index((step, LANES)) // leaf * leaf ^ jnp.where(odd, HALF, 0)

    @pl.loop(0, rows // step)
    def _(block):
        here = pl.ds(pl.multiple_of(block * step, step), step)
        index = order_ref[here, :] + base
        for part in range(2):
            values = values_ref[here, part * LANES : (part + 1) * LANES].astype(F32)
            out_ref[pl.ds(block * (2 * step) + part, step, stride=2), :] = jnp.take_along_axis(
                values, index, axis=1
            )


def odd_pair(pair):
    return bin(pair).count("1") % 2 == 1


def maps_kernel(leaf, leaf_ref, mixing_ref, eval_ref, nodes_ref, maps, leaf_maps, eval_maps, node_maps):
    levels = mixing_ref.shape[0]
    pairs = leaf_maps.shape[0]
    group = 2 * pairs
    low = lane_index((HALF, LANES)) < HALF

    @pl.loop(0, levels)
    def _(level):
        for source in range(2):
            for part in range(2):
                rows = slice(part * HALF, (part + 1) * HALF)
                to_first = mixing_ref[level, 0, source, rows, :].astype(F32)
                to_second = mixing_ref[level, 1, source, rows, :].astype(F32)
                first_far, second_far = swapped(to_first), swapped(to_second)
                for order in range(2):
                    top = part * LANES + (source ^ order) * HALF
                    place = maps.at[level, order, top : top + HALF]
                    if order == 0:
                        real = jnp.where(low, to_first, second_far)
                        imag = jnp.where(low, first_far, to_second)
                    else:
                        real = jnp.where(low, to_second, first_far)
                        imag = jnp.where(low, second_far, to_first)
                    place[:, :LANES] = real.astype(B16)
                    place[:, LANES:] = imag.astype(B16)

    leaf_rows = leaf_ref[...].astype(F32)
    low = lane_index((LANES, LANES)) < HALF
    box_of_row = row_index((LANES, LANES)) // leaf
    box_of_lane = lane_index((HALF, LANES)) // leaf
    slot = lane_index((2 * leaf, 2 * LANES))
    spread = (slot // LANES * leaf + slot % leaf == row_index((2 * leaf, 2 * LANES))).astype(B16)
    eval_rows = jnp.dot(eval_ref[...], spread, preferred_element_type=F32)
    node_row = row_index((LANES, LANES))
    nodes = jnp.zeros((LANES, LANES), F32)
    for piece in range(3):
        nodes = jnp.where(node_row // group == piece, nodes_ref[piece : piece + 1, :], nodes)
    node_maps[...] = jnp.zeros(node_maps.shape, B16)
    for pair in range(pairs):
        left, right = (pair + pairs, pair) if odd_pair(pair) else (pair, pair + pairs)
        for part in range(2):
            tiled = jnp.broadcast_to(
                leaf_rows[part * leaf : (part + 1) * leaf][None], (group, leaf, LANES)
            ).reshape(LANES, LANES)
            far = swapped(tiled)
            first, second = box_of_row == left, box_of_row == right
            here = slice(part * LANES, (part + 1) * LANES)
            leaf_maps[pair, here, :LANES] = jnp.where(
                low, jnp.where(first, tiled, 0.0), jnp.where(second, far, 0.0)
            ).astype(B16)
            leaf_maps[pair, here, LANES:] = jnp.where(
                low, jnp.where(first, far, 0.0), jnp.where(second, tiled, 0.0)
            ).astype(B16)
            for number, box in enumerate((left, right)):
                top = (2 * part + number) * HALF
                for side in range(2):
                    lanes = slice(side * LANES, (side + 1) * LANES)
                    block = eval_rows[part * HALF : (part + 1) * HALF, lanes]
                    eval_maps[pair, top : top + HALF, lanes] = jnp.where(
                        box_of_lane == box, block, 0.0
                    ).astype(B16)
        lanes = slice(pair % 2 * LANES, (pair % 2 + 1) * LANES)
        mine = node_row % group == jnp.where(low, left, right)
        node_maps[pair // 2, :LANES, lanes] = jnp.where(mine, nodes, 0.0).astype(B16)


def sine_cosine(turns):
    u = turns - jnp.round(turns)
    w = u * u
    sin_terms = [(-1) ** i * math.pi ** (2 * i + 1) / math.factorial(2 * i + 1) for i in range(7)]
    cos_terms = [(-1) ** i * math.pi ** (2 * i) / math.factorial(2 * i) for i in range(7)]
    half_sin = jnp.full_like(w, sin_terms[-1])
    for term in sin_terms[-2::-1]:
        half_sin = half_sin * w + term
    half_sin = half_sin * u
    half_cos = jnp.full_like(w, cos_terms[-1])
    for term in cos_terms[-2::-1]:
        half_cos = half_cos * w + term
    twice = half_sin + half_sin
    return twice * half_cos, 1.0 - twice * half_sin


def butterfly_kernel(
    plan, packed_ref, maps, leaf_maps, eval_maps, node_maps, out_ref,
    state_a, state_b, twice_ref, *tables,
):
    rows = packed_ref.shape[0]
    pairs = leaf_maps.shape[0]
    levels = len(plan)
    states = (state_a, state_b)
    cosines, sines = tables[:3], tables[3:]
    low = lane_index((TILE, LANES)) < HALF
    low16 = lax.broadcasted_iota(jnp.int16, (TILE, LANES), 1) < jnp.int16(HALF)

    def merged(mask, first, second):
        return jnp.concatenate(
            [
                jnp.where(mask, first[:, :LANES], second[:, :LANES]),
                jnp.where(mask, first[:, LANES:], second[:, LANES:]),
            ],
            axis=1,
        )

    def turned(level, tile, real, imag):
        now, last, coming = level % 3, (level - 1) % 3, (level + 1) % 3
        cosine, sine = cosines[now][tile], sines[now][tile]
        target = states[1 - level % 2]
        target[tile, :, :LANES] = (real * cosine - imag * sine).astype(B16)
        target[tile, :, LANES:] = (real * sine + imag * cosine).astype(B16)
        if level + 1 < levels:
            twice = twice_ref[tile]
            last_cosine = cosines[last][tile] if level else 1.0
            cosines[coming][tile] = twice * cosine - last_cosine
            sines[coming][tile] = twice * sine - sines[last][tile] if level else twice * sine

    half_tiles = state_a.shape[0] // 2
    units = min(UNITS, half_tiles)
    blocks = half_tiles // units

    def tiles_of(level, block, unit):
        bit = plan[level][1]
        stride = 1 << bit
        if stride >= units:
            start = block * units
            base = lax.shift_left(lax.shift_right_logical(start, bit), bit + 1) | (
                start & (stride - 1)
            )
            tile = base + unit
        else:
            tile = block * (2 * units) + (unit >> bit << (bit + 1) | unit & (stride - 1))
        return tile, tile + stride

    def run(*accumulators):
        def load_maps(level):
            for order in range(2):
                pltpu.matmul_push_rhs(maps[level, order], 0, order)

        def send(level, block, unit, fresh):
            source = states[level % 2]
            first, second = (source[tile] for tile in tiles_of(level, block, unit))
            for order in range(2):
                pltpu.matmul_acc_lhs(
                    accumulators[2 * unit + order],
                    merged(low16, *((second, first) if order else (first, second))),
                    load_staged_rhs=0 if fresh and unit == 0 else None,
                )

        def finish(level, block, unit):
            one, other = (pltpu.matmul_pop(accumulators[2 * unit + order]) for order in range(2))
            for target, tile in enumerate(tiles_of(level, block, unit)):
                left, right = (other, one) if target else (one, other)
                turned(
                    level, tile,
                    jnp.where(low, left[:, :LANES], right[:, :LANES]),
                    jnp.where(low, left[:, LANES:], right[:, LANES:]),
                )

        def within_tiles(level):
            stride = plan[level][1]
            upper = row_index((TILE, 2 * LANES)) // stride % 2 == 1
            mask = (lane_index((TILE, 2 * LANES)) % LANES < HALF) != upper

            def one_tile(tile, fresh):
                own = states[level % 2][tile].astype(F32)
                far = jnp.where(
                    upper, pltpu.roll(own, stride, 0), pltpu.roll(own, TILE - stride, 0)
                )
                pre = []
                for order in range(2):
                    lhs = jnp.where(mask, far, own) if order else jnp.where(mask, own, far)
                    pltpu.matmul_acc_lhs(
                        accumulators[order], lhs.astype(B16), load_staged_rhs=0 if fresh else None
                    )
                    pre.append(pltpu.matmul_pop(accumulators[order]))
                mixed = jnp.where(mask, *pre)
                turned(level, tile, mixed[:, :LANES], mixed[:, LANES:])

            one_tile(0, True)

            @pl.loop(1, 2 * half_tiles)
            def _(tile):
                one_tile(tile, False)

        row_tiles = rows // TILE
        few = min(TILE, row_tiles)

        @pl.loop(0, pairs // 2 * (row_tiles // few))
        def _(item):
            duo, start = item // (row_tiles // few), item % (row_tiles // few) * few
            for order in range(2):
                pltpu.matmul_push_rhs(node_maps[duo], 0, order)
                pltpu.matmul_push_rhs(leaf_maps[2 * duo + order], 1, order)
            strips = [pl.ds(pl.multiple_of((start + i) * TILE, TILE), TILE) for i in range(few)]
            for i, strip in enumerate(strips):
                speeds = packed_ref[strip, 2 * LANES :]
                pltpu.matmul_acc_lhs(
                    accumulators[2 * few + i],
                    jnp.concatenate([speeds, speeds], axis=1),
                    load_staged_rhs=0 if i < 2 else None,
                )
            for i, strip in enumerate(strips):
                for order in range(2):
                    pltpu.matmul_acc_lhs(
                        accumulators[2 * i + order],
                        packed_ref[strip, : 2 * LANES],
                        load_staged_rhs=1 if i == 0 else None,
                    )
            for i in range(few):
                turns = pltpu.matmul_pop(accumulators[2 * few + i])
                for order in range(2):
                    tile = (start + i) * pairs + 2 * duo + order
                    sine, cosine = sine_cosine(turns[:, order * LANES : (order + 1) * LANES])
                    twice_ref[tile] = cosine + cosine
                    cosines[0][tile] = cosine
                    sines[0][tile] = sine
                    state_a[tile] = pltpu.matmul_pop(accumulators[2 * i + order]).astype(B16)

        flowing = False
        for level in range(levels):
            if not flowing:
                load_maps(level)
            if plan[level][0] == "rows":
                within_tiles(level)
                continue
            if not flowing:
                for unit in range(units):
                    send(level, 0, unit, True)

            @pl.loop(0, blocks - 1)
            def _(block):
                for unit in range(units):
                    finish(level, block, unit)
                    send(level, block + 1, unit, False)

            flowing = blocks > 2 and level + 1 < levels and plan[level + 1][0] == "tiles"
            if flowing:
                load_maps(level + 1)
            for unit in range(units):
                finish(level, blocks - 1, unit)
                if flowing:
                    send(level + 1, 0, unit, True)

        final = states[levels % 2]
        share = row_tiles // 2
        for pair in range(pairs):
            for order in range(2):
                pltpu.matmul_push_rhs(eval_maps[pair], pair % 2, order)
            for i in range(share):
                for order in range(2):
                    pltpu.matmul_acc_lhs(
                        accumulators[2 * i + order],
                        final[(order * share + i) * pairs + pair],
                        load_staged_rhs=pair % 2 if i == 0 else None,
                    )
        for i in range(share):
            for order in range(2):
                top = (order * share + i) * TILE
                out_ref[top : top + TILE, :] = pltpu.matmul_pop(
                    accumulators[2 * i + order]
                ).astype(B16)

    pl.run_scoped(
        run, *[pltpu.ACC(order)((TILE, 2 * LANES), F32) for _ in range(units) for order in range(2)]
    )


def split_nodes(rank):
    nodes = np.cos(np.pi * (np.arange(rank) + 0.5) / rank) / 2
    pieces = []
    rest = np.tile(nodes, LANES // rank)
    for _ in range(3):
        piece = rest.astype(B16)
        pieces.append(piece.astype(np.float32))
        rest = rest - piece.astype(np.float64)
    return np.stack(pieces)


def level_plan(levels, local_levels, rows_per):
    plan = [("tiles", level) for level in range(local_levels)]
    stride = rows_per
    for _ in range(levels - local_levels):
        if stride < TILE:
            plan.append(("rows", stride))
        else:
            plan.append(("tiles", local_levels + (stride // TILE).bit_length() - 1))
        stride *= 2
    return tuple(plan)


def on_device(charges, source_order, velocity, leaf_weight, mixing, eval_weight, target_order):
    leaf = leaf_weight.shape[0] // 2
    width = leaf_weight.shape[1]
    boxes = charges.shape[1] // leaf
    group = LANES // leaf
    pairs = group // 2
    rows = boxes // group
    devices = lax.axis_size("wide") * lax.axis_size("narrow")
    rows_per = rows // devices
    levels = mixing.shape[0]
    local_levels = levels - (devices.bit_length() - 1)
    assert width == LANES and 1 << local_levels == pairs

    charge_rows = charges.reshape(2, rows, LANES).transpose(1, 0, 2).reshape(2 * rows, LANES)
    packed = pl.pallas_call(
        functools.partial(pack_kernel, leaf),
        out_shape=jax.ShapeDtypeStruct((rows, 3 * LANES), B16),
        compiler_params=vmem(8),
        name="pack",
    )(charge_rows, source_order.reshape(rows, LANES), velocity.reshape(boxes // LANES, LANES))

    packed = lax.all_to_all(
        packed.reshape(devices, rows_per, 3 * LANES), AXES, 0, 0, tiled=True
    ).reshape(rows, 3 * LANES)

    square = (2 * LANES, 2 * LANES)
    weights = pl.pallas_call(
        functools.partial(maps_kernel, leaf),
        out_shape=[
            jax.ShapeDtypeStruct((levels, 2, *square), B16),
            jax.ShapeDtypeStruct((pairs, *square), B16),
            jax.ShapeDtypeStruct((pairs, *square), B16),
            jax.ShapeDtypeStruct((pairs // 2, *square), B16),
        ],
        compiler_params=vmem(20),
        cost_estimate=pl.CostEstimate(flops=10**9, bytes_accessed=10**7, transcendentals=0),
        name="maps",
    )(leaf_weight, mixing, eval_weight, jnp.asarray(split_nodes(width // 2)))

    tiles = rows // TILE * pairs
    state = pltpu.VMEM((tiles, TILE, 2 * LANES), B16)
    table = pltpu.VMEM((tiles, TILE, LANES), F32)
    values = pl.pallas_call(
        functools.partial(butterfly_kernel, level_plan(levels, local_levels, rows_per)),
        out_shape=jax.ShapeDtypeStruct((rows, 2 * LANES), B16),
        scratch_shapes=[state, state] + [table] * 7,
        compiler_params=vmem(32),
        name="butterfly",
    )(packed, *weights)

    values = lax.all_to_all(
        values.reshape(devices, rows_per, 2 * LANES), AXES, 0, 0, tiled=True
    ).reshape(rows, 2 * LANES)

    out = pl.pallas_call(
        functools.partial(unpack_kernel, leaf),
        out_shape=jax.ShapeDtypeStruct((2 * rows, LANES), F32),
        compiler_params=vmem(8),
        name="unpack",
    )(values, target_order.reshape(rows, LANES))
    return out.reshape(rows, 2, LANES).transpose(1, 0, 2).reshape(2, rows * LANES)


def solution(mesh):
    mapped = jax.shard_map(
        on_device,
        mesh=mesh,
        in_specs=(
            P(None, AXES),
            P(AXES),
            P(AXES),
            P(),
            P(),
            P(),
            P(AXES),
        ),
        out_specs=P(None, AXES),
        check_vma=False,
    )

    def program(*arrays):
        with jax.sharding.use_abstract_mesh(mesh.abstract_mesh):
            return mapped(*arrays)

    return program
```

```python
import functools
import math

import jax
import jax.numpy as jnp
import numpy as np
from jax import lax
from jax.experimental import pallas as pl
from jax.experimental.pallas import tpu as pltpu
from jax.sharding import PartitionSpec as P

LANES = 128
HALF = LANES // 2
TILE = 16
AXES = ("wide", "narrow")
F32, B16 = jnp.float32, jnp.bfloat16
UNITS = 32
ROOM = 200
def vmem(mebibytes):
    return pltpu.CompilerParams(vmem_limit_bytes=mebibytes * 2**20)


def lane_index(shape):
    return lax.broadcasted_iota(jnp.int32, shape, len(shape) - 1)


def row_index(shape):
    return lax.broadcasted_iota(jnp.int32, shape, len(shape) - 2)


def swapped(x):
    return pltpu.roll(x, HALF, 1)


def odd_bits(number):
    for shift in (16, 8, 4, 2, 1):
        number = number ^ lax.shift_right_logical(number, shift)
    return number & 1


def device_number():
    return lax.axis_index("wide") * lax.axis_size("narrow") + lax.axis_index("narrow")


def pack_kernel(leaf, charges_ref, order_ref, velocity_ref, out_ref):
    rows = order_ref.shape[0]
    odd = odd_bits(device_number()) == 1
    step = min(rows, 64)
    lanes = lane_index((step, LANES))
    group = LANES // leaf

    @pl.loop(0, rows // step)
    def _(block):
        here = pl.ds(pl.multiple_of(block * step, step), step)
        index = order_ref[here, :] + lanes // leaf * leaf
        for part in range(2):
            values = charges_ref[pl.ds(block * (2 * step) + part, step, stride=2), :]
            values = jnp.take_along_axis(values, index, axis=1)
            values = jnp.where(odd, swapped(values), values)
            out_ref[here, part * LANES : (part + 1) * LANES] = values.astype(B16)

    speeds = velocity_ref[...].astype(F32)
    lanes = lane_index(speeds.shape)
    speeds = jnp.take_along_axis(speeds, lanes ^ jnp.where(odd, group // 2, 0), axis=1)
    count = speeds.shape[0]
    speeds = jnp.broadcast_to(speeds[:, None, :], (count, leaf, LANES)).reshape(rows, LANES)
    own = lane_index(speeds.shape) // group == row_index(speeds.shape) % leaf
    speeds = jnp.where(own, speeds, 0.0)
    shift = group
    while shift < LANES:
        speeds = speeds + pltpu.roll(speeds, shift, 1)
        shift *= 2
    out_ref[:, 2 * LANES :] = speeds.astype(B16)


def unpack_kernel(leaf, values_ref, order_ref, out_ref):
    rows = order_ref.shape[0]
    odd = odd_bits(device_number()) == 1
    step = min(rows, 64)
    base = lane_index((step, LANES)) // leaf * leaf ^ jnp.where(odd, HALF, 0)

    @pl.loop(0, rows // step)
    def _(block):
        here = pl.ds(pl.multiple_of(block * step, step), step)
        index = order_ref[here, :] + base
        for part in range(2):
            values = values_ref[here, part * LANES : (part + 1) * LANES].astype(F32)
            out_ref[pl.ds(block * (2 * step) + part, step, stride=2), :] = jnp.take_along_axis(
                values, index, axis=1
            )


def odd_pair(pair):
    return bin(pair).count("1") % 2 == 1


def boxes_of_pair(pair, pairs):
    return (pair + pairs, pair) if odd_pair(pair) else (pair, pair + pairs)


def maps_kernel(leaf, mixing_ref, eval_ref, weights):
    levels = mixing_ref.shape[0]
    pairs = LANES // leaf // 2
    low = lane_index((HALF, LANES)) < HALF

    @pl.loop(0, levels)
    def _(level):
        for source in range(2):
            for part in range(2):
                rows = slice(part * HALF, (part + 1) * HALF)
                to_first = mixing_ref[level, 0, source, rows, :].astype(F32)
                to_second = mixing_ref[level, 1, source, rows, :].astype(F32)
                first_far, second_far = swapped(to_first), swapped(to_second)
                for order in range(2):
                    top = part * LANES + (source ^ order) * HALF
                    place = weights.at[2 * level + order, top : top + HALF]
                    if order == 0:
                        real = jnp.where(low, to_first, second_far)
                        imag = jnp.where(low, first_far, to_second)
                    else:
                        real = jnp.where(low, to_second, first_far)
                        imag = jnp.where(low, second_far, to_first)
                    place[:, :LANES] = real.astype(B16)
                    place[:, LANES:] = imag.astype(B16)

    box_of_lane = lane_index((HALF, LANES)) // leaf
    slot = lane_index((2 * leaf, 2 * LANES))
    spread = (slot // LANES * leaf + slot % leaf == row_index((2 * leaf, 2 * LANES))).astype(B16)
    eval_rows = jnp.dot(eval_ref[...], spread, preferred_element_type=F32)
    for pair in range(pairs):
        for number, box in enumerate(boxes_of_pair(pair, pairs)):
            for part in range(2):
                top = (2 * part + number) * HALF
                for side in range(2):
                    lanes = slice(side * LANES, (side + 1) * LANES)
                    block = eval_rows[part * HALF : (part + 1) * HALF, lanes]
                    weights[2 * levels + pair, top : top + HALF, lanes] = jnp.where(
                        box_of_lane == box, block, 0.0
                    ).astype(B16)


def first_maps(leaf, pairs, leaf_ref, nodes_ref, leaf_maps, node_maps):
    group = 2 * pairs
    leaf_rows = leaf_ref[...].astype(F32)
    shape = (LANES, LANES)
    low = lane_index(shape) < HALF
    box_of_row = row_index(shape) // leaf
    node_row = row_index(shape)
    nodes = jnp.zeros(shape, F32)
    for piece in range(3):
        nodes = jnp.where(node_row // group == piece, nodes_ref[piece : piece + 1, :], nodes)
    for part in range(2):
        tiled = jnp.broadcast_to(
            leaf_rows[part * leaf : (part + 1) * leaf][None], (group, leaf, LANES)
        ).reshape(shape)
        far = swapped(tiled)
        here = slice(part * LANES, (part + 1) * LANES)
        for pair in range(pairs):
            left, right = boxes_of_pair(pair, pairs)
            first, second = box_of_row == left, box_of_row == right
            leaf_maps[pair, here, :LANES] = jnp.where(
                low, jnp.where(first, tiled, 0.0), jnp.where(second, far, 0.0)
            ).astype(B16)
            leaf_maps[pair, here, LANES:] = jnp.where(
                low, jnp.where(first, far, 0.0), jnp.where(second, tiled, 0.0)
            ).astype(B16)
            lanes = slice(pair % 2 * LANES, (pair % 2 + 1) * LANES)
            mine = node_row % group == jnp.where(low, left, right)
            node_maps[pair // 2, here, lanes] = jnp.where(
                mine, nodes if part == 0 else 0.0, 0.0
            ).astype(B16)


def sine_cosine(turns):
    u = turns - jnp.round(turns)
    w = u * u
    sin_terms = [(-1) ** i * math.pi ** (2 * i + 1) / math.factorial(2 * i + 1) for i in range(7)]
    cos_terms = [(-1) ** i * math.pi ** (2 * i) / math.factorial(2 * i) for i in range(7)]
    half_sin = jnp.full_like(w, sin_terms[-1])
    for term in sin_terms[-2::-1]:
        half_sin = half_sin * w + term
    half_sin = half_sin * u
    half_cos = jnp.full_like(w, cos_terms[-1])
    for term in cos_terms[-2::-1]:
        half_cos = half_cos * w + term
    twice = half_sin + half_sin
    return twice * half_cos, 1.0 - twice * half_sin


def butterfly_kernel(
    plan, leaf, pairs, packed_ref, leaf_ref, nodes_ref, weights_ref, out_ref,
    leaf_maps, node_maps, weights, arrived,
    state_a, state_b, twice_ref, *tables,
):
    rows = packed_ref.shape[0]
    levels = len(plan)
    states = (state_a, state_b)
    cosines, sines = tables[:3], tables[3:]
    low = lane_index((TILE, LANES)) < HALF
    low16 = lax.broadcasted_iota(jnp.int16, (TILE, LANES), 1) < jnp.int16(HALF)

    def merged(mask, first, second):
        return jnp.concatenate(
            [
                jnp.where(mask, first[:, :LANES], second[:, :LANES]),
                jnp.where(mask, first[:, LANES:], second[:, LANES:]),
            ],
            axis=1,
        )

    def turned(level, tile, real, imag):
        now, last, coming = level % 3, (level - 1) % 3, (level + 1) % 3
        cosine, sine = cosines[now][tile], sines[now][tile]
        target = states[1 - level % 2]
        target[tile, :, :LANES] = (real * cosine - imag * sine).astype(B16)
        target[tile, :, LANES:] = (real * sine + imag * cosine).astype(B16)
        if level + 1 < levels:
            twice = twice_ref[tile]
            last_cosine = cosines[last][tile] if level else 1.0
            cosines[coming][tile] = twice * cosine - last_cosine
            sines[coming][tile] = twice * sine - sines[last][tile] if level else twice * sine

    half_tiles = state_a.shape[0] // 2
    units = min(UNITS, half_tiles)
    blocks = half_tiles // units

    def tiles_of(level, block, unit):
        bit = plan[level][1]
        stride = 1 << bit
        if stride >= units:
            start = block * units
            base = lax.shift_left(lax.shift_right_logical(start, bit), bit + 1) | (
                start & (stride - 1)
            )
            tile = base + unit
        else:
            tile = block * (2 * units) + (unit >> bit << (bit + 1) | unit & (stride - 1))
        return tile, tile + stride

    bounds = (0, 2 * levels, 2 * levels + pairs)
    fetches = [
        pltpu.make_async_copy(
            weights_ref.at[start:stop], weights.at[start:stop], arrived.at[number]
        )
        for number, (start, stop) in enumerate(zip(bounds, bounds[1:]))
    ]
    for fetch in fetches:
        fetch.start()
    first_maps(leaf, pairs, leaf_ref, nodes_ref, leaf_maps, node_maps)

    def run(*accumulators):
        def load_maps(level):
            for order in range(2):
                pltpu.matmul_push_rhs(weights[2 * level + order], 0, order)

        def send(level, block, unit, fresh):
            source = states[level % 2]
            first, second = (source[tile] for tile in tiles_of(level, block, unit))
            for order in range(2):
                pltpu.matmul_acc_lhs(
                    accumulators[2 * unit + order],
                    merged(low16, *((second, first) if order else (first, second))),
                    load_staged_rhs=0 if fresh and unit == 0 else None,
                )

        def finish(level, block, unit):
            one, other = (pltpu.matmul_pop(accumulators[2 * unit + order]) for order in range(2))
            for target, tile in enumerate(tiles_of(level, block, unit)):
                left, right = (other, one) if target else (one, other)
                turned(
                    level, tile,
                    jnp.where(low, left[:, :LANES], right[:, :LANES]),
                    jnp.where(low, left[:, LANES:], right[:, LANES:]),
                )

        def within_tiles(level):
            stride = plan[level][1]
            upper = row_index((TILE, 2 * LANES)) // stride % 2 == 1
            mask = (lane_index((TILE, 2 * LANES)) % LANES < HALF) != upper

            def one_tile(tile, fresh):
                own = states[level % 2][tile].astype(F32)
                far = jnp.where(
                    upper, pltpu.roll(own, stride, 0), pltpu.roll(own, TILE - stride, 0)
                )
                pre = []
                for order in range(2):
                    lhs = jnp.where(mask, far, own) if order else jnp.where(mask, own, far)
                    pltpu.matmul_acc_lhs(
                        accumulators[order], lhs.astype(B16), load_staged_rhs=0 if fresh else None
                    )
                    pre.append(pltpu.matmul_pop(accumulators[order]))
                mixed = jnp.where(mask, *pre)
                turned(level, tile, mixed[:, :LANES], mixed[:, LANES:])

            one_tile(0, True)

            @pl.loop(1, 2 * half_tiles)
            def _(tile):
                one_tile(tile, False)

        row_tiles = rows // TILE
        few = min(TILE, row_tiles)

        @pl.loop(0, pairs // 2 * (row_tiles // few))
        def _(item):
            duo, start = item // (row_tiles // few), item % (row_tiles // few) * few
            for order in range(2):
                pltpu.matmul_push_rhs(node_maps[duo], 0, order)
                pltpu.matmul_push_rhs(leaf_maps[2 * duo + order], 1, order)
            strips = [pl.ds(pl.multiple_of((start + i) * TILE, TILE), TILE) for i in range(few)]
            for i, strip in enumerate(strips):
                speeds = packed_ref[strip, 2 * LANES :]
                pltpu.matmul_acc_lhs(
                    accumulators[2 * few + i],
                    jnp.concatenate([speeds, speeds], axis=1),
                    load_staged_rhs=0 if i < 2 else None,
                )
            for i, strip in enumerate(strips):
                for order in range(2):
                    pltpu.matmul_acc_lhs(
                        accumulators[2 * i + order],
                        packed_ref[strip, : 2 * LANES],
                        load_staged_rhs=1 if i == 0 else None,
                    )
            for i in range(few):
                turns = pltpu.matmul_pop(accumulators[2 * few + i])
                for order in range(2):
                    tile = (start + i) * pairs + 2 * duo + order
                    sine, cosine = sine_cosine(turns[:, order * LANES : (order + 1) * LANES])
                    twice_ref[tile] = cosine + cosine
                    cosines[0][tile] = cosine
                    sines[0][tile] = sine
                    state_a[tile] = pltpu.matmul_pop(accumulators[2 * i + order]).astype(B16)

        fetches[0].wait()
        flowing = False
        for level in range(levels):
            if not flowing:
                load_maps(level)
            if plan[level][0] == "rows":
                within_tiles(level)
                continue
            if not flowing:
                for unit in range(units):
                    send(level, 0, unit, True)

            @pl.loop(0, blocks - 1)
            def _(block):
                for unit in range(units):
                    finish(level, block, unit)
                    send(level, block + 1, unit, False)

            flowing = blocks > 2 and level + 1 < levels and plan[level + 1][0] == "tiles"
            if flowing:
                load_maps(level + 1)
            for unit in range(units):
                finish(level, blocks - 1, unit)
                if flowing:
                    send(level + 1, 0, unit, True)

        fetches[1].wait()
        final = states[levels % 2]
        share = row_tiles // 2
        for pair in range(pairs):
            for order in range(2):
                pltpu.matmul_push_rhs(weights[2 * levels + pair], pair % 2, order)
            for i in range(share):
                for order in range(2):
                    pltpu.matmul_acc_lhs(
                        accumulators[2 * i + order],
                        final[(order * share + i) * pairs + pair],
                        load_staged_rhs=pair % 2 if i == 0 else None,
                    )
        for i in range(share):
            for order in range(2):
                top = (order * share + i) * TILE
                out_ref[top : top + TILE, :] = pltpu.matmul_pop(
                    accumulators[2 * i + order]
                ).astype(B16)

    pl.run_scoped(
        run, *[pltpu.ACC(order)((TILE, 2 * LANES), F32) for _ in range(units) for order in range(2)]
    )


def split_nodes(rank):
    nodes = np.cos(np.pi * (np.arange(rank) + 0.5) / rank) / 2
    pieces = []
    rest = np.tile(nodes, LANES // rank)
    for _ in range(3):
        piece = rest.astype(B16)
        pieces.append(piece.astype(np.float32))
        rest = rest - piece.astype(np.float64)
    return np.stack(pieces)


def level_plan(levels, local_levels, rows_per):
    plan = [("tiles", level) for level in range(local_levels)]
    stride = rows_per
    for _ in range(levels - local_levels):
        if stride < TILE:
            plan.append(("rows", stride))
        else:
            plan.append(("tiles", local_levels + (stride // TILE).bit_length() - 1))
        stride *= 2
    return tuple(plan)


def on_device(charges, source_order, velocity, leaf_weight, mixing, eval_weight, target_order):
    leaf = leaf_weight.shape[0] // 2
    width = leaf_weight.shape[1]
    boxes = charges.shape[1] // leaf
    group = LANES // leaf
    pairs = group // 2
    rows = boxes // group
    devices = lax.axis_size("wide") * lax.axis_size("narrow")
    rows_per = rows // devices
    levels = mixing.shape[0]
    local_levels = levels - (devices.bit_length() - 1)
    assert width == LANES and 1 << local_levels == pairs

    charge_rows = charges.reshape(2, rows, LANES).transpose(1, 0, 2).reshape(2 * rows, LANES)
    packed = pl.pallas_call(
        functools.partial(pack_kernel, leaf),
        out_shape=jax.ShapeDtypeStruct((rows, 3 * LANES), B16),
        compiler_params=vmem(56),
        name="pack",
    )(charge_rows, source_order.reshape(rows, LANES), velocity.reshape(boxes // LANES, LANES))

    packed = lax.all_to_all(
        packed.reshape(devices, rows_per, 3 * LANES), AXES, 0, 0, tiled=True
    ).reshape(rows, 3 * LANES)

    square = (2 * LANES, 2 * LANES)
    count = 2 * levels + pairs
    weights = pl.pallas_call(
        functools.partial(maps_kernel, leaf),
        grid=(1,),
        out_specs=pl.BlockSpec((count, *square), lambda step: (0, 0, 0)),
        out_shape=jax.ShapeDtypeStruct((max(count, ROOM), *square), B16),
        compiler_params=vmem(56),
        cost_estimate=pl.CostEstimate(flops=10**9, bytes_accessed=10**7, transcendentals=0),
        name="maps",
    )(mixing, eval_weight)

    tiles = rows // TILE * pairs
    state = pltpu.VMEM((tiles, TILE, 2 * LANES), B16)
    table = pltpu.VMEM((tiles, TILE, LANES), F32)
    values = pl.pallas_call(
        functools.partial(butterfly_kernel, level_plan(levels, local_levels, rows_per), leaf, pairs),
        out_shape=jax.ShapeDtypeStruct((rows, 2 * LANES), B16),
        in_specs=[pl.BlockSpec(memory_space=pltpu.VMEM)] * 3
        + [pl.BlockSpec(memory_space=pltpu.HBM)],
        scratch_shapes=[
            pltpu.VMEM((pairs, *square), B16),
            pltpu.VMEM((pairs // 2, *square), B16),
            pltpu.VMEM((count, *square), B16),
            pltpu.SemaphoreType.DMA((2,)),
            state,
            state,
        ]
        + [table] * 7,
        compiler_params=vmem(40),
        name="butterfly",
    )(packed, leaf_weight, jnp.asarray(split_nodes(width // 2)), weights)

    values = lax.all_to_all(
        values.reshape(devices, rows_per, 2 * LANES), AXES, 0, 0, tiled=True
    ).reshape(rows, 2 * LANES)

    out = pl.pallas_call(
        functools.partial(unpack_kernel, leaf),
        out_shape=jax.ShapeDtypeStruct((2 * rows, LANES), F32),
        compiler_params=vmem(8),
        name="unpack",
    )(values, target_order.reshape(rows, LANES))
    return out.reshape(rows, 2, LANES).transpose(1, 0, 2).reshape(2, rows * LANES)


def solution(mesh):
    mapped = jax.shard_map(
        on_device,
        mesh=mesh,
        in_specs=(
            P(None, AXES),
            P(AXES),
            P(AXES),
            P(),
            P(),
            P(),
            P(AXES),
        ),
        out_specs=P(None, AXES),
        check_vma=False,
    )

    def program(*arrays):
        with jax.sharding.use_abstract_mesh(mesh.abstract_mesh):
            return mapped(*arrays)

    return program
```

```python
import functools
import math

import jax
import jax.numpy as jnp
import numpy as np
from jax import lax
from jax.experimental import pallas as pl
from jax.experimental.pallas import tpu as pltpu
from jax.sharding import PartitionSpec as P

LANES = 128
HALF = LANES // 2
QUARTER = LANES // 4
TILE = 16
AXES = ("wide", "narrow")
F32, B16 = jnp.float32, jnp.bfloat16
UNITS = 32
ROOM = 200
def vmem(mebibytes):
    return pltpu.CompilerParams(vmem_limit_bytes=mebibytes * 2**20)


def lane_index(shape):
    return lax.broadcasted_iota(jnp.int32, shape, len(shape) - 1)


def row_index(shape):
    return lax.broadcasted_iota(jnp.int32, shape, len(shape) - 2)


def swapped(x):
    return pltpu.roll(x, HALF, 1)


def odd_bits(number):
    for shift in (16, 8, 4, 2, 1):
        number = number ^ lax.shift_right_logical(number, shift)
    return number & 1


def device_number():
    return lax.axis_index("wide") * lax.axis_size("narrow") + lax.axis_index("narrow")


def pack_kernel(leaf, charges_ref, order_ref, velocity_ref, out_ref):
    rows = order_ref.shape[0]
    odd = odd_bits(device_number()) == 1
    step = min(rows, 64)
    lanes = lane_index((step, LANES))
    group = LANES // leaf

    @pl.loop(0, rows // step)
    def _(block):
        here = pl.ds(pl.multiple_of(block * step, step), step)
        index = order_ref[here, :] + lanes // leaf * leaf
        for part in range(2):
            values = charges_ref[pl.ds(block * (2 * step) + part, step, stride=2), :]
            values = jnp.take_along_axis(values, index, axis=1)
            values = jnp.where(odd, swapped(values), values)
            out_ref[here, part * LANES : (part + 1) * LANES] = values.astype(B16)

    speeds = velocity_ref[...].astype(F32)
    lanes = lane_index(speeds.shape)
    speeds = jnp.take_along_axis(speeds, lanes ^ jnp.where(odd, group // 2, 0), axis=1)
    count = speeds.shape[0]
    speeds = jnp.broadcast_to(speeds[:, None, :], (count, leaf, LANES)).reshape(rows, LANES)
    own = lane_index(speeds.shape) // group == row_index(speeds.shape) % leaf
    speeds = jnp.where(own, speeds, 0.0)
    shift = group
    while shift < LANES:
        speeds = speeds + pltpu.roll(speeds, shift, 1)
        shift *= 2
    out_ref[:, 2 * LANES :] = speeds.astype(B16)


def unpack_kernel(leaf, values_ref, order_ref, out_ref):
    rows = order_ref.shape[0]
    odd = odd_bits(device_number()) == 1
    step = min(rows, 64)
    base = lane_index((step, LANES)) // leaf * leaf ^ jnp.where(odd, HALF, 0)

    @pl.loop(0, rows // step)
    def _(block):
        here = pl.ds(pl.multiple_of(block * step, step), step)
        index = order_ref[here, :] + base
        for part in range(2):
            values = values_ref[here, part * LANES : (part + 1) * LANES].astype(F32)
            out_ref[pl.ds(block * (2 * step) + part, step, stride=2), :] = jnp.take_along_axis(
                values, index, axis=1
            )


def odd_pair(pair):
    return bin(pair).count("1") % 2 == 1


def mirrored(index):
    place = index % HALF
    return index - place + jnp.where(place < QUARTER, place, HALF + QUARTER - 1 - place)


def sign_of(index):
    return jnp.where((index >= HALF) & (index % HALF >= QUARTER), -1.0, 1.0)


def boxes_of_pair(pair, pairs):
    return (pair + pairs, pair) if odd_pair(pair) else (pair, pair + pairs)


def maps_kernel(leaf, mixing_ref, eval_ref, weights):
    levels = mixing_ref.shape[0]
    pairs = LANES // leaf // 2
    low = lane_index((HALF, LANES)) < HALF
    shape = (LANES, LANES)
    mirror = jnp.where(
        row_index(shape) == mirrored(lane_index(shape)), sign_of(lane_index(shape)), 0.0
    ).astype(B16)
    mirror_back = jnp.where(
        lane_index(shape) == mirrored(row_index(shape)), sign_of(row_index(shape)), 0.0
    ).astype(B16)

    def mirrored_map(matrix):
        matrix = jnp.dot(matrix, mirror, preferred_element_type=F32).astype(B16)
        return jnp.dot(mirror_back, matrix, preferred_element_type=F32)

    @pl.loop(0, levels)
    def _(level):
        for source in range(2):
            both = [mirrored_map(mixing_ref[level, target, source]) for target in range(2)]
            for part in range(2):
                to_first, to_second = (
                    matrix[part * HALF : (part + 1) * HALF] for matrix in both
                )
                first_far, second_far = swapped(to_first), swapped(to_second)
                for order in range(2):
                    top = part * LANES + (source ^ order) * HALF
                    place = weights.at[2 * level + order, top : top + HALF]
                    if order == 0:
                        real = jnp.where(low, to_first, second_far)
                        imag = jnp.where(low, first_far, to_second)
                    else:
                        real = jnp.where(low, to_second, first_far)
                        imag = jnp.where(low, second_far, to_first)
                    place[:, :LANES] = real.astype(B16)
                    place[:, LANES:] = imag.astype(B16)

    box_of_lane = lane_index((HALF, LANES)) // leaf
    slot = lane_index((2 * leaf, 2 * LANES))
    spread = (slot // LANES * leaf + slot % leaf == row_index((2 * leaf, 2 * LANES))).astype(B16)
    eval_rows = jnp.dot(mirror_back, eval_ref[...], preferred_element_type=F32).astype(B16)
    eval_rows = jnp.dot(eval_rows, spread, preferred_element_type=F32)
    for pair in range(pairs):
        for number, box in enumerate(boxes_of_pair(pair, pairs)):
            for part in range(2):
                top = (2 * part + number) * HALF
                for side in range(2):
                    lanes = slice(side * LANES, (side + 1) * LANES)
                    block = eval_rows[part * HALF : (part + 1) * HALF, lanes]
                    weights[2 * levels + pair, top : top + HALF, lanes] = jnp.where(
                        box_of_lane == box, block, 0.0
                    ).astype(B16)


def first_maps(leaf, pairs, leaf_ref, nodes_ref, leaf_maps, node_maps):
    group = 2 * pairs
    leaf_rows = leaf_ref[...].astype(F32)
    lanes = lane_index(leaf_rows.shape)
    leaf_rows = jnp.take_along_axis(leaf_rows, mirrored(lanes), axis=1) * sign_of(lanes)
    shape = (LANES, LANES)
    in_left = lane_index(shape) % HALF < QUARTER
    low = lane_index(shape) < HALF
    box_of_row = row_index(shape) // leaf
    node_row = row_index(shape)
    nodes = jnp.zeros(shape, F32)
    for piece in range(3):
        nodes = jnp.where(node_row // group == piece, nodes_ref[piece : piece + 1, :], nodes)
    for part in range(2):
        tiled = jnp.broadcast_to(
            leaf_rows[part * leaf : (part + 1) * leaf][None], (group, leaf, LANES)
        ).reshape(shape)
        far = swapped(tiled)
        here = slice(part * LANES, (part + 1) * LANES)
        for pair in range(pairs):
            left, right = boxes_of_pair(pair, pairs)
            first, second = box_of_row == left, box_of_row == right
            leaf_maps[pair, here, :LANES] = jnp.where(
                low, jnp.where(first, tiled, 0.0), jnp.where(second, far, 0.0)
            ).astype(B16)
            leaf_maps[pair, here, LANES:] = jnp.where(
                low, jnp.where(first, far, 0.0), jnp.where(second, tiled, 0.0)
            ).astype(B16)
            lanes = slice(pair % 2 * LANES, (pair % 2 + 1) * LANES)
            mine = (node_row % group == jnp.where(in_left, left, right)) & (
                lane_index(shape) // HALF == part
            )
            node_maps[pair // 2, here, lanes] = jnp.where(mine, nodes, 0.0).astype(B16)


def sine_cosine(turns):
    u = turns - jnp.round(turns)
    w = u * u
    sin_terms = [(-1) ** i * math.pi ** (2 * i + 1) / math.factorial(2 * i + 1) for i in range(7)]
    cos_terms = [(-1) ** i * math.pi ** (2 * i) / math.factorial(2 * i) for i in range(7)]
    half_sin = jnp.full_like(w, sin_terms[-1])
    for term in sin_terms[-2::-1]:
        half_sin = half_sin * w + term
    half_sin = half_sin * u
    half_cos = jnp.full_like(w, cos_terms[-1])
    for term in cos_terms[-2::-1]:
        half_cos = half_cos * w + term
    twice = half_sin + half_sin
    return twice * half_cos, 1.0 - twice * half_sin


def reversed_bits(number, bits):
    return sum((number >> bit & 1) << (bits - 1 - bit) for bit in range(bits))


def butterfly_kernel(
    plan, leaf, pairs, packed_ref, leaf_ref, nodes_ref, weights_ref, out_ref,
    leaf_maps, node_maps, weights, arrived, state_a, state_b, tables,
):
    rows = packed_ref.shape[0]
    levels = len(plan)
    states = (state_a, state_b)
    rotations = [sum(kind == "tiles" for kind, _ in plan[:level]) for level in range(levels)]
    row_tiles = rows // TILE
    row_bits, pair_bits = row_tiles.bit_length() - 1, pairs.bit_length() - 1
    half_tiles = state_a.shape[0] // 2
    units = min(UNITS, half_tiles)
    blocks = half_tiles // units
    index_bits = row_bits + pair_bits
    bounds = (0, 2 * levels, 2 * levels + pairs)
    fetches = [
        pltpu.make_async_copy(
            weights_ref.at[start:stop], weights.at[start:stop], arrived.at[number]
        )
        for number, (start, stop) in enumerate(zip(bounds, bounds[1:]))
    ]
    for fetch in fetches:
        fetch.start()
    first_maps(leaf, pairs, leaf_ref, nodes_ref, leaf_maps, node_maps)

    low = lax.broadcasted_iota(jnp.int16, (TILE, LANES), 1) < jnp.int16(HALF)
    lanes = lane_index((TILE // 2, LANES))
    upper_rows = lanes // HALF * QUARTER + lanes % QUARTER
    lower_rows = upper_rows + HALF

    def place_of(row_tile, pair):
        return reversed_bits(pair, pair_bits) << row_bits | reversed_bits(row_tile, row_bits)

    def merged(first, second):
        return jnp.concatenate(
            [
                jnp.where(low, first[:, :LANES], second[:, :LANES]),
                jnp.where(low, first[:, LANES:], second[:, LANES:]),
            ],
            axis=1,
        )

    def spread(table):
        return jnp.concatenate(
            [
                jnp.take_along_axis(table, upper_rows, axis=1),
                jnp.take_along_axis(table, lower_rows, axis=1),
            ],
            axis=0,
        )

    def moved(place, count):
        count = count % index_bits
        return (place << count | place >> (index_bits - count)) & (2 * half_tiles - 1)

    def turned(mixed, level, state, source, place):
        real, imag = mixed[:, :LANES], mixed[:, LANES:]
        cosine, sine = tables[level, source, :, :LANES], tables[level, source, :, LANES:]
        state[place, :, :LANES] = real * cosine - imag * sine
        state[place, :, LANES:] = real * sine + imag * cosine

    def run(*accumulators):
        few = min(TILE, row_tiles)

        @pl.loop(0, pairs // 2 * (row_tiles // few))
        def _(item):
            duo, start = item // (row_tiles // few), item % (row_tiles // few) * few
            base = place_of(start, 2 * duo)
            for order in range(2):
                pltpu.matmul_push_rhs(node_maps[duo], 0, order)
                pltpu.matmul_push_rhs(leaf_maps[2 * duo + order], 1, order)
            strips = [pl.ds(pl.multiple_of((start + i) * TILE, TILE), TILE) for i in range(few)]
            for i in range(0, few, 2):
                speeds = [packed_ref[strips[i + side], 2 * LANES :].astype(F32) for side in range(2)]
                speeds = jnp.concatenate(
                    [
                        jnp.concatenate([part[: TILE // 2] for part in speeds], axis=0),
                        jnp.concatenate([part[TILE // 2 :] for part in speeds], axis=0),
                    ],
                    axis=1,
                ).astype(B16)
                pltpu.matmul_acc_lhs(
                    accumulators[2 * few + i // 2], speeds, load_staged_rhs=0 if i < 4 else None
                )
            for i, strip in enumerate(strips):
                for order in range(2):
                    pltpu.matmul_acc_lhs(
                        accumulators[2 * i + order],
                        packed_ref[strip, : 2 * LANES],
                        load_staged_rhs=1 if i == 0 else None,
                    )
            for i in range(0, few, 2):
                turns = pltpu.matmul_pop(accumulators[2 * few + i // 2])
                for order in range(2):
                    sine, cosine = sine_cosine(turns[:, order * LANES : (order + 1) * LANES])
                    for side in range(2):
                        place = base + place_of(i + side, order)
                        state_a[place] = pltpu.matmul_pop(
                            accumulators[2 * (i + side) + order]
                        ).astype(B16)
                        here = slice(side * TILE // 2, (side + 1) * TILE // 2)
                        cosines, sines = spread(cosine[here]), spread(sine[here])
                        twice = cosines + cosines
                        last_cosines, last_sines = 1.0, 0.0
                        for level in range(levels):
                            spot = moved(base, rotations[level]) + moved(
                                place_of(i + side, order), rotations[level]
                            )
                            tables[level, spot, :, :LANES] = cosines.astype(B16)
                            tables[level, spot, :, LANES:] = sines.astype(B16)
                            cosines, last_cosines = twice * cosines - last_cosines, cosines
                            sines, last_sines = twice * sines - last_sines, sines

        def load_maps(level):
            for order in range(2):
                pltpu.matmul_push_rhs(weights[2 * level + order], 0, order)

        def send(state, block, unit, fresh):
            number = block * units + unit
            first, second = state[number], state[number + half_tiles]
            for order in range(2):
                pltpu.matmul_acc_lhs(
                    accumulators[2 * unit + order],
                    merged(second, first) if order else merged(first, second),
                    load_staged_rhs=0 if fresh and unit == 0 else None,
                )

        def received(unit):
            return [
                pltpu.matmul_pop(accumulators[2 * unit + order]).astype(B16) for order in range(2)
            ]

        def finish(level, target, block, unit):
            one, other = received(unit)
            number = block * units + unit
            turned(merged(one, other), level, target, number, 2 * number)
            turned(merged(other, one), level, target, number + half_tiles, 2 * number + 1)

        def across_tiles(level, source, target, next_level):
            @pl.loop(0, blocks - 1)
            def _(block):
                for unit in range(units):
                    finish(level, target, block, unit)
                    send(source, block + 1, unit, False)

            if next_level is not None:
                load_maps(next_level)
            for unit in range(units):
                finish(level, target, blocks - 1, unit)
                if next_level is not None:
                    send(target, 0, unit, True)

        def within_tiles(level, source, target, stride):
            upper = row_index((TILE, 2 * LANES)) // stride % 2 == 1
            mask = (lane_index((TILE, 2 * LANES)) % LANES < HALF) != upper

            def one_tile(place, fresh):
                own = source[place].astype(F32)
                other = jnp.where(
                    upper, pltpu.roll(own, stride, 0), pltpu.roll(own, TILE - stride, 0)
                )
                pre = []
                for order in range(2):
                    lhs = jnp.where(mask, other, own) if order else jnp.where(mask, own, other)
                    pltpu.matmul_acc_lhs(
                        accumulators[order], lhs.astype(B16), load_staged_rhs=0 if fresh else None
                    )
                    pre.append(pltpu.matmul_pop(accumulators[order]))
                turned(jnp.where(mask, *pre).astype(B16), level, target, place, place)

            one_tile(0, True)

            @pl.loop(1, 2 * half_tiles)
            def _(place):
                one_tile(place, False)

        fetches[0].wait()
        if levels % 2 == 0 and blocks > 3 and all(kind == "tiles" for kind, _ in plan):
            load_maps(0)
            for unit in range(units):
                send(state_a, 0, unit, True)

            @pl.loop(0, levels // 2)
            def _(two):
                across_tiles(2 * two, state_a, state_b, 2 * two + 1)
                across_tiles(2 * two + 1, state_b, state_a, jnp.minimum(2 * two + 2, levels - 1))

            for unit in range(units):
                received(unit)
        else:
            for level, (kind, stride) in enumerate(plan):
                source, target = states[level % 2], states[1 - level % 2]
                load_maps(level)
                if kind == "rows":
                    within_tiles(level, source, target, stride)
                    continue
                for unit in range(units):
                    send(source, 0, unit, True)
                across_tiles(level, source, target, None)

        fetches[1].wait()
        final = states[levels % 2]
        share = row_tiles // 2
        for pair in range(pairs):
            for order in range(2):
                pltpu.matmul_push_rhs(weights[2 * levels + pair], pair % 2, order)
            for i in range(share):
                for order in range(2):
                    pltpu.matmul_acc_lhs(
                        accumulators[2 * i + order],
                        final[place_of(order * share + i, pair)],
                        load_staged_rhs=pair % 2 if i == 0 else None,
                    )
        for i in range(share):
            for order in range(2):
                top = (order * share + i) * TILE
                out_ref[top : top + TILE, :] = pltpu.matmul_pop(
                    accumulators[2 * i + order]
                ).astype(B16)

    pl.run_scoped(
        run, *[pltpu.ACC(order)((TILE, 2 * LANES), F32) for _ in range(units) for order in range(2)]
    )


def split_nodes(rank):
    nodes = np.cos(np.pi * (np.arange(QUARTER) + 0.5) / rank) / 2
    pieces = []
    rest = np.tile(nodes, LANES // QUARTER)
    for _ in range(3):
        piece = rest.astype(B16)
        pieces.append(piece.astype(np.float32))
        rest = rest - piece.astype(np.float64)
    return np.stack(pieces)


def level_plan(levels, local_levels, rows_per):
    plan = [("tiles", level) for level in range(local_levels)]
    stride = rows_per
    for _ in range(levels - local_levels):
        if stride < TILE:
            plan.append(("rows", stride))
        else:
            plan.append(("tiles", local_levels + (stride // TILE).bit_length() - 1))
        stride *= 2
    return tuple(plan)


def on_device(charges, source_order, velocity, leaf_weight, mixing, eval_weight, target_order):
    leaf = leaf_weight.shape[0] // 2
    width = leaf_weight.shape[1]
    boxes = charges.shape[1] // leaf
    group = LANES // leaf
    pairs = group // 2
    rows = boxes // group
    devices = lax.axis_size("wide") * lax.axis_size("narrow")
    rows_per = rows // devices
    levels = mixing.shape[0]
    local_levels = levels - (devices.bit_length() - 1)
    assert width == LANES and 1 << local_levels == pairs

    charge_rows = charges.reshape(2, rows, LANES).transpose(1, 0, 2).reshape(2 * rows, LANES)
    packed = pl.pallas_call(
        functools.partial(pack_kernel, leaf),
        out_shape=jax.ShapeDtypeStruct((rows, 3 * LANES), B16),
        compiler_params=vmem(56),
        name="pack",
    )(charge_rows, source_order.reshape(rows, LANES), velocity.reshape(boxes // LANES, LANES))

    packed = lax.all_to_all(
        packed.reshape(devices, rows_per, 3 * LANES), AXES, 0, 0, tiled=True
    ).reshape(rows, 3 * LANES)

    square = (2 * LANES, 2 * LANES)
    count = 2 * levels + pairs
    weights = pl.pallas_call(
        functools.partial(maps_kernel, leaf),
        grid=(1,),
        out_specs=pl.BlockSpec((count, *square), lambda step: (0, 0, 0)),
        out_shape=jax.ShapeDtypeStruct((max(count, ROOM), *square), B16),
        compiler_params=vmem(56),
        cost_estimate=pl.CostEstimate(flops=10**9, bytes_accessed=10**7, transcendentals=0),
        name="maps",
    )(mixing, eval_weight)

    tiles = rows // TILE * pairs
    state = pltpu.VMEM((tiles, TILE, 2 * LANES), B16)
    values = pl.pallas_call(
        functools.partial(butterfly_kernel, level_plan(levels, local_levels, rows_per), leaf, pairs),
        out_shape=jax.ShapeDtypeStruct((rows, 2 * LANES), B16),
        in_specs=[pl.BlockSpec(memory_space=pltpu.VMEM)] * 3
        + [pl.BlockSpec(memory_space=pltpu.HBM)],
        scratch_shapes=[
            pltpu.VMEM((pairs, *square), B16),
            pltpu.VMEM((pairs // 2, *square), B16),
            pltpu.VMEM((count, *square), B16),
            pltpu.SemaphoreType.DMA((2,)),
            state,
            state,
            pltpu.VMEM((levels, tiles, TILE, 2 * LANES), B16),
        ],
        compiler_params=vmem(40),
        name="butterfly",
    )(packed, leaf_weight, jnp.asarray(split_nodes(width // 2)), weights)

    values = lax.all_to_all(
        values.reshape(devices, rows_per, 2 * LANES), AXES, 0, 0, tiled=True
    ).reshape(rows, 2 * LANES)

    out = pl.pallas_call(
        functools.partial(unpack_kernel, leaf),
        out_shape=jax.ShapeDtypeStruct((2 * rows, LANES), F32),
        compiler_params=vmem(8),
        name="unpack",
    )(values, target_order.reshape(rows, LANES))
    return out.reshape(rows, 2, LANES).transpose(1, 0, 2).reshape(2, rows * LANES)


def solution(mesh):
    mapped = jax.shard_map(
        on_device,
        mesh=mesh,
        in_specs=(
            P(None, AXES),
            P(AXES),
            P(AXES),
            P(),
            P(),
            P(),
            P(AXES),
        ),
        out_specs=P(None, AXES),
        check_vma=False,
    )

    def program(*arrays):
        with jax.sharding.use_abstract_mesh(mesh.abstract_mesh):
            return mapped(*arrays)

    return program
```

```python
import functools
import math

import jax
import jax.numpy as jnp
import numpy as np
from jax import lax
from jax.experimental import pallas as pl
from jax.experimental.pallas import tpu as pltpu
from jax.sharding import PartitionSpec as P

LANES = 128
HALF = LANES // 2
QUARTER = LANES // 4
TILE = 16
AXES = ("wide", "narrow")
F32, B16 = jnp.float32, jnp.bfloat16
UNITS = 32
ROOM = 200
def vmem(mebibytes):
    return pltpu.CompilerParams(vmem_limit_bytes=mebibytes * 2**20)


STRIPS = 4


def lane_index(shape):
    return lax.broadcasted_iota(jnp.int32, shape, len(shape) - 1)


def row_index(shape):
    return lax.broadcasted_iota(jnp.int32, shape, len(shape) - 2)


def swapped(x):
    return pltpu.roll(x, HALF, 1)


def odd_bits(number):
    for shift in (16, 8, 4, 2, 1):
        number = number ^ lax.shift_right_logical(number, shift)
    return number & 1


def device_number():
    return lax.axis_index("wide") * lax.axis_size("narrow") + lax.axis_index("narrow")


def pack_kernel(
    leaf, charges_hbm, order_hbm, velocity_hbm, out_hbm,
    charges_ref, order_ref, velocity_ref, out_ref, arrived, gone,
):
    rows = order_ref.shape[0]
    strip = rows // STRIPS
    group = LANES // leaf
    pairs = ((charges_hbm, charges_ref), (order_hbm, order_ref), (velocity_hbm, velocity_ref))

    def part(ref, number):
        height = ref.shape[0] // STRIPS
        return ref.at[number * height : (number + 1) * height]

    fetches = [
        [
            pltpu.make_async_copy(part(far, number), part(near, number), arrived.at[number, kind])
            for kind, (far, near) in enumerate(pairs)
        ]
        for number in range(STRIPS)
    ]
    stores = [
        pltpu.make_async_copy(part(out_ref, number), part(out_hbm, number), gone.at[number])
        for number in range(STRIPS)
    ]
    for fetch in sum(fetches, []):
        fetch.start()
    odd = odd_bits(device_number()) == 1
    lanes = lane_index((strip, LANES))
    own = lanes // group == row_index((strip, LANES)) % leaf
    speed_lanes = lane_index((strip // leaf, LANES)) ^ jnp.where(odd, group // 2, 0)
    for number in range(STRIPS):
        for fetch in fetches[number]:
            fetch.wait()
        here = slice(number * strip, (number + 1) * strip)
        index = order_ref[here, :] + lanes // leaf * leaf
        for half in range(2):
            values = charges_ref[pl.ds(2 * number * strip + half, strip, stride=2), :]
            values = jnp.take_along_axis(values, index, axis=1)
            values = jnp.where(odd, swapped(values), values)
            out_ref[here, half * LANES : (half + 1) * LANES] = values.astype(B16)
        top = number * strip // leaf
        speeds = velocity_ref[top : top + strip // leaf, :].astype(F32)
        speeds = jnp.take_along_axis(speeds, speed_lanes, axis=1)
        speeds = jnp.broadcast_to(speeds[:, None, :], (strip // leaf, leaf, LANES))
        speeds = jnp.where(own, speeds.reshape(strip, LANES), 0.0)
        shift = group
        while shift < LANES:
            speeds = speeds + pltpu.roll(speeds, shift, 1)
            shift *= 2
        out_ref[here, 2 * LANES :] = speeds.astype(B16)
        stores[number].start()
    for store in stores:
        store.wait()


def unpack_kernel(leaf, values_ref, order_ref, out_hbm, out_ref, gone):
    rows = order_ref.shape[0]
    strip = rows // STRIPS
    odd = odd_bits(device_number()) == 1
    base = lane_index((strip, LANES)) // leaf * leaf ^ jnp.where(odd, HALF, 0)
    stores = []
    for number in range(STRIPS):
        here = slice(number * strip, (number + 1) * strip)
        index = order_ref[here, :] + base
        for half in range(2):
            values = values_ref[here, half * LANES : (half + 1) * LANES].astype(F32)
            out_ref[pl.ds(2 * number * strip + half, strip, stride=2), :] = jnp.take_along_axis(
                values, index, axis=1
            )
        wide = slice(2 * number * strip, 2 * (number + 1) * strip)
        stores.append(pltpu.make_async_copy(out_ref.at[wide], out_hbm.at[wide], gone.at[number]))
        stores[-1].start()
    for store in stores:
        store.wait()


def odd_pair(pair):
    return bin(pair).count("1") % 2 == 1


def mirrored(index):
    place = index % HALF
    return index - place + jnp.where(place < QUARTER, place, HALF + QUARTER - 1 - place)


def sign_of(index):
    return jnp.where((index >= HALF) & (index % HALF >= QUARTER), -1.0, 1.0)


def boxes_of_pair(pair, pairs):
    return (pair + pairs, pair) if odd_pair(pair) else (pair, pair + pairs)


def maps_kernel(leaf, mixing_ref, eval_ref, weights):
    levels = mixing_ref.shape[0]
    pairs = LANES // leaf // 2
    low = lane_index((HALF, LANES)) < HALF
    shape = (LANES, LANES)
    mirror = jnp.where(
        row_index(shape) == mirrored(lane_index(shape)), sign_of(lane_index(shape)), 0.0
    ).astype(B16)
    mirror_back = jnp.where(
        lane_index(shape) == mirrored(row_index(shape)), sign_of(row_index(shape)), 0.0
    ).astype(B16)

    def mirrored_map(matrix):
        matrix = jnp.dot(matrix, mirror, preferred_element_type=F32).astype(B16)
        return jnp.dot(mirror_back, matrix, preferred_element_type=F32)

    @pl.loop(0, levels)
    def _(level):
        for source in range(2):
            both = [mirrored_map(mixing_ref[level, target, source]) for target in range(2)]
            for part in range(2):
                to_first, to_second = (
                    matrix[part * HALF : (part + 1) * HALF] for matrix in both
                )
                first_far, second_far = swapped(to_first), swapped(to_second)
                for order in range(2):
                    top = part * LANES + (source ^ order) * HALF
                    place = weights.at[2 * level + order, top : top + HALF]
                    if order == 0:
                        real = jnp.where(low, to_first, second_far)
                        imag = jnp.where(low, first_far, to_second)
                    else:
                        real = jnp.where(low, to_second, first_far)
                        imag = jnp.where(low, second_far, to_first)
                    place[:, :LANES] = real.astype(B16)
                    place[:, LANES:] = imag.astype(B16)

    box_of_lane = lane_index((HALF, LANES)) // leaf
    slot = lane_index((2 * leaf, 2 * LANES))
    spread = (slot // LANES * leaf + slot % leaf == row_index((2 * leaf, 2 * LANES))).astype(B16)
    eval_rows = jnp.dot(mirror_back, eval_ref[...], preferred_element_type=F32).astype(B16)
    eval_rows = jnp.dot(eval_rows, spread, preferred_element_type=F32)
    for pair in range(pairs):
        for number, box in enumerate(boxes_of_pair(pair, pairs)):
            for part in range(2):
                top = (2 * part + number) * HALF
                for side in range(2):
                    lanes = slice(side * LANES, (side + 1) * LANES)
                    block = eval_rows[part * HALF : (part + 1) * HALF, lanes]
                    weights[2 * levels + pair, top : top + HALF, lanes] = jnp.where(
                        box_of_lane == box, block, 0.0
                    ).astype(B16)


def first_maps(leaf, pairs, leaf_ref, nodes_ref, leaf_maps, node_maps):
    group = 2 * pairs
    leaf_rows = leaf_ref[...].astype(F32)
    lanes = lane_index(leaf_rows.shape)
    leaf_rows = jnp.take_along_axis(leaf_rows, mirrored(lanes), axis=1) * sign_of(lanes)
    shape = (LANES, LANES)
    in_left = lane_index(shape) % HALF < QUARTER
    low = lane_index(shape) < HALF
    box_of_row = row_index(shape) // leaf
    node_row = row_index(shape)
    nodes = jnp.zeros(shape, F32)
    for piece in range(3):
        nodes = jnp.where(node_row // group == piece, nodes_ref[piece : piece + 1, :], nodes)
    for part in range(2):
        tiled = jnp.broadcast_to(
            leaf_rows[part * leaf : (part + 1) * leaf][None], (group, leaf, LANES)
        ).reshape(shape)
        far = swapped(tiled)
        here = slice(part * LANES, (part + 1) * LANES)
        for pair in range(pairs):
            left, right = boxes_of_pair(pair, pairs)
            first, second = box_of_row == left, box_of_row == right
            leaf_maps[pair, here, :LANES] = jnp.where(
                low, jnp.where(first, tiled, 0.0), jnp.where(second, far, 0.0)
            ).astype(B16)
            leaf_maps[pair, here, LANES:] = jnp.where(
                low, jnp.where(first, far, 0.0), jnp.where(second, tiled, 0.0)
            ).astype(B16)
            lanes = slice(pair % 2 * LANES, (pair % 2 + 1) * LANES)
            mine = (node_row % group == jnp.where(in_left, left, right)) & (
                lane_index(shape) // HALF == part
            )
            node_maps[pair // 2, here, lanes] = jnp.where(mine, nodes, 0.0).astype(B16)


def sine_cosine(turns):
    u = turns - jnp.round(turns)
    w = u * u
    sin_terms = [(-1) ** i * math.pi ** (2 * i + 1) / math.factorial(2 * i + 1) for i in range(7)]
    cos_terms = [(-1) ** i * math.pi ** (2 * i) / math.factorial(2 * i) for i in range(7)]
    half_sin = jnp.full_like(w, sin_terms[-1])
    for term in sin_terms[-2::-1]:
        half_sin = half_sin * w + term
    half_sin = half_sin * u
    half_cos = jnp.full_like(w, cos_terms[-1])
    for term in cos_terms[-2::-1]:
        half_cos = half_cos * w + term
    twice = half_sin + half_sin
    return twice * half_cos, 1.0 - twice * half_sin


def reversed_bits(number, bits):
    return sum((number >> bit & 1) << (bits - 1 - bit) for bit in range(bits))


def butterfly_kernel(
    plan, leaf, pairs, packed_ref, leaf_ref, nodes_ref, weights_ref, out_ref,
    leaf_maps, node_maps, weights, arrived, state_a, state_b, tables,
):
    rows = packed_ref.shape[0]
    levels = len(plan)
    states = (state_a, state_b)
    rotations = [sum(kind == "tiles" for kind, _ in plan[:level]) for level in range(levels)]
    row_tiles = rows // TILE
    row_bits, pair_bits = row_tiles.bit_length() - 1, pairs.bit_length() - 1
    half_tiles = state_a.shape[0] // 2
    units = min(UNITS, half_tiles)
    blocks = half_tiles // units
    index_bits = row_bits + pair_bits
    bounds = (0, 2 * levels, 2 * levels + pairs)
    fetches = [
        pltpu.make_async_copy(
            weights_ref.at[start:stop], weights.at[start:stop], arrived.at[number]
        )
        for number, (start, stop) in enumerate(zip(bounds, bounds[1:]))
    ]
    for fetch in fetches:
        fetch.start()
    first_maps(leaf, pairs, leaf_ref, nodes_ref, leaf_maps, node_maps)

    low = lax.broadcasted_iota(jnp.int16, (TILE, LANES), 1) < jnp.int16(HALF)
    lanes = lane_index((TILE // 2, LANES))
    upper_rows = lanes // HALF * QUARTER + lanes % QUARTER
    lower_rows = upper_rows + HALF

    def place_of(row_tile, pair):
        return reversed_bits(pair, pair_bits) << row_bits | reversed_bits(row_tile, row_bits)

    def merged(first, second):
        return jnp.concatenate(
            [
                jnp.where(low, first[:, :LANES], second[:, :LANES]),
                jnp.where(low, first[:, LANES:], second[:, LANES:]),
            ],
            axis=1,
        )

    def spread(table):
        return jnp.concatenate(
            [
                jnp.take_along_axis(table, upper_rows, axis=1),
                jnp.take_along_axis(table, lower_rows, axis=1),
            ],
            axis=0,
        )

    def moved(place, count):
        count = count % index_bits
        return (place << count | place >> (index_bits - count)) & (2 * half_tiles - 1)

    def turned(mixed, level, state, source, place):
        real, imag = mixed[:, :LANES], mixed[:, LANES:]
        cosine, sine = tables[level, source, :, :LANES], tables[level, source, :, LANES:]
        state[place, :, :LANES] = real * cosine - imag * sine
        state[place, :, LANES:] = real * sine + imag * cosine

    def run(*accumulators):
        few = min(TILE, row_tiles)

        rounds = row_tiles // few

        def strip_of(item, i):
            return pl.ds(pl.multiple_of((item % rounds * few + i) * TILE, TILE), TILE)

        def push_nodes(item):
            for order in range(2):
                pltpu.matmul_push_rhs(node_maps[item // rounds], 0, order)

        def send_speeds(item, i):
            speeds = [packed_ref[strip_of(item, i + side), 2 * LANES :] for side in range(2)]
            speeds = [part.astype(F32) for part in speeds]
            speeds = jnp.concatenate(
                [
                    jnp.concatenate([part[: TILE // 2] for part in speeds], axis=0),
                    jnp.concatenate([part[TILE // 2 :] for part in speeds], axis=0),
                ],
                axis=1,
            ).astype(B16)
            pltpu.matmul_acc_lhs(
                accumulators[2 * few + i // 2], speeds, load_staged_rhs=0 if i < 4 else None
            )

        items = pairs // 2 * rounds
        push_nodes(0)
        for i in range(0, few, 2):
            send_speeds(0, i)

        @pl.loop(0, items)
        def _(item):
            duo, start = item // rounds, item % rounds * few
            base = place_of(start, 2 * duo)
            coming = jnp.minimum(item + 1, items - 1)
            for order in range(2):
                pltpu.matmul_push_rhs(leaf_maps[2 * duo + order], 1, order)
            strips = [strip_of(item, i) for i in range(few)]
            for i, strip in enumerate(strips):
                for order in range(2):
                    pltpu.matmul_acc_lhs(
                        accumulators[2 * i + order],
                        packed_ref[strip, : 2 * LANES],
                        load_staged_rhs=1 if i == 0 else None,
                    )
            push_nodes(coming)
            for i in range(0, few, 2):
                turns = pltpu.matmul_pop(accumulators[2 * few + i // 2])
                send_speeds(coming, i)
                for order in range(2):
                    sine, cosine = sine_cosine(turns[:, order * LANES : (order + 1) * LANES])
                    for side in range(2):
                        place = base + place_of(i + side, order)
                        state_a[place] = pltpu.matmul_pop(
                            accumulators[2 * (i + side) + order]
                        ).astype(B16)
                        here = slice(side * TILE // 2, (side + 1) * TILE // 2)
                        cosines, sines = spread(cosine[here]), spread(sine[here])
                        twice = cosines + cosines
                        last_cosines, last_sines = 1.0, 0.0
                        for level in range(levels):
                            spot = moved(base, rotations[level]) + moved(
                                place_of(i + side, order), rotations[level]
                            )
                            tables[level, spot, :, :LANES] = cosines.astype(B16)
                            tables[level, spot, :, LANES:] = sines.astype(B16)
                            cosines, last_cosines = twice * cosines - last_cosines, cosines
                            sines, last_sines = twice * sines - last_sines, sines

        for i in range(0, few, 2):
            pltpu.matmul_pop(accumulators[2 * few + i // 2])

        def load_maps(level):
            for order in range(2):
                pltpu.matmul_push_rhs(weights[2 * level + order], 0, order)

        def send(state, block, unit, fresh):
            number = block * units + unit
            first, second = state[number], state[number + half_tiles]
            for order in range(2):
                pltpu.matmul_acc_lhs(
                    accumulators[2 * unit + order],
                    merged(second, first) if order else merged(first, second),
                    load_staged_rhs=0 if fresh and unit == 0 else None,
                )

        def received(unit):
            return [
                pltpu.matmul_pop(accumulators[2 * unit + order]).astype(B16) for order in range(2)
            ]

        def finish(level, target, block, unit):
            one, other = received(unit)
            number = block * units + unit
            turned(merged(one, other), level, target, number, 2 * number)
            turned(merged(other, one), level, target, number + half_tiles, 2 * number + 1)

        def across_tiles(level, source, target, next_level):
            @pl.loop(0, blocks - 1)
            def _(block):
                for unit in range(units):
                    finish(level, target, block, unit)
                    send(source, block + 1, unit, False)

            if next_level is not None:
                load_maps(next_level)
            for unit in range(units):
                finish(level, target, blocks - 1, unit)
                if next_level is not None:
                    send(target, 0, unit, True)

        def within_tiles(level, source, target, stride):
            upper = row_index((TILE, 2 * LANES)) // stride % 2 == 1
            mask = (lane_index((TILE, 2 * LANES)) % LANES < HALF) != upper

            def one_tile(place, fresh):
                own = source[place].astype(F32)
                other = jnp.where(
                    upper, pltpu.roll(own, stride, 0), pltpu.roll(own, TILE - stride, 0)
                )
                pre = []
                for order in range(2):
                    lhs = jnp.where(mask, other, own) if order else jnp.where(mask, own, other)
                    pltpu.matmul_acc_lhs(
                        accumulators[order], lhs.astype(B16), load_staged_rhs=0 if fresh else None
                    )
                    pre.append(pltpu.matmul_pop(accumulators[order]))
                turned(jnp.where(mask, *pre).astype(B16), level, target, place, place)

            one_tile(0, True)

            @pl.loop(1, 2 * half_tiles)
            def _(place):
                one_tile(place, False)

        fetches[0].wait()
        if levels % 2 == 0 and blocks > 3 and all(kind == "tiles" for kind, _ in plan):
            load_maps(0)
            for unit in range(units):
                send(state_a, 0, unit, True)

            @pl.loop(0, levels // 2)
            def _(two):
                across_tiles(2 * two, state_a, state_b, 2 * two + 1)
                across_tiles(2 * two + 1, state_b, state_a, jnp.minimum(2 * two + 2, levels - 1))

            for unit in range(units):
                received(unit)
        else:
            for level, (kind, stride) in enumerate(plan):
                source, target = states[level % 2], states[1 - level % 2]
                load_maps(level)
                if kind == "rows":
                    within_tiles(level, source, target, stride)
                    continue
                for unit in range(units):
                    send(source, 0, unit, True)
                across_tiles(level, source, target, None)

        fetches[1].wait()
        final = states[levels % 2]
        share = row_tiles // 2
        for pair in range(pairs):
            for order in range(2):
                pltpu.matmul_push_rhs(weights[2 * levels + pair], pair % 2, order)
            for i in range(share):
                for order in range(2):
                    pltpu.matmul_acc_lhs(
                        accumulators[2 * i + order],
                        final[place_of(order * share + i, pair)],
                        load_staged_rhs=pair % 2 if i == 0 else None,
                    )
        for i in range(share):
            for order in range(2):
                top = (order * share + i) * TILE
                out_ref[top : top + TILE, :] = pltpu.matmul_pop(
                    accumulators[2 * i + order]
                ).astype(B16)

    pl.run_scoped(
        run, *[pltpu.ACC(order)((TILE, 2 * LANES), F32) for _ in range(units) for order in range(2)]
    )


def split_nodes(rank):
    nodes = np.cos(np.pi * (np.arange(QUARTER) + 0.5) / rank) / 2
    pieces = []
    rest = np.tile(nodes, LANES // QUARTER)
    for _ in range(3):
        piece = rest.astype(B16)
        pieces.append(piece.astype(np.float32))
        rest = rest - piece.astype(np.float64)
    return np.stack(pieces)


def level_plan(levels, local_levels, rows_per):
    plan = [("tiles", level) for level in range(local_levels)]
    stride = rows_per
    for _ in range(levels - local_levels):
        if stride < TILE:
            plan.append(("rows", stride))
        else:
            plan.append(("tiles", local_levels + (stride // TILE).bit_length() - 1))
        stride *= 2
    return tuple(plan)


def on_device(charges, source_order, velocity, leaf_weight, mixing, eval_weight, target_order):
    leaf = leaf_weight.shape[0] // 2
    width = leaf_weight.shape[1]
    boxes = charges.shape[1] // leaf
    group = LANES // leaf
    pairs = group // 2
    rows = boxes // group
    devices = lax.axis_size("wide") * lax.axis_size("narrow")
    rows_per = rows // devices
    levels = mixing.shape[0]
    local_levels = levels - (devices.bit_length() - 1)
    assert width == LANES and 1 << local_levels == pairs

    charge_rows = charges.reshape(2, rows, LANES).transpose(1, 0, 2).reshape(2 * rows, LANES)
    in_hbm = pl.BlockSpec(memory_space=pltpu.HBM)
    packed = pl.pallas_call(
        functools.partial(pack_kernel, leaf),
        in_specs=[in_hbm] * 3,
        out_specs=in_hbm,
        out_shape=jax.ShapeDtypeStruct((rows, 3 * LANES), B16),
        scratch_shapes=[
            pltpu.VMEM((2 * rows, LANES), F32),
            pltpu.VMEM((rows, LANES), jnp.int32),
            pltpu.VMEM((boxes // LANES, LANES), B16),
            pltpu.VMEM((rows, 3 * LANES), B16),
            pltpu.SemaphoreType.DMA((STRIPS, 3)),
            pltpu.SemaphoreType.DMA((STRIPS,)),
        ],
        compiler_params=vmem(56),
        name="pack",
    )(charge_rows, source_order.reshape(rows, LANES), velocity.reshape(boxes // LANES, LANES))

    packed = lax.all_to_all(
        packed.reshape(devices, rows_per, 3 * LANES), AXES, 0, 0, tiled=True
    ).reshape(rows, 3 * LANES)

    square = (2 * LANES, 2 * LANES)
    count = 2 * levels + pairs
    weights = pl.pallas_call(
        functools.partial(maps_kernel, leaf),
        grid=(1,),
        out_specs=pl.BlockSpec((count, *square), lambda step: (0, 0, 0)),
        out_shape=jax.ShapeDtypeStruct((max(count, ROOM), *square), B16),
        compiler_params=vmem(56),
        cost_estimate=pl.CostEstimate(flops=10**9, bytes_accessed=10**7, transcendentals=0),
        name="maps",
    )(mixing, eval_weight)

    tiles = rows // TILE * pairs
    state = pltpu.VMEM((tiles, TILE, 2 * LANES), B16)
    values = pl.pallas_call(
        functools.partial(butterfly_kernel, level_plan(levels, local_levels, rows_per), leaf, pairs),
        out_shape=jax.ShapeDtypeStruct((rows, 2 * LANES), B16),
        in_specs=[pl.BlockSpec(memory_space=pltpu.VMEM)] * 3
        + [in_hbm],
        scratch_shapes=[
            pltpu.VMEM((pairs, *square), B16),
            pltpu.VMEM((pairs // 2, *square), B16),
            pltpu.VMEM((count, *square), B16),
            pltpu.SemaphoreType.DMA((2,)),
            state,
            state,
            pltpu.VMEM((levels, tiles, TILE, 2 * LANES), B16),
        ],
        compiler_params=vmem(40),
        name="butterfly",
    )(packed, leaf_weight, jnp.asarray(split_nodes(width // 2)), weights)

    values = lax.all_to_all(
        values.reshape(devices, rows_per, 2 * LANES), AXES, 0, 0, tiled=True
    ).reshape(rows, 2 * LANES)

    out = pl.pallas_call(
        functools.partial(unpack_kernel, leaf),
        out_specs=in_hbm,
        out_shape=jax.ShapeDtypeStruct((2 * rows, LANES), F32),
        scratch_shapes=[pltpu.VMEM((2 * rows, LANES), F32), pltpu.SemaphoreType.DMA((STRIPS,))],
        compiler_params=vmem(8),
        name="unpack",
    )(values, target_order.reshape(rows, LANES))
    return out.reshape(rows, 2, LANES).transpose(1, 0, 2).reshape(2, rows * LANES)


def solution(mesh):
    mapped = jax.shard_map(
        on_device,
        mesh=mesh,
        in_specs=(
            P(None, AXES),
            P(AXES),
            P(AXES),
            P(),
            P(),
            P(),
            P(AXES),
        ),
        out_specs=P(None, AXES),
        check_vma=False,
    )

    def program(*arrays):
        with jax.sharding.use_abstract_mesh(mesh.abstract_mesh):
            return mapped(*arrays)

    return program
```

```python
import functools
import math

import jax
import jax.numpy as jnp
import numpy as np
from jax import lax
from jax.experimental import pallas as pl
from jax.experimental.pallas import tpu as pltpu
from jax.sharding import PartitionSpec as P

LANES = 128
HALF = LANES // 2
QUARTER = LANES // 4
TILE = 16
AXES = ("wide", "narrow")
F32, B16 = jnp.float32, jnp.bfloat16
UNITS = 32
ROOM = 200
def vmem(mebibytes):
    return pltpu.CompilerParams(vmem_limit_bytes=mebibytes * 2**20)


STRIPS = 4


def lane_index(shape):
    return lax.broadcasted_iota(jnp.int32, shape, len(shape) - 1)


def row_index(shape):
    return lax.broadcasted_iota(jnp.int32, shape, len(shape) - 2)


def swapped(x):
    return pltpu.roll(x, HALF, 1)


def repeated(x, group):
    while group < LANES:
        x = x + pltpu.roll(x, group, 1)
        group *= 2
    return x


def odd_bits(number):
    for shift in (16, 8, 4, 2, 1):
        number = number ^ lax.shift_right_logical(number, shift)
    return number & 1


def device_number():
    return lax.axis_index("wide") * lax.axis_size("narrow") + lax.axis_index("narrow")


def pack_kernel(
    leaf, charges_hbm, order_hbm, velocity_hbm, out_hbm,
    charges_ref, order_ref, velocity_ref, out_ref, arrived, gone,
):
    slabs = len(out_ref.shape) == 3
    rows = order_ref.shape[0]
    strip = rows // STRIPS
    group = LANES // leaf
    pairs = ((charges_hbm, charges_ref), (order_hbm, order_ref), (velocity_hbm, velocity_ref))

    def part(ref, number):
        height = ref.shape[0] // STRIPS
        return ref.at[number * height : (number + 1) * height]

    fetches = [
        [
            pltpu.make_async_copy(part(far, number), part(near, number), arrived.at[number, kind])
            for kind, (far, near) in enumerate(pairs)
        ]
        for number in range(STRIPS)
    ]
    stores = [
        pltpu.make_async_copy(part(out_ref, number), part(out_hbm, number), gone.at[number])
        for number in range(STRIPS)
    ]
    for fetch in sum(fetches, []):
        fetch.start()
    odd = odd_bits(device_number()) == 1
    lanes = lane_index((strip, LANES))
    own = lanes // group == row_index((strip, LANES)) % leaf
    speed_lanes = lane_index((strip // leaf, LANES)) ^ jnp.where(odd, group // 2, 0)
    for number in range(STRIPS):
        for fetch in fetches[number]:
            fetch.wait()
        here = slice(number * strip, (number + 1) * strip)
        index = order_ref[here, :] + lanes // leaf * leaf
        for half in range(2):
            values = charges_ref[pl.ds(2 * number * strip + half, strip, stride=2), :]
            values = jnp.take_along_axis(values, index, axis=1)
            values = jnp.where(odd, swapped(values), values).astype(B16)
            if slabs:
                for slab in range(strip // TILE):
                    out_ref[number * (strip // TILE) + slab, half * TILE : (half + 1) * TILE, :] = (
                        values[slab * TILE : (slab + 1) * TILE]
                    )
            else:
                out_ref[here, half * LANES : (half + 1) * LANES] = values
        top = number * strip // leaf
        speeds = velocity_ref[top : top + strip // leaf, :].astype(F32)
        speeds = jnp.take_along_axis(speeds, speed_lanes, axis=1)
        if slabs:
            for slab in range(strip // TILE):
                first = slab * TILE // leaf
                own_rows = speeds[first // 8 * 8 : first // 8 * 8 + 8]
                if first % 8:
                    own_rows = pltpu.roll(own_rows, 8 - first % 8, 0)
                out_ref[number * (strip // TILE) + slab, 2 * TILE :, :] = jnp.where(
                    row_index((8, LANES)) < TILE // leaf, own_rows, 0.0
                ).astype(B16)
        else:
            speeds = jnp.broadcast_to(speeds[:, None, :], (strip // leaf, leaf, LANES))
            speeds = jnp.where(own, speeds.reshape(strip, LANES), 0.0)
            out_ref[here, 2 * LANES :] = repeated(speeds, group).astype(B16)
        stores[number].start()
    for store in stores:
        store.wait()


def unpack_kernel(leaf, values_ref, order_ref, out_hbm, out_ref, gone):
    rows = order_ref.shape[0]
    strip = rows // STRIPS
    odd = odd_bits(device_number()) == 1
    base = lane_index((strip, LANES)) // leaf * leaf ^ jnp.where(odd, HALF, 0)
    stores = []
    for number in range(STRIPS):
        here = slice(number * strip, (number + 1) * strip)
        index = order_ref[here, :] + base
        for half in range(2):
            values = values_ref[here, half * LANES : (half + 1) * LANES].astype(F32)
            out_ref[pl.ds(2 * number * strip + half, strip, stride=2), :] = jnp.take_along_axis(
                values, index, axis=1
            )
        wide = slice(2 * number * strip, 2 * (number + 1) * strip)
        stores.append(pltpu.make_async_copy(out_ref.at[wide], out_hbm.at[wide], gone.at[number]))
        stores[-1].start()
    for store in stores:
        store.wait()


def odd_pair(pair):
    return bin(pair).count("1") % 2 == 1


def mirrored(index):
    place = index % HALF
    return index - place + jnp.where(place < QUARTER, place, HALF + QUARTER - 1 - place)


def sign_of(index):
    return jnp.where((index >= HALF) & (index % HALF >= QUARTER), -1.0, 1.0)


def boxes_of_pair(pair, pairs):
    return (pair + pairs, pair) if odd_pair(pair) else (pair, pair + pairs)


def maps_kernel(leaf, mixing_ref, eval_ref, weights):
    levels = mixing_ref.shape[0]
    pairs = LANES // leaf // 2
    low = lane_index((HALF, LANES)) < HALF
    shape = (LANES, LANES)
    mirror = jnp.where(
        row_index(shape) == mirrored(lane_index(shape)), sign_of(lane_index(shape)), 0.0
    ).astype(B16)
    mirror_back = jnp.where(
        lane_index(shape) == mirrored(row_index(shape)), sign_of(row_index(shape)), 0.0
    ).astype(B16)

    order_of_four = [(target, source) for target in range(2) for source in range(2)]

    @pl.loop(0, levels)
    def _(level):
        four = jnp.concatenate([mixing_ref[level, *place] for place in order_of_four], axis=0)
        four = jnp.dot(four, mirror, preferred_element_type=F32).astype(B16)
        four = jnp.concatenate(
            [four[number * LANES : (number + 1) * LANES] for number in range(4)], axis=1
        )
        four = jnp.dot(mirror_back, four, preferred_element_type=F32)
        for source in range(2):
            both = [
                four[:, (2 * target + source) * LANES : (2 * target + source + 1) * LANES]
                for target in range(2)
            ]
            for part in range(2):
                to_first, to_second = (
                    matrix[part * HALF : (part + 1) * HALF] for matrix in both
                )
                first_far, second_far = swapped(to_first), swapped(to_second)
                for order in range(2):
                    top = part * LANES + (source ^ order) * HALF
                    place = weights.at[2 * level + order, top : top + HALF]
                    if order == 0:
                        real = jnp.where(low, to_first, second_far)
                        imag = jnp.where(low, first_far, to_second)
                    else:
                        real = jnp.where(low, to_second, first_far)
                        imag = jnp.where(low, second_far, to_first)
                    place[:, :LANES] = real.astype(B16)
                    place[:, LANES:] = imag.astype(B16)

    box_of_lane = lane_index((HALF, LANES)) // leaf
    slot = lane_index((2 * leaf, 2 * LANES))
    spread = (slot // LANES * leaf + slot % leaf == row_index((2 * leaf, 2 * LANES))).astype(B16)
    eval_rows = lax.dot_general(
        eval_ref[...], spread, (((0,), (0,)), ((), ())), preferred_element_type=F32
    ).astype(B16)
    eval_rows = jnp.dot(mirror_back, eval_rows, preferred_element_type=F32)
    for pair in range(pairs):
        for number, box in enumerate(boxes_of_pair(pair, pairs)):
            for part in range(2):
                top = (2 * part + number) * HALF
                for side in range(2):
                    lanes = slice(side * LANES, (side + 1) * LANES)
                    block = eval_rows[part * HALF : (part + 1) * HALF, lanes]
                    weights[2 * levels + pair, top : top + HALF, lanes] = jnp.where(
                        box_of_lane == box, block, 0.0
                    ).astype(B16)


def first_maps(leaf, pairs, leaf_ref, nodes_ref, leaf_maps, node_maps):
    group = 2 * pairs
    leaf_rows = leaf_ref[...].astype(F32)
    lanes = lane_index(leaf_rows.shape)
    leaf_rows = jnp.take_along_axis(leaf_rows, mirrored(lanes), axis=1) * sign_of(lanes)
    shape = (LANES, LANES)
    in_left = lane_index(shape) % HALF < QUARTER
    low = lane_index(shape) < HALF
    box_of_row = row_index(shape) // leaf
    node_row = row_index(shape)
    nodes = jnp.zeros(shape, F32)
    for piece in range(3):
        nodes = jnp.where(node_row // group == piece, nodes_ref[piece : piece + 1, :], nodes)
    tiles = [
        jnp.broadcast_to(
            leaf_rows[part * leaf : (part + 1) * leaf][None], (group, leaf, LANES)
        ).reshape(shape)
        for part in range(2)
    ]

    @pl.loop(0, pairs)
    def _(pair):
        odd = odd_bits(pair) == 1
        left = pair + jnp.where(odd, pairs, 0)
        right = pair + jnp.where(odd, 0, pairs)
        mine = node_row % group == jnp.where(in_left, left, right)
        for part in range(2):
            tiled = tiles[part]
            far = swapped(tiled)
            here = slice(part * LANES, (part + 1) * LANES)
            first, second = box_of_row == left, box_of_row == right
            leaf_maps[pair, here, :LANES] = jnp.where(
                low, jnp.where(first, tiled, 0.0), jnp.where(second, far, 0.0)
            ).astype(B16)
            leaf_maps[pair, here, LANES:] = jnp.where(
                low, jnp.where(first, far, 0.0), jnp.where(second, tiled, 0.0)
            ).astype(B16)
            node_maps[pair, here, :] = jnp.where(
                mine & (lane_index(shape) // HALF == part), nodes, 0.0
            ).astype(B16)


def sine_cosine(turns):
    u = turns - jnp.round(turns)
    w = u * u
    sin_terms = [(-1) ** i * math.pi ** (2 * i + 1) / math.factorial(2 * i + 1) for i in range(6)]
    cos_terms = [(-1) ** i * math.pi ** (2 * i) / math.factorial(2 * i) for i in range(6)]
    half_sin = jnp.full_like(w, sin_terms[-1])
    for term in sin_terms[-2::-1]:
        half_sin = half_sin * w + term
    half_sin = half_sin * u
    half_cos = jnp.full_like(w, cos_terms[-1])
    for term in cos_terms[-2::-1]:
        half_cos = half_cos * w + term
    twice = half_sin + half_sin
    return twice * half_cos, 1.0 - twice * half_sin


def reversed_bits(number, bits):
    return sum((number >> bit & 1) << (bits - 1 - bit) for bit in range(bits))


def butterfly_kernel(
    plan, leaf, pairs, packed_ref, leaf_ref, nodes_ref, weights_ref, out_ref,
    leaf_maps, node_maps, weights, arrived, states_ref, tables, speeds_ref,
):
    slabs = len(packed_ref.shape) == 3
    rows = packed_ref.shape[0] * (TILE if slabs else 1)
    levels = len(plan)
    states = pltpu.annotate(states_ref, no_hazard_no_deps=True)
    rotations = [sum(kind == "tiles" for kind, _ in plan[:level]) for level in range(levels)]
    row_tiles = rows // TILE
    row_bits, pair_bits = row_tiles.bit_length() - 1, pairs.bit_length() - 1
    half_tiles = states_ref.shape[1] // 2
    units = min(UNITS, half_tiles)
    blocks = half_tiles // units
    index_bits = row_bits + pair_bits
    bounds = (0, 2 * levels, 2 * levels + pairs)
    fetches = [
        pltpu.make_async_copy(
            weights_ref.at[start:stop], weights.at[start:stop], arrived.at[number]
        )
        for number, (start, stop) in enumerate(zip(bounds, bounds[1:]))
    ]
    for fetch in fetches:
        fetch.start()
    first_maps(leaf, pairs, leaf_ref, nodes_ref, leaf_maps, node_maps)

    low = lax.broadcasted_iota(jnp.int16, (TILE, LANES), 1) < jnp.int16(HALF)
    lanes = lane_index((TILE // 2, LANES))
    upper_rows = lanes // HALF * QUARTER + lanes % QUARTER
    lower_rows = upper_rows + HALF

    def place_of(row_tile, pair):
        return reversed_bits(pair, pair_bits) << row_bits | reversed_bits(row_tile, row_bits)

    def merged(first, second):
        return jnp.concatenate(
            [
                jnp.where(low, first[:, :LANES], second[:, :LANES]),
                jnp.where(low, first[:, LANES:], second[:, LANES:]),
            ],
            axis=1,
        )

    def spread(table):
        return jnp.concatenate(
            [
                jnp.take_along_axis(table, upper_rows, axis=1),
                jnp.take_along_axis(table, lower_rows, axis=1),
            ],
            axis=0,
        )

    def moved(place, count):
        count = count % index_bits
        return (place << count | place >> (index_bits - count)) & (2 * half_tiles - 1)

    def turned(mixed, level, source, place):
        real, imag = mixed[:, :LANES], mixed[:, LANES:]
        cosine, sine = tables[level, source, :, :LANES], tables[level, source, :, LANES:]
        after = 1 - level % 2
        states[after, place, :, :LANES] = real * cosine - imag * sine
        states[after, place, :, LANES:] = real * sine + imag * cosine

    def run(*accumulators):
        few = min(TILE, row_tiles)

        rounds = row_tiles // few

        def charges_of(row_tile):
            if slabs:
                halves = [packed_ref[row_tile, half * TILE : (half + 1) * TILE] for half in range(2)]
                return jnp.concatenate(halves, axis=1)
            return packed_ref[pl.ds(pl.multiple_of(row_tile * TILE, TILE), TILE), : 2 * LANES]

        def speeds_of(row_tile):
            if slabs:
                raw = packed_ref[row_tile, 2 * TILE :].astype(F32)
                group = 2 * pairs
                own = lanes // group == row_index(lanes.shape)
                return [
                    repeated(jnp.where(own, raw[half : half + 1], 0.0), group) for half in range(2)
                ]
            speeds = packed_ref[row_tile * TILE : (row_tile + 1) * TILE, 2 * LANES :].astype(F32)
            return [speeds[: TILE // 2], speeds[TILE // 2 :]]

        for i in range(0, row_tiles, 2):
            both = [speeds_of(i), speeds_of(i + 1)]
            speeds_ref[i // 2] = jnp.concatenate(
                [jnp.concatenate([both[0][half], both[1][half]], axis=0) for half in range(2)],
                axis=1,
            ).astype(B16)

        def push_nodes(item):
            for order in range(2):
                both = [node_maps[item // rounds * 2 + side] for side in range(2)]
                pltpu.matmul_push_rhs(jnp.concatenate(both, axis=1), 0, order)

        def send_speeds(item, i):
            pltpu.matmul_acc_lhs(
                accumulators[2 * few + i // 2],
                speeds_ref[(item % rounds * few + i) // 2],
                load_staged_rhs=0 if i < 4 else None,
            )

        items = pairs // 2 * rounds
        push_nodes(0)
        for i in range(0, few, 2):
            send_speeds(0, i)

        @pl.loop(0, items)
        def _(item):
            duo, start = item // rounds, item % rounds * few
            base = place_of(start, 2 * duo)
            coming = jnp.minimum(item + 1, items - 1)
            for order in range(2):
                pltpu.matmul_push_rhs(leaf_maps[2 * duo + order], 1, order)
            for i in range(few):
                charges = charges_of(start + i)
                for order in range(2):
                    pltpu.matmul_acc_lhs(
                        accumulators[2 * i + order],
                        charges,
                        load_staged_rhs=1 if i == 0 else None,
                    )
            push_nodes(coming)
            for i in range(0, few, 2):
                turns = pltpu.matmul_pop(accumulators[2 * few + i // 2])
                send_speeds(coming, i)
                for order in range(2):
                    sine, cosine = sine_cosine(turns[:, order * LANES : (order + 1) * LANES])
                    for side in range(2):
                        place = base + place_of(i + side, order)
                        states_ref[0, place] = pltpu.matmul_pop(
                            accumulators[2 * (i + side) + order]
                        ).astype(B16)
                        here = slice(side * TILE // 2, (side + 1) * TILE // 2)
                        cosines, sines = spread(cosine[here]), spread(sine[here])
                        twice = cosines + cosines
                        last_cosines, last_sines = 1.0, 0.0
                        for level in range(levels):
                            spot = moved(base, rotations[level]) + moved(
                                place_of(i + side, order), rotations[level]
                            )
                            tables[level, spot, :, :LANES] = cosines.astype(B16)
                            tables[level, spot, :, LANES:] = sines.astype(B16)
                            cosines, last_cosines = twice * cosines - last_cosines, cosines
                            sines, last_sines = twice * sines - last_sines, sines

        for i in range(0, few, 2):
            pltpu.matmul_pop(accumulators[2 * few + i // 2])

        def load_maps(level):
            for order in range(2):
                pltpu.matmul_push_rhs(weights[2 * level + order], 0, order)

        def send(level, block, unit, fresh):
            number = block * units + unit
            first = states[level % 2, number]
            second = states[level % 2, number + half_tiles]
            for order in range(2):
                pltpu.matmul_acc_lhs(
                    accumulators[2 * unit + order],
                    merged(second, first) if order else merged(first, second),
                    load_staged_rhs=0 if fresh and unit == 0 else None,
                )

        def received(unit):
            return [
                pltpu.matmul_pop(accumulators[2 * unit + order]).astype(B16) for order in range(2)
            ]

        def finish(level, block, unit):
            one, other = received(unit)
            number = block * units + unit
            turned(merged(one, other), level, number, 2 * number)
            turned(merged(other, one), level, number + half_tiles, 2 * number + 1)

        def across_tiles(first_level, count):
            load_maps(first_level)
            for unit in range(units):
                send(first_level, 0, unit, True)

            @pl.loop(first_level, first_level + count)
            def _(level):
                @pl.loop(0, blocks - 1)
                def _(block):
                    for unit in range(units):
                        finish(level, block, unit)
                        send(level, block + 1, unit, False)

                next_level = jnp.minimum(level + 1, levels - 1)
                load_maps(next_level)
                for unit in range(units):
                    finish(level, blocks - 1, unit)
                    send(next_level, 0, unit, True)

            for unit in range(units):
                received(unit)

        def within_tiles(level, stride):
            upper = row_index((TILE, 2 * LANES)) // stride % 2 == 1
            mask = (lane_index((TILE, 2 * LANES)) % LANES < HALF) != upper

            def one_tile(place, fresh):
                own = states_ref[level % 2, place].astype(F32)
                other = jnp.where(
                    upper, pltpu.roll(own, stride, 0), pltpu.roll(own, TILE - stride, 0)
                )
                pre = []
                for order in range(2):
                    lhs = jnp.where(mask, other, own) if order else jnp.where(mask, own, other)
                    pltpu.matmul_acc_lhs(
                        accumulators[order], lhs.astype(B16), load_staged_rhs=0 if fresh else None
                    )
                    pre.append(pltpu.matmul_pop(accumulators[order]))
                turned(jnp.where(mask, *pre).astype(B16), level, place, place)

            one_tile(0, True)

            @pl.loop(1, 2 * half_tiles)
            def _(place):
                one_tile(place, False)

        fetches[0].wait()
        level = 0
        while level < levels:
            kind, stride = plan[level]
            if kind == "rows":
                load_maps(level)
                within_tiles(level, stride)
                level += 1
                continue
            count = 1
            while blocks > 3 and level + count < levels and plan[level + count][0] == kind:
                count += 1
            across_tiles(level, count)
            level += count

        fetches[1].wait()
        final = states_ref.at[levels % 2]
        share = row_tiles // 2
        @pl.loop(0, pairs)
        def _(pair):
            base = place_of(0, pair)
            for order in range(2):
                pltpu.matmul_push_rhs(weights[2 * levels + pair], 0, order)
            for i in range(share):
                for order in range(2):
                    pltpu.matmul_acc_lhs(
                        accumulators[2 * i + order],
                        final[base + place_of(order * share + i, 0)],
                        load_staged_rhs=0 if i == 0 else None,
                    )

        for i in range(share):
            for order in range(2):
                top = (order * share + i) * TILE
                out_ref[top : top + TILE, :] = pltpu.matmul_pop(
                    accumulators[2 * i + order]
                ).astype(B16)

    pl.run_scoped(
        run, *[pltpu.ACC(order)((TILE, 2 * LANES), F32) for _ in range(units) for order in range(2)]
    )


def split_nodes(rank):
    nodes = np.cos(np.pi * (np.arange(QUARTER) + 0.5) / rank) / 2
    pieces = []
    rest = np.tile(nodes, LANES // QUARTER)
    for _ in range(3):
        piece = rest.astype(B16)
        pieces.append(piece.astype(np.float32))
        rest = rest - piece.astype(np.float64)
    return np.stack(pieces)


def level_plan(levels, local_levels, rows_per):
    plan = [("tiles", level) for level in range(local_levels)]
    stride = rows_per
    for _ in range(levels - local_levels):
        if stride < TILE:
            plan.append(("rows", stride))
        else:
            plan.append(("tiles", local_levels + (stride // TILE).bit_length() - 1))
        stride *= 2
    return tuple(plan)


def on_device(charges, source_order, velocity, leaf_weight, mixing, eval_weight, target_order):
    leaf = leaf_weight.shape[0] // 2
    width = leaf_weight.shape[1]
    boxes = charges.shape[1] // leaf
    group = LANES // leaf
    pairs = group // 2
    rows = boxes // group
    devices = lax.axis_size("wide") * lax.axis_size("narrow")
    rows_per = rows // devices
    levels = mixing.shape[0]
    local_levels = levels - (devices.bit_length() - 1)
    assert width == LANES and 1 << local_levels == pairs

    charge_rows = charges.reshape(2, rows, LANES).transpose(1, 0, 2).reshape(2 * rows, LANES)
    in_hbm = pl.BlockSpec(memory_space=pltpu.HBM)
    if rows_per == TILE:
        packed_shape = (devices, 2 * TILE + 8, LANES)
    else:
        packed_shape = (rows, 3 * LANES)
    packed = pl.pallas_call(
        functools.partial(pack_kernel, leaf),
        in_specs=[in_hbm] * 3,
        out_specs=in_hbm,
        out_shape=jax.ShapeDtypeStruct(packed_shape, B16),
        scratch_shapes=[
            pltpu.VMEM((2 * rows, LANES), F32),
            pltpu.VMEM((rows, LANES), jnp.int32),
            pltpu.VMEM((boxes // LANES, LANES), B16),
            pltpu.VMEM(packed_shape, B16),
            pltpu.SemaphoreType.DMA((STRIPS, 3)),
            pltpu.SemaphoreType.DMA((STRIPS,)),
        ],
        compiler_params=vmem(56),
        name="pack",
    )(charge_rows, source_order.reshape(rows, LANES), velocity.reshape(boxes // LANES, LANES))

    packed = lax.all_to_all(
        packed.reshape(devices, -1, packed_shape[-1]), AXES, 0, 0, tiled=True
    ).reshape(packed_shape)

    square = (2 * LANES, 2 * LANES)
    count = 2 * levels + pairs
    weights = pl.pallas_call(
        functools.partial(maps_kernel, leaf),
        grid=(1,),
        out_specs=pl.BlockSpec((count, *square), lambda step: (0, 0, 0)),
        out_shape=jax.ShapeDtypeStruct((max(count, ROOM), *square), B16),
        compiler_params=vmem(56),
        cost_estimate=pl.CostEstimate(flops=10**9, bytes_accessed=10**7, transcendentals=0),
        name="maps",
    )(mixing, eval_weight.T)

    tiles = rows // TILE * pairs
    values = pl.pallas_call(
        functools.partial(butterfly_kernel, level_plan(levels, local_levels, rows_per), leaf, pairs),
        out_shape=jax.ShapeDtypeStruct((rows, 2 * LANES), B16),
        in_specs=[pl.BlockSpec(memory_space=pltpu.VMEM)] * 3
        + [in_hbm],
        scratch_shapes=[
            pltpu.VMEM((pairs, *square), B16),
            pltpu.VMEM((pairs, 2 * LANES, LANES), B16),
            pltpu.VMEM((count, *square), B16),
            pltpu.SemaphoreType.DMA((2,)),
            pltpu.VMEM((2, tiles, TILE, 2 * LANES), B16),
            pltpu.VMEM((levels, tiles, TILE, 2 * LANES), B16),
            pltpu.VMEM((rows // TILE // 2, TILE, 2 * LANES), B16),
        ],
        compiler_params=vmem(40),
        name="butterfly",
    )(packed, leaf_weight, jnp.asarray(split_nodes(width // 2)), weights)

    values = lax.all_to_all(
        values.reshape(devices, rows_per, 2 * LANES), AXES, 0, 0, tiled=True
    ).reshape(rows, 2 * LANES)

    out = pl.pallas_call(
        functools.partial(unpack_kernel, leaf),
        out_specs=in_hbm,
        out_shape=jax.ShapeDtypeStruct((2 * rows, LANES), F32),
        scratch_shapes=[pltpu.VMEM((2 * rows, LANES), F32), pltpu.SemaphoreType.DMA((STRIPS,))],
        compiler_params=vmem(8),
        name="unpack",
    )(values, target_order.reshape(rows, LANES))
    return out.reshape(rows, 2, LANES).transpose(1, 0, 2).reshape(2, rows * LANES)


def solution(mesh):
    mapped = jax.shard_map(
        on_device,
        mesh=mesh,
        in_specs=(
            P(None, AXES),
            P(AXES),
            P(AXES),
            P(),
            P(),
            P(),
            P(AXES),
        ),
        out_specs=P(None, AXES),
        check_vma=False,
    )

    def program(*arrays):
        with jax.sharding.use_abstract_mesh(mesh.abstract_mesh):
            return mapped(*arrays)

    return program
```

```python
import functools
import math

import jax
import jax.numpy as jnp
import numpy as np
from jax import lax
from jax.experimental import pallas as pl
from jax.experimental.pallas import tpu as pltpu
from jax.sharding import PartitionSpec as P

LANES = 128
HALF = LANES // 2
QUARTER = LANES // 4
TILE = 16
AXES = ("wide", "narrow")
F32, B16 = jnp.float32, jnp.bfloat16
UNITS = 32
ROOM = 200
def vmem(mebibytes):
    return pltpu.CompilerParams(vmem_limit_bytes=mebibytes * 2**20)


STRIPS = 4


def lane_index(shape):
    return lax.broadcasted_iota(jnp.int32, shape, len(shape) - 1)


def row_index(shape):
    return lax.broadcasted_iota(jnp.int32, shape, len(shape) - 2)


def swapped(x):
    return pltpu.roll(x, HALF, 1)


def repeated(x, group):
    while group < LANES:
        x = x + pltpu.roll(x, group, 1)
        group *= 2
    return x


def odd_bits(number):
    for shift in (16, 8, 4, 2, 1):
        number = number ^ lax.shift_right_logical(number, shift)
    return number & 1


def device_number():
    return lax.axis_index("wide") * lax.axis_size("narrow") + lax.axis_index("narrow")


def pack_kernel(
    leaf, charges_hbm, order_hbm, velocity_hbm, out_hbm,
    charges_ref, order_ref, velocity_ref, out_ref, arrived, gone,
):
    slabs = len(out_ref.shape) == 3
    rows = order_ref.shape[0]
    strip = rows // STRIPS
    group = LANES // leaf
    pairs = ((charges_hbm, charges_ref), (order_hbm, order_ref), (velocity_hbm, velocity_ref))

    def part(ref, number):
        height = ref.shape[0] // STRIPS
        return ref.at[number * height : (number + 1) * height]

    fetches = [
        [
            pltpu.make_async_copy(part(far, number), part(near, number), arrived.at[number, kind])
            for kind, (far, near) in enumerate(pairs)
        ]
        for number in range(STRIPS)
    ]
    stores = [
        pltpu.make_async_copy(part(out_ref, number), part(out_hbm, number), gone.at[number])
        for number in range(STRIPS)
    ]
    for fetch in sum(fetches, []):
        fetch.start()
    odd = odd_bits(device_number()) == 1
    lanes = lane_index((strip, LANES))
    own = lanes // group == row_index((strip, LANES)) % leaf
    speed_lanes = lane_index((strip // leaf, LANES)) ^ jnp.where(odd, group // 2, 0)
    for number in range(STRIPS):
        for fetch in fetches[number]:
            fetch.wait()
        here = slice(number * strip, (number + 1) * strip)
        index = order_ref[here, :] + lanes // leaf * leaf
        for half in range(2):
            values = charges_ref[pl.ds(2 * number * strip + half, strip, stride=2), :]
            values = jnp.take_along_axis(values, index, axis=1)
            values = jnp.where(odd, swapped(values), values).astype(B16)
            if slabs:
                for slab in range(strip // TILE):
                    out_ref[number * (strip // TILE) + slab, half * TILE : (half + 1) * TILE, :] = (
                        values[slab * TILE : (slab + 1) * TILE]
                    )
            else:
                out_ref[here, half * LANES : (half + 1) * LANES] = values
        top = number * strip // leaf
        speeds = velocity_ref[top : top + strip // leaf, :].astype(F32)
        speeds = jnp.take_along_axis(speeds, speed_lanes, axis=1)
        if slabs:
            for slab in range(strip // TILE):
                first = slab * TILE // leaf
                own_rows = speeds[first // 8 * 8 : first // 8 * 8 + 8]
                if first % 8:
                    own_rows = pltpu.roll(own_rows, 8 - first % 8, 0)
                out_ref[number * (strip // TILE) + slab, 2 * TILE :, :] = jnp.where(
                    row_index((8, LANES)) < TILE // leaf, own_rows, 0.0
                ).astype(B16)
        else:
            speeds = jnp.broadcast_to(speeds[:, None, :], (strip // leaf, leaf, LANES))
            speeds = jnp.where(own, speeds.reshape(strip, LANES), 0.0)
            out_ref[here, 2 * LANES :] = repeated(speeds, group).astype(B16)
        stores[number].start()
    for store in stores:
        store.wait()


def unpack_kernel(leaf, values_ref, order_ref, out_hbm, out_ref, gone):
    rows = order_ref.shape[0]
    strip = rows // STRIPS
    odd = odd_bits(device_number()) == 1
    base = lane_index((strip, LANES)) // leaf * leaf ^ jnp.where(odd, HALF, 0)
    stores = []
    for number in range(STRIPS):
        here = slice(number * strip, (number + 1) * strip)
        index = order_ref[here, :] + base
        for half in range(2):
            values = values_ref[here, half * LANES : (half + 1) * LANES].astype(F32)
            out_ref[pl.ds(2 * number * strip + half, strip, stride=2), :] = jnp.take_along_axis(
                values, index, axis=1
            )
        wide = slice(2 * number * strip, 2 * (number + 1) * strip)
        stores.append(pltpu.make_async_copy(out_ref.at[wide], out_hbm.at[wide], gone.at[number]))
        stores[-1].start()
    for store in stores:
        store.wait()


def odd_pair(pair):
    return bin(pair).count("1") % 2 == 1


def mirrored(index):
    place = index % HALF
    return index - place + jnp.where(place < QUARTER, place, HALF + QUARTER - 1 - place)


def sign_of(index):
    return jnp.where((index >= HALF) & (index % HALF >= QUARTER), -1.0, 1.0)


def boxes_of_pair(pair, pairs):
    return (pair + pairs, pair) if odd_pair(pair) else (pair, pair + pairs)


def maps_kernel(leaf, mixing_ref, eval_ref, weights):
    levels = mixing_ref.shape[0]
    pairs = LANES // leaf // 2
    low = lane_index((HALF, LANES)) < HALF
    shape = (LANES, LANES)
    mirror = jnp.where(
        row_index(shape) == mirrored(lane_index(shape)), sign_of(lane_index(shape)), 0.0
    ).astype(B16)
    mirror_back = jnp.where(
        lane_index(shape) == mirrored(row_index(shape)), sign_of(row_index(shape)), 0.0
    ).astype(B16)

    order_of_four = [(target, source) for target in range(2) for source in range(2)]

    @pl.loop(0, levels)
    def _(level):
        four = jnp.concatenate([mixing_ref[level, *place] for place in order_of_four], axis=0)
        four = jnp.dot(four, mirror, preferred_element_type=F32).astype(B16)
        four = jnp.concatenate(
            [four[number * LANES : (number + 1) * LANES] for number in range(4)], axis=1
        )
        four = jnp.dot(mirror_back, four, preferred_element_type=F32)
        for source in range(2):
            both = [
                four[:, (2 * target + source) * LANES : (2 * target + source + 1) * LANES]
                for target in range(2)
            ]
            for part in range(2):
                to_first, to_second = (
                    matrix[part * HALF : (part + 1) * HALF] for matrix in both
                )
                first_far, second_far = swapped(to_first), swapped(to_second)
                for order in range(2):
                    top = part * LANES + (source ^ order) * HALF
                    place = weights.at[2 * level + order, top : top + HALF]
                    if order == 0:
                        real = jnp.where(low, to_first, second_far)
                        imag = jnp.where(low, first_far, to_second)
                    else:
                        real = jnp.where(low, to_second, first_far)
                        imag = jnp.where(low, second_far, to_first)
                    place[:, :LANES] = real.astype(B16)
                    place[:, LANES:] = imag.astype(B16)

    box_of_lane = lane_index((HALF, LANES)) // leaf
    slot = lane_index((2 * leaf, 2 * LANES))
    spread = (slot // LANES * leaf + slot % leaf == row_index((2 * leaf, 2 * LANES))).astype(B16)
    eval_rows = lax.dot_general(
        eval_ref[...], spread, (((0,), (0,)), ((), ())), preferred_element_type=F32
    ).astype(B16)
    eval_rows = jnp.dot(mirror_back, eval_rows, preferred_element_type=F32)
    for pair in range(pairs):
        for number, box in enumerate(boxes_of_pair(pair, pairs)):
            for part in range(2):
                top = (2 * part + number) * HALF
                for side in range(2):
                    lanes = slice(side * LANES, (side + 1) * LANES)
                    block = eval_rows[part * HALF : (part + 1) * HALF, lanes]
                    weights[2 * levels + pair, top : top + HALF, lanes] = jnp.where(
                        box_of_lane == box, block, 0.0
                    ).astype(B16)


def first_maps(leaf, pairs, leaf_ref, nodes_ref, leaf_maps, node_maps):
    group = 2 * pairs
    leaf_rows = leaf_ref[...].astype(F32)
    lanes = lane_index(leaf_rows.shape)
    leaf_rows = jnp.take_along_axis(leaf_rows, mirrored(lanes), axis=1) * sign_of(lanes)
    shape = (LANES, LANES)
    in_left = lane_index(shape) % HALF < QUARTER
    low = lane_index(shape) < HALF
    box_of_row = row_index(shape) // leaf
    node_row = row_index(shape)
    nodes = jnp.zeros(shape, F32)
    for piece in range(3):
        nodes = jnp.where(node_row // group == piece, nodes_ref[piece : piece + 1, :], nodes)
    tiles = [
        jnp.broadcast_to(
            leaf_rows[part * leaf : (part + 1) * leaf][None], (group, leaf, LANES)
        ).reshape(shape)
        for part in range(2)
    ]

    @pl.loop(0, pairs)
    def _(pair):
        odd = odd_bits(pair) == 1
        left = pair + jnp.where(odd, pairs, 0)
        right = pair + jnp.where(odd, 0, pairs)
        mine = node_row % group == jnp.where(in_left, left, right)
        for part in range(2):
            tiled = tiles[part]
            far = swapped(tiled)
            here = slice(part * LANES, (part + 1) * LANES)
            first, second = box_of_row == left, box_of_row == right
            leaf_maps[pair, here, :LANES] = jnp.where(
                low, jnp.where(first, tiled, 0.0), jnp.where(second, far, 0.0)
            ).astype(B16)
            leaf_maps[pair, here, LANES:] = jnp.where(
                low, jnp.where(first, far, 0.0), jnp.where(second, tiled, 0.0)
            ).astype(B16)
            node_maps[pair, here, :] = jnp.where(
                mine & (lane_index(shape) // HALF == part), nodes, 0.0
            ).astype(B16)


def sine_cosine(turns):
    u = turns - jnp.round(turns)
    w = u * u
    sin_terms = [(-1) ** i * math.pi ** (2 * i + 1) / math.factorial(2 * i + 1) for i in range(6)]
    cos_terms = [(-1) ** i * math.pi ** (2 * i) / math.factorial(2 * i) for i in range(6)]
    half_sin = jnp.full_like(w, sin_terms[-1])
    for term in sin_terms[-2::-1]:
        half_sin = half_sin * w + term
    half_sin = half_sin * u
    half_cos = jnp.full_like(w, cos_terms[-1])
    for term in cos_terms[-2::-1]:
        half_cos = half_cos * w + term
    twice = half_sin + half_sin
    return twice * half_cos, 1.0 - twice * half_sin


def reversed_bits(number, bits):
    return sum((number >> bit & 1) << (bits - 1 - bit) for bit in range(bits))


def butterfly_kernel(
    plan, leaf, pairs, packed_ref, leaf_ref, nodes_ref, weights_ref, out_ref,
    leaf_maps, node_maps, weights, arrived, states_ref, tables, speeds_ref,
):
    slabs = len(packed_ref.shape) == 3
    rows = packed_ref.shape[0] * (TILE if slabs else 1)
    levels = len(plan)
    states = pltpu.annotate(states_ref, no_hazard_no_deps=True)
    rotations = [sum(kind == "tiles" for kind, _ in plan[:level]) for level in range(levels)]
    row_tiles = rows // TILE
    row_bits, pair_bits = row_tiles.bit_length() - 1, pairs.bit_length() - 1
    half_tiles = states_ref.shape[1] // 2
    units = min(UNITS, half_tiles)
    blocks = half_tiles // units
    index_bits = row_bits + pair_bits
    bounds = (0, 2 * levels, 2 * levels + pairs)
    fetches = [
        pltpu.make_async_copy(
            weights_ref.at[start:stop], weights.at[start:stop], arrived.at[number]
        )
        for number, (start, stop) in enumerate(zip(bounds, bounds[1:]))
    ]
    for fetch in fetches:
        fetch.start()
    first_maps(leaf, pairs, leaf_ref, nodes_ref, leaf_maps, node_maps)

    low = lax.broadcasted_iota(jnp.int16, (TILE, LANES), 1) < jnp.int16(HALF)
    lanes = lane_index((TILE // 2, LANES))
    upper_rows = lanes // HALF * QUARTER + lanes % QUARTER
    lower_rows = upper_rows + HALF

    def place_of(row_tile, pair):
        return reversed_bits(pair, pair_bits) << row_bits | reversed_bits(row_tile, row_bits)

    def merged(first, second):
        return jnp.concatenate(
            [
                jnp.where(low, first[:, :LANES], second[:, :LANES]),
                jnp.where(low, first[:, LANES:], second[:, LANES:]),
            ],
            axis=1,
        )

    def spread(table):
        return jnp.concatenate(
            [
                jnp.take_along_axis(table, upper_rows, axis=1),
                jnp.take_along_axis(table, lower_rows, axis=1),
            ],
            axis=0,
        )

    def moved(place, count):
        count = count % index_bits
        return (place << count | place >> (index_bits - count)) & (2 * half_tiles - 1)

    def turned(mixed, level, source, place):
        real, imag = mixed[:, :LANES], mixed[:, LANES:]
        cosine, sine = tables[level, source, :, :LANES], tables[level, source, :, LANES:]
        after = 1 - level % 2
        states[after, place, :, :LANES] = real * cosine - imag * sine
        states[after, place, :, LANES:] = real * sine + imag * cosine

    def run(*accumulators):
        few = min(2 * TILE, row_tiles)

        rounds = row_tiles // few

        def charges_of(row_tile):
            if slabs:
                halves = [packed_ref[row_tile, half * TILE : (half + 1) * TILE] for half in range(2)]
                return jnp.concatenate(halves, axis=1)
            return packed_ref[pl.ds(pl.multiple_of(row_tile * TILE, TILE), TILE), : 2 * LANES]

        def speeds_of(row_tile):
            if slabs:
                raw = packed_ref[row_tile, 2 * TILE :].astype(F32)
                group = 2 * pairs
                own = lanes // group == row_index(lanes.shape)
                return [
                    repeated(jnp.where(own, raw[half : half + 1], 0.0), group) for half in range(2)
                ]
            speeds = packed_ref[row_tile * TILE : (row_tile + 1) * TILE, 2 * LANES :].astype(F32)
            return [speeds[: TILE // 2], speeds[TILE // 2 :]]

        for i in range(0, row_tiles, 2):
            both = [speeds_of(i), speeds_of(i + 1)]
            speeds_ref[i // 2] = jnp.concatenate(
                [jnp.concatenate([both[0][half], both[1][half]], axis=0) for half in range(2)],
                axis=1,
            ).astype(B16)

        def push_nodes(item):
            for order in range(2):
                both = [node_maps[item // rounds * 2 + side] for side in range(2)]
                pltpu.matmul_push_rhs(jnp.concatenate(both, axis=1), 0, order)

        def send_speeds(item, i):
            pltpu.matmul_acc_lhs(
                accumulators[2 * few + i // 2],
                speeds_ref[(item % rounds * few + i) // 2],
                load_staged_rhs=0 if i < 4 else None,
            )

        items = pairs // 2 * rounds
        push_nodes(0)
        for i in range(0, few, 2):
            send_speeds(0, i)

        @pl.loop(0, items)
        def _(item):
            duo, start = item // rounds, item % rounds * few
            base = place_of(start, 2 * duo)
            coming = jnp.minimum(item + 1, items - 1)
            for order in range(2):
                pltpu.matmul_push_rhs(leaf_maps[2 * duo + order], 1, order)
            for i in range(few):
                charges = charges_of(start + i)
                for order in range(2):
                    pltpu.matmul_acc_lhs(
                        accumulators[2 * i + order],
                        charges,
                        load_staged_rhs=1 if i == 0 else None,
                    )
            push_nodes(coming)
            for i in range(0, few, 2):
                turns = pltpu.matmul_pop(accumulators[2 * few + i // 2])
                send_speeds(coming, i)
                for order in range(2):
                    sine, cosine = sine_cosine(turns[:, order * LANES : (order + 1) * LANES])
                    for side in range(2):
                        place = base + place_of(i + side, order)
                        states_ref[0, place] = pltpu.matmul_pop(
                            accumulators[2 * (i + side) + order]
                        ).astype(B16)
                        here = slice(side * TILE // 2, (side + 1) * TILE // 2)
                        cosines, sines = spread(cosine[here]), spread(sine[here])
                        twice = cosines + cosines
                        last_cosines, last_sines = 1.0, 0.0
                        for level in range(levels):
                            spot = moved(base, rotations[level]) + moved(
                                place_of(i + side, order), rotations[level]
                            )
                            tables[level, spot, :, :LANES] = cosines.astype(B16)
                            tables[level, spot, :, LANES:] = sines.astype(B16)
                            cosines, last_cosines = twice * cosines - last_cosines, cosines
                            sines, last_sines = twice * sines - last_sines, sines

        for i in range(0, few, 2):
            pltpu.matmul_pop(accumulators[2 * few + i // 2])

        def load_maps(level):
            for order in range(2):
                pltpu.matmul_push_rhs(weights[2 * level + order], 0, order)

        def send(level, block, unit, fresh):
            number = block * units + unit
            first = states[level % 2, number]
            second = states[level % 2, number + half_tiles]
            for order in range(2):
                pltpu.matmul_acc_lhs(
                    accumulators[2 * unit + order],
                    merged(second, first) if order else merged(first, second),
                    load_staged_rhs=0 if fresh and unit == 0 else None,
                )

        def received(unit):
            return [
                pltpu.matmul_pop(accumulators[2 * unit + order]).astype(B16) for order in range(2)
            ]

        def finish(level, block, unit):
            one, other = received(unit)
            number = block * units + unit
            turned(merged(one, other), level, number, 2 * number)
            turned(merged(other, one), level, number + half_tiles, 2 * number + 1)

        def across_tiles(first_level, count):
            load_maps(first_level)
            for unit in range(units):
                send(first_level, 0, unit, True)

            @pl.loop(first_level, first_level + count)
            def _(level):
                @pl.loop(0, blocks - 1)
                def _(block):
                    for unit in range(units):
                        finish(level, block, unit)
                        send(level, block + 1, unit, False)

                next_level = jnp.minimum(level + 1, levels - 1)
                load_maps(next_level)
                for unit in range(units):
                    finish(level, blocks - 1, unit)
                    send(next_level, 0, unit, True)

            for unit in range(units):
                received(unit)

        def within_tiles(level, stride):
            upper = row_index((TILE, 2 * LANES)) // stride % 2 == 1
            mask = (lane_index((TILE, 2 * LANES)) % LANES < HALF) != upper

            def one_tile(place, fresh):
                own = states_ref[level % 2, place].astype(F32)
                other = jnp.where(
                    upper, pltpu.roll(own, stride, 0), pltpu.roll(own, TILE - stride, 0)
                )
                pre = []
                for order in range(2):
                    lhs = jnp.where(mask, other, own) if order else jnp.where(mask, own, other)
                    pltpu.matmul_acc_lhs(
                        accumulators[order], lhs.astype(B16), load_staged_rhs=0 if fresh else None
                    )
                    pre.append(pltpu.matmul_pop(accumulators[order]))
                turned(jnp.where(mask, *pre).astype(B16), level, place, place)

            one_tile(0, True)

            @pl.loop(1, 2 * half_tiles)
            def _(place):
                one_tile(place, False)

        fetches[0].wait()
        level = 0
        while level < levels:
            kind, stride = plan[level]
            if kind == "rows":
                load_maps(level)
                within_tiles(level, stride)
                level += 1
                continue
            count = 1
            while blocks > 3 and level + count < levels and plan[level + count][0] == kind:
                count += 1
            across_tiles(level, count)
            level += count

        fetches[1].wait()
        final = states_ref.at[levels % 2]
        share = row_tiles // 2
        @pl.loop(0, pairs)
        def _(pair):
            base = place_of(0, pair)
            for order in range(2):
                pltpu.matmul_push_rhs(weights[2 * levels + pair], 0, order)
            for i in range(share):
                for order in range(2):
                    pltpu.matmul_acc_lhs(
                        accumulators[2 * i + order],
                        final[base + place_of(order * share + i, 0)],
                        load_staged_rhs=0 if i == 0 else None,
                    )

        for i in range(share):
            for order in range(2):
                top = (order * share + i) * TILE
                out_ref[top : top + TILE, :] = pltpu.matmul_pop(
                    accumulators[2 * i + order]
                ).astype(B16)

    pl.run_scoped(
        run, *[pltpu.ACC(order)((TILE, 2 * LANES), F32) for _ in range(2 * units) for order in range(2)]
    )


def split_nodes(rank):
    nodes = np.cos(np.pi * (np.arange(QUARTER) + 0.5) / rank) / 2
    pieces = []
    rest = np.tile(nodes, LANES // QUARTER)
    for _ in range(3):
        piece = rest.astype(B16)
        pieces.append(piece.astype(np.float32))
        rest = rest - piece.astype(np.float64)
    return np.stack(pieces)


def level_plan(levels, local_levels, rows_per):
    plan = [("tiles", level) for level in range(local_levels)]
    stride = rows_per
    for _ in range(levels - local_levels):
        if stride < TILE:
            plan.append(("rows", stride))
        else:
            plan.append(("tiles", local_levels + (stride // TILE).bit_length() - 1))
        stride *= 2
    return tuple(plan)


def on_device(charges, source_order, velocity, leaf_weight, mixing, eval_weight, target_order):
    leaf = leaf_weight.shape[0] // 2
    width = leaf_weight.shape[1]
    boxes = charges.shape[1] // leaf
    group = LANES // leaf
    pairs = group // 2
    rows = boxes // group
    devices = lax.axis_size("wide") * lax.axis_size("narrow")
    rows_per = rows // devices
    levels = mixing.shape[0]
    local_levels = levels - (devices.bit_length() - 1)
    assert width == LANES and 1 << local_levels == pairs

    charge_rows = charges.reshape(2, rows, LANES).transpose(1, 0, 2).reshape(2 * rows, LANES)
    in_hbm = pl.BlockSpec(memory_space=pltpu.HBM)
    if rows_per == TILE:
        packed_shape = (devices, 2 * TILE + 8, LANES)
    else:
        packed_shape = (rows, 3 * LANES)
    packed = pl.pallas_call(
        functools.partial(pack_kernel, leaf),
        in_specs=[in_hbm] * 3,
        out_specs=in_hbm,
        out_shape=jax.ShapeDtypeStruct(packed_shape, B16),
        scratch_shapes=[
            pltpu.VMEM((2 * rows, LANES), F32),
            pltpu.VMEM((rows, LANES), jnp.int32),
            pltpu.VMEM((boxes // LANES, LANES), B16),
            pltpu.VMEM(packed_shape, B16),
            pltpu.SemaphoreType.DMA((STRIPS, 3)),
            pltpu.SemaphoreType.DMA((STRIPS,)),
        ],
        compiler_params=vmem(56),
        name="pack",
    )(charge_rows, source_order.reshape(rows, LANES), velocity.reshape(boxes // LANES, LANES))

    packed = lax.all_to_all(
        packed.reshape(devices, -1, packed_shape[-1]), AXES, 0, 0, tiled=True
    ).reshape(packed_shape)

    square = (2 * LANES, 2 * LANES)
    count = 2 * levels + pairs
    weights = pl.pallas_call(
        functools.partial(maps_kernel, leaf),
        grid=(1,),
        out_specs=pl.BlockSpec((count, *square), lambda step: (0, 0, 0)),
        out_shape=jax.ShapeDtypeStruct((max(count, ROOM), *square), B16),
        compiler_params=vmem(56),
        cost_estimate=pl.CostEstimate(flops=10**9, bytes_accessed=10**7, transcendentals=0),
        name="maps",
    )(mixing, eval_weight.T)

    tiles = rows // TILE * pairs
    values = pl.pallas_call(
        functools.partial(butterfly_kernel, level_plan(levels, local_levels, rows_per), leaf, pairs),
        out_shape=jax.ShapeDtypeStruct((rows, 2 * LANES), B16),
        in_specs=[pl.BlockSpec(memory_space=pltpu.VMEM)] * 3
        + [in_hbm],
        scratch_shapes=[
            pltpu.VMEM((pairs, *square), B16),
            pltpu.VMEM((pairs, 2 * LANES, LANES), B16),
            pltpu.VMEM((count, *square), B16),
            pltpu.SemaphoreType.DMA((2,)),
            pltpu.VMEM((2, tiles, TILE, 2 * LANES), B16),
            pltpu.VMEM((levels, tiles, TILE, 2 * LANES), B16),
            pltpu.VMEM((rows // TILE // 2, TILE, 2 * LANES), B16),
        ],
        compiler_params=vmem(40),
        name="butterfly",
    )(packed, leaf_weight, jnp.asarray(split_nodes(width // 2)), weights)

    values = lax.all_to_all(
        values.reshape(devices, rows_per, 2 * LANES), AXES, 0, 0, tiled=True
    ).reshape(rows, 2 * LANES)

    out = pl.pallas_call(
        functools.partial(unpack_kernel, leaf),
        out_specs=in_hbm,
        out_shape=jax.ShapeDtypeStruct((2 * rows, LANES), F32),
        scratch_shapes=[pltpu.VMEM((2 * rows, LANES), F32), pltpu.SemaphoreType.DMA((STRIPS,))],
        compiler_params=vmem(8),
        name="unpack",
    )(values, target_order.reshape(rows, LANES))
    return out.reshape(rows, 2, LANES).transpose(1, 0, 2).reshape(2, rows * LANES)


def solution(mesh):
    mapped = jax.shard_map(
        on_device,
        mesh=mesh,
        in_specs=(
            P(None, AXES),
            P(AXES),
            P(AXES),
            P(),
            P(),
            P(),
            P(AXES),
        ),
        out_specs=P(None, AXES),
        check_vma=False,
    )

    def program(*arrays):
        with jax.sharding.use_abstract_mesh(mesh.abstract_mesh):
            return mapped(*arrays)

    return program
```

```python
import functools
import math

import jax
import jax.numpy as jnp
import numpy as np
from jax import lax
from jax.experimental import pallas as pl
from jax.experimental.pallas import tpu as pltpu
from jax.sharding import PartitionSpec as P

LANES = 128
HALF = LANES // 2
QUARTER = LANES // 4
TILE = 16
AXES = ("wide", "narrow")
F32, B16 = jnp.float32, jnp.bfloat16
UNITS = 32
ROOM = 200
def vmem(mebibytes):
    return pltpu.CompilerParams(vmem_limit_bytes=mebibytes * 2**20)


STRIPS = 2


def lane_index(shape):
    return lax.broadcasted_iota(jnp.int32, shape, len(shape) - 1)


def row_index(shape):
    return lax.broadcasted_iota(jnp.int32, shape, len(shape) - 2)


def swapped(x):
    return pltpu.roll(x, HALF, 1)


def repeated(x, group):
    while group < LANES:
        x = x + pltpu.roll(x, group, 1)
        group *= 2
    return x


def odd_bits(number):
    for shift in (16, 8, 4, 2, 1):
        number = number ^ lax.shift_right_logical(number, shift)
    return number & 1


def device_number():
    return lax.axis_index("wide") * lax.axis_size("narrow") + lax.axis_index("narrow")


def pack_kernel(
    leaf, charges_hbm, order_hbm, velocity_hbm, out_hbm,
    charges_ref, order_ref, velocity_ref, out_ref, arrived, gone,
):
    slabs = len(out_ref.shape) == 3
    rows = order_ref.shape[0]
    strip = rows // STRIPS
    group = LANES // leaf
    pairs = ((charges_hbm, charges_ref), (order_hbm, order_ref), (velocity_hbm, velocity_ref))

    def part(ref, number):
        height = ref.shape[0] // STRIPS
        return ref.at[number * height : (number + 1) * height]

    fetches = [
        [
            pltpu.make_async_copy(part(far, number), part(near, number), arrived.at[number, kind])
            for kind, (far, near) in enumerate(pairs)
        ]
        for number in range(STRIPS)
    ]
    stores = [
        pltpu.make_async_copy(part(out_ref, number), part(out_hbm, number), gone.at[number])
        for number in range(STRIPS)
    ]
    for fetch in sum(fetches, []):
        fetch.start()
    odd = odd_bits(device_number()) == 1
    lanes = lane_index((strip, LANES))
    own = lanes // group == row_index((strip, LANES)) % leaf
    speed_lanes = lane_index((strip // leaf, LANES)) ^ jnp.where(odd, group // 2, 0)
    for number in range(STRIPS):
        for fetch in fetches[number]:
            fetch.wait()
        here = slice(number * strip, (number + 1) * strip)
        index = order_ref[here, :] + lanes // leaf * leaf
        for half in range(2):
            values = charges_ref[pl.ds(2 * number * strip + half, strip, stride=2), :]
            values = jnp.take_along_axis(values, index, axis=1)
            values = jnp.where(odd, swapped(values), values).astype(B16)
            if slabs:
                for slab in range(strip // TILE):
                    out_ref[number * (strip // TILE) + slab, half * TILE : (half + 1) * TILE, :] = (
                        values[slab * TILE : (slab + 1) * TILE]
                    )
            else:
                out_ref[here, half * LANES : (half + 1) * LANES] = values
        top = number * strip // leaf
        speeds = velocity_ref[top : top + strip // leaf, :].astype(F32)
        speeds = jnp.take_along_axis(speeds, speed_lanes, axis=1)
        if slabs:
            for slab in range(strip // TILE):
                first = slab * TILE // leaf
                own_rows = speeds[first // 8 * 8 : first // 8 * 8 + 8]
                if first % 8:
                    own_rows = pltpu.roll(own_rows, 8 - first % 8, 0)
                out_ref[number * (strip // TILE) + slab, 2 * TILE :, :] = jnp.where(
                    row_index((8, LANES)) < TILE // leaf, own_rows, 0.0
                ).astype(B16)
        else:
            speeds = jnp.broadcast_to(speeds[:, None, :], (strip // leaf, leaf, LANES))
            speeds = jnp.where(own, speeds.reshape(strip, LANES), 0.0)
            out_ref[here, 2 * LANES :] = repeated(speeds, group).astype(B16)
        stores[number].start()
    for store in stores:
        store.wait()


def unpack_kernel(leaf, values_ref, order_ref, out_hbm, out_ref, gone):
    rows = order_ref.shape[0]
    strip = rows // STRIPS
    odd = odd_bits(device_number()) == 1
    base = lane_index((strip, LANES)) // leaf * leaf ^ jnp.where(odd, HALF, 0)
    stores = []
    for number in range(STRIPS):
        here = slice(number * strip, (number + 1) * strip)
        index = order_ref[here, :] + base
        for half in range(2):
            values = values_ref[here, half * LANES : (half + 1) * LANES].astype(F32)
            out_ref[pl.ds(2 * number * strip + half, strip, stride=2), :] = jnp.take_along_axis(
                values, index, axis=1
            )
        wide = slice(2 * number * strip, 2 * (number + 1) * strip)
        stores.append(pltpu.make_async_copy(out_ref.at[wide], out_hbm.at[wide], gone.at[number]))
        stores[-1].start()
    for store in stores:
        store.wait()


def odd_pair(pair):
    return bin(pair).count("1") % 2 == 1


def mirrored(index):
    place = index % HALF
    return index - place + jnp.where(place < QUARTER, place, HALF + QUARTER - 1 - place)


def sign_of(index):
    return jnp.where((index >= HALF) & (index % HALF >= QUARTER), -1.0, 1.0)


def boxes_of_pair(pair, pairs):
    return (pair + pairs, pair) if odd_pair(pair) else (pair, pair + pairs)


def maps_kernel(leaf, mixing_ref, eval_ref, weights):
    levels = mixing_ref.shape[0]
    pairs = LANES // leaf // 2
    low = lane_index((HALF, LANES)) < HALF
    shape = (LANES, LANES)
    mirror = jnp.where(
        row_index(shape) == mirrored(lane_index(shape)), sign_of(lane_index(shape)), 0.0
    ).astype(B16)
    mirror_back = jnp.where(
        lane_index(shape) == mirrored(row_index(shape)), sign_of(row_index(shape)), 0.0
    ).astype(B16)

    order_of_four = [(target, source) for target in range(2) for source in range(2)]

    @pl.loop(0, levels)
    def _(level):
        four = jnp.concatenate([mixing_ref[level, *place] for place in order_of_four], axis=0)
        four = jnp.dot(four, mirror, preferred_element_type=F32).astype(B16)
        four = jnp.concatenate(
            [four[number * LANES : (number + 1) * LANES] for number in range(4)], axis=1
        )
        four = jnp.dot(mirror_back, four, preferred_element_type=F32)
        for source in range(2):
            both = [
                four[:, (2 * target + source) * LANES : (2 * target + source + 1) * LANES]
                for target in range(2)
            ]
            for part in range(2):
                to_first, to_second = (
                    matrix[part * HALF : (part + 1) * HALF] for matrix in both
                )
                first_far, second_far = swapped(to_first), swapped(to_second)
                for order in range(2):
                    top = part * LANES + (source ^ order) * HALF
                    place = weights.at[2 * level + order, top : top + HALF]
                    if order == 0:
                        real = jnp.where(low, to_first, second_far)
                        imag = jnp.where(low, first_far, to_second)
                    else:
                        real = jnp.where(low, to_second, first_far)
                        imag = jnp.where(low, second_far, to_first)
                    place[:, :LANES] = real.astype(B16)
                    place[:, LANES:] = imag.astype(B16)

    box_of_lane = lane_index((HALF, LANES)) // leaf
    slot = lane_index((2 * leaf, 2 * LANES))
    spread = (slot // LANES * leaf + slot % leaf == row_index((2 * leaf, 2 * LANES))).astype(B16)
    eval_rows = lax.dot_general(
        eval_ref[...], spread, (((0,), (0,)), ((), ())), preferred_element_type=F32
    ).astype(B16)
    eval_rows = jnp.dot(mirror_back, eval_rows, preferred_element_type=F32)
    for pair in range(pairs):
        for number, box in enumerate(boxes_of_pair(pair, pairs)):
            for part in range(2):
                top = (2 * part + number) * HALF
                for side in range(2):
                    lanes = slice(side * LANES, (side + 1) * LANES)
                    block = eval_rows[part * HALF : (part + 1) * HALF, lanes]
                    weights[2 * levels + pair, top : top + HALF, lanes] = jnp.where(
                        box_of_lane == box, block, 0.0
                    ).astype(B16)


def first_maps(leaf, pairs, leaf_ref, nodes_ref, leaf_maps, node_maps):
    group = 2 * pairs
    leaf_rows = leaf_ref[...].astype(F32)
    lanes = lane_index(leaf_rows.shape)
    leaf_rows = jnp.take_along_axis(leaf_rows, mirrored(lanes), axis=1) * sign_of(lanes)
    shape = (LANES, LANES)
    in_left = lane_index(shape) % HALF < QUARTER
    low = lane_index(shape) < HALF
    box_of_row = row_index(shape) // leaf
    node_row = row_index(shape)
    nodes = jnp.zeros(shape, F32)
    for piece in range(3):
        nodes = jnp.where(node_row // group == piece, nodes_ref[piece : piece + 1, :], nodes)
    tiles = [
        jnp.broadcast_to(
            leaf_rows[part * leaf : (part + 1) * leaf][None], (group, leaf, LANES)
        ).reshape(shape)
        for part in range(2)
    ]

    @pl.loop(0, pairs)
    def _(pair):
        odd = odd_bits(pair) == 1
        left = pair + jnp.where(odd, pairs, 0)
        right = pair + jnp.where(odd, 0, pairs)
        mine = node_row % group == jnp.where(in_left, left, right)
        for part in range(2):
            tiled = tiles[part]
            far = swapped(tiled)
            here = slice(part * LANES, (part + 1) * LANES)
            first, second = box_of_row == left, box_of_row == right
            leaf_maps[pair, here, :LANES] = jnp.where(
                low, jnp.where(first, tiled, 0.0), jnp.where(second, far, 0.0)
            ).astype(B16)
            leaf_maps[pair, here, LANES:] = jnp.where(
                low, jnp.where(first, far, 0.0), jnp.where(second, tiled, 0.0)
            ).astype(B16)
            node_maps[pair, here, :] = jnp.where(
                mine & (lane_index(shape) // HALF == part), nodes, 0.0
            ).astype(B16)


def sine_cosine(turns):
    u = turns - jnp.round(turns)
    w = u * u
    sin_terms = [(-1) ** i * math.pi ** (2 * i + 1) / math.factorial(2 * i + 1) for i in range(6)]
    cos_terms = [(-1) ** i * math.pi ** (2 * i) / math.factorial(2 * i) for i in range(6)]
    half_sin = jnp.full_like(w, sin_terms[-1])
    for term in sin_terms[-2::-1]:
        half_sin = half_sin * w + term
    half_sin = half_sin * u
    half_cos = jnp.full_like(w, cos_terms[-1])
    for term in cos_terms[-2::-1]:
        half_cos = half_cos * w + term
    twice = half_sin + half_sin
    return twice * half_cos, 1.0 - twice * half_sin


def reversed_bits(number, bits):
    return sum((number >> bit & 1) << (bits - 1 - bit) for bit in range(bits))


def butterfly_kernel(
    plan, leaf, pairs, packed_ref, leaf_ref, nodes_ref, weights_ref, out_ref,
    leaf_maps, node_maps, weights, arrived, states_ref, tables, speeds_ref,
):
    slabs = len(packed_ref.shape) == 3
    rows = packed_ref.shape[0] * (TILE if slabs else 1)
    levels = len(plan)
    states = pltpu.annotate(states_ref, no_hazard_no_deps=True)
    rotations = [sum(kind == "tiles" for kind, _ in plan[:level]) for level in range(levels)]
    row_tiles = rows // TILE
    row_bits, pair_bits = row_tiles.bit_length() - 1, pairs.bit_length() - 1
    half_tiles = states_ref.shape[1] // 2
    units = min(UNITS, half_tiles)
    blocks = half_tiles // units
    index_bits = row_bits + pair_bits
    bounds = (0, 2 * levels, 2 * levels + pairs)
    fetches = [
        pltpu.make_async_copy(
            weights_ref.at[start:stop], weights.at[start:stop], arrived.at[number]
        )
        for number, (start, stop) in enumerate(zip(bounds, bounds[1:]))
    ]
    for fetch in fetches:
        fetch.start()
    first_maps(leaf, pairs, leaf_ref, nodes_ref, leaf_maps, node_maps)

    low = lax.broadcasted_iota(jnp.int16, (TILE, LANES), 1) < jnp.int16(HALF)
    lanes = lane_index((TILE // 2, LANES))
    upper_rows = lanes // HALF * QUARTER + lanes % QUARTER
    lower_rows = upper_rows + HALF

    def place_of(row_tile, pair):
        return reversed_bits(pair, pair_bits) << row_bits | reversed_bits(row_tile, row_bits)

    def merged(first, second):
        return jnp.concatenate(
            [
                jnp.where(low, first[:, :LANES], second[:, :LANES]),
                jnp.where(low, first[:, LANES:], second[:, LANES:]),
            ],
            axis=1,
        )

    def spread(table):
        return jnp.concatenate(
            [
                jnp.take_along_axis(table, upper_rows, axis=1),
                jnp.take_along_axis(table, lower_rows, axis=1),
            ],
            axis=0,
        )

    def moved(place, count):
        count = count % index_bits
        return (place << count | place >> (index_bits - count)) & (2 * half_tiles - 1)

    def turned(mixed, level, source, place):
        real, imag = mixed[:, :LANES], mixed[:, LANES:]
        cosine, sine = tables[level, source, :, :LANES], tables[level, source, :, LANES:]
        after = 1 - level % 2
        states[after, place, :, :LANES] = real * cosine - imag * sine
        states[after, place, :, LANES:] = real * sine + imag * cosine

    def run(*accumulators):
        few = min(2 * TILE, row_tiles)

        rounds = row_tiles // few

        def charges_of(row_tile):
            if slabs:
                halves = [packed_ref[row_tile, half * TILE : (half + 1) * TILE] for half in range(2)]
                return jnp.concatenate(halves, axis=1)
            return packed_ref[pl.ds(pl.multiple_of(row_tile * TILE, TILE), TILE), : 2 * LANES]

        def speeds_of(row_tile):
            if slabs:
                raw = packed_ref[row_tile, 2 * TILE :].astype(F32)
                group = 2 * pairs
                own = lanes // group == row_index(lanes.shape)
                return [
                    repeated(jnp.where(own, raw[half : half + 1], 0.0), group) for half in range(2)
                ]
            speeds = packed_ref[row_tile * TILE : (row_tile + 1) * TILE, 2 * LANES :].astype(F32)
            return [speeds[: TILE // 2], speeds[TILE // 2 :]]

        for i in range(0, row_tiles, 2):
            both = [speeds_of(i), speeds_of(i + 1)]
            speeds_ref[i // 2] = jnp.concatenate(
                [jnp.concatenate([both[0][half], both[1][half]], axis=0) for half in range(2)],
                axis=1,
            ).astype(B16)

        def push_nodes(item):
            for order in range(2):
                both = [node_maps[item // rounds * 2 + side] for side in range(2)]
                pltpu.matmul_push_rhs(jnp.concatenate(both, axis=1), 0, order)

        def send_speeds(item, i):
            pltpu.matmul_acc_lhs(
                accumulators[2 * few + i // 2],
                speeds_ref[(item % rounds * few + i) // 2],
                load_staged_rhs=0 if i < 4 else None,
            )

        items = pairs // 2 * rounds
        push_nodes(0)
        for i in range(0, few, 2):
            send_speeds(0, i)

        @pl.loop(0, items)
        def _(item):
            duo, start = item // rounds, item % rounds * few
            base = place_of(start, 2 * duo)
            coming = jnp.minimum(item + 1, items - 1)
            for order in range(2):
                pltpu.matmul_push_rhs(leaf_maps[2 * duo + order], 1, order)
            for i in range(few):
                charges = charges_of(start + i)
                for order in range(2):
                    pltpu.matmul_acc_lhs(
                        accumulators[2 * i + order],
                        charges,
                        load_staged_rhs=1 if i == 0 else None,
                    )
            push_nodes(coming)
            for i in range(0, few, 2):
                turns = pltpu.matmul_pop(accumulators[2 * few + i // 2])
                send_speeds(coming, i)
                for order in range(2):
                    sine, cosine = sine_cosine(turns[:, order * LANES : (order + 1) * LANES])
                    for side in range(2):
                        place = base + place_of(i + side, order)
                        states_ref[0, place] = pltpu.matmul_pop(
                            accumulators[2 * (i + side) + order]
                        ).astype(B16)
                        here = slice(side * TILE // 2, (side + 1) * TILE // 2)
                        cosines, sines = spread(cosine[here]), spread(sine[here])
                        twice = cosines + cosines
                        last_cosines, last_sines = 1.0, 0.0
                        for level in range(levels):
                            spot = moved(base, rotations[level]) + moved(
                                place_of(i + side, order), rotations[level]
                            )
                            tables[level, spot, :, :LANES] = cosines.astype(B16)
                            tables[level, spot, :, LANES:] = sines.astype(B16)
                            cosines, last_cosines = twice * cosines - last_cosines, cosines
                            sines, last_sines = twice * sines - last_sines, sines

        for i in range(0, few, 2):
            pltpu.matmul_pop(accumulators[2 * few + i // 2])

        def load_maps(level):
            for order in range(2):
                pltpu.matmul_push_rhs(weights[2 * level + order], 0, order)

        def send(level, block, unit, fresh):
            number = block * units + unit
            first = states[level % 2, number]
            second = states[level % 2, number + half_tiles]
            for order in range(2):
                pltpu.matmul_acc_lhs(
                    accumulators[2 * unit + order],
                    merged(second, first) if order else merged(first, second),
                    load_staged_rhs=0 if fresh and unit == 0 else None,
                )

        def received(unit):
            return [
                pltpu.matmul_pop(accumulators[2 * unit + order]).astype(B16) for order in range(2)
            ]

        def finish(level, block, unit):
            one, other = received(unit)
            number = block * units + unit
            turned(merged(one, other), level, number, 2 * number)
            turned(merged(other, one), level, number + half_tiles, 2 * number + 1)

        def across_tiles(first_level, count):
            load_maps(first_level)
            for unit in range(units):
                send(first_level, 0, unit, True)

            @pl.loop(first_level, first_level + count)
            def _(level):
                @pl.loop(0, blocks - 1)
                def _(block):
                    for unit in range(units):
                        finish(level, block, unit)
                        send(level, block + 1, unit, False)

                next_level = jnp.minimum(level + 1, levels - 1)
                load_maps(next_level)
                for unit in range(units):
                    finish(level, blocks - 1, unit)
                    send(next_level, 0, unit, True)

            for unit in range(units):
                received(unit)

        def within_tiles(level, stride):
            upper = row_index((TILE, 2 * LANES)) // stride % 2 == 1
            mask = (lane_index((TILE, 2 * LANES)) % LANES < HALF) != upper

            def one_tile(place, fresh):
                own = states_ref[level % 2, place].astype(F32)
                other = jnp.where(
                    upper, pltpu.roll(own, stride, 0), pltpu.roll(own, TILE - stride, 0)
                )
                pre = []
                for order in range(2):
                    lhs = jnp.where(mask, other, own) if order else jnp.where(mask, own, other)
                    pltpu.matmul_acc_lhs(
                        accumulators[order], lhs.astype(B16), load_staged_rhs=0 if fresh else None
                    )
                    pre.append(pltpu.matmul_pop(accumulators[order]))
                turned(jnp.where(mask, *pre).astype(B16), level, place, place)

            one_tile(0, True)

            @pl.loop(1, 2 * half_tiles)
            def _(place):
                one_tile(place, False)

        fetches[0].wait()
        level = 0
        while level < levels:
            kind, stride = plan[level]
            if kind == "rows":
                load_maps(level)
                within_tiles(level, stride)
                level += 1
                continue
            count = 1
            while blocks > 3 and level + count < levels and plan[level + count][0] == kind:
                count += 1
            across_tiles(level, count)
            level += count

        fetches[1].wait()
        final = states_ref.at[levels % 2]
        share = row_tiles // 2
        @pl.loop(0, pairs)
        def _(pair):
            base = place_of(0, pair)
            for order in range(2):
                pltpu.matmul_push_rhs(weights[2 * levels + pair], 0, order)
            for i in range(share):
                for order in range(2):
                    pltpu.matmul_acc_lhs(
                        accumulators[2 * i + order],
                        final[base + place_of(order * share + i, 0)],
                        load_staged_rhs=0 if i == 0 else None,
                    )

        for i in range(share):
            for order in range(2):
                top = (order * share + i) * TILE
                out_ref[top : top + TILE, :] = pltpu.matmul_pop(
                    accumulators[2 * i + order]
                ).astype(B16)

    pl.run_scoped(
        run, *[pltpu.ACC(order)((TILE, 2 * LANES), F32) for _ in range(2 * units) for order in range(2)]
    )


def split_nodes(rank):
    nodes = np.cos(np.pi * (np.arange(QUARTER) + 0.5) / rank) / 2
    pieces = []
    rest = np.tile(nodes, LANES // QUARTER)
    for _ in range(3):
        piece = rest.astype(B16)
        pieces.append(piece.astype(np.float32))
        rest = rest - piece.astype(np.float64)
    return np.stack(pieces)


def level_plan(levels, local_levels, rows_per):
    plan = [("tiles", level) for level in range(local_levels)]
    stride = rows_per
    for _ in range(levels - local_levels):
        if stride < TILE:
            plan.append(("rows", stride))
        else:
            plan.append(("tiles", local_levels + (stride // TILE).bit_length() - 1))
        stride *= 2
    return tuple(plan)


def on_device(charges, source_order, velocity, leaf_weight, mixing, eval_weight, target_order):
    leaf = leaf_weight.shape[0] // 2
    width = leaf_weight.shape[1]
    boxes = charges.shape[1] // leaf
    group = LANES // leaf
    pairs = group // 2
    rows = boxes // group
    devices = lax.axis_size("wide") * lax.axis_size("narrow")
    rows_per = rows // devices
    levels = mixing.shape[0]
    local_levels = levels - (devices.bit_length() - 1)
    assert width == LANES and 1 << local_levels == pairs

    charge_rows = charges.reshape(2, rows, LANES).transpose(1, 0, 2).reshape(2 * rows, LANES)
    in_hbm = pl.BlockSpec(memory_space=pltpu.HBM)
    if rows_per == TILE:
        packed_shape = (devices, 2 * TILE + 8, LANES)
    else:
        packed_shape = (rows, 3 * LANES)
    packed = pl.pallas_call(
        functools.partial(pack_kernel, leaf),
        in_specs=[in_hbm] * 3,
        out_specs=in_hbm,
        out_shape=jax.ShapeDtypeStruct(packed_shape, B16),
        scratch_shapes=[
            pltpu.VMEM((2 * rows, LANES), F32),
            pltpu.VMEM((rows, LANES), jnp.int32),
            pltpu.VMEM((boxes // LANES, LANES), B16),
            pltpu.VMEM(packed_shape, B16),
            pltpu.SemaphoreType.DMA((STRIPS, 3)),
            pltpu.SemaphoreType.DMA((STRIPS,)),
        ],
        compiler_params=vmem(56),
        name="pack",
    )(charge_rows, source_order.reshape(rows, LANES), velocity.reshape(boxes // LANES, LANES))

    packed = lax.all_to_all(
        packed.reshape(devices, -1, packed_shape[-1]), AXES, 0, 0, tiled=True
    ).reshape(packed_shape)

    square = (2 * LANES, 2 * LANES)
    count = 2 * levels + pairs
    weights = pl.pallas_call(
        functools.partial(maps_kernel, leaf),
        grid=(1,),
        out_specs=pl.BlockSpec((count, *square), lambda step: (0, 0, 0)),
        out_shape=jax.ShapeDtypeStruct((max(count, ROOM), *square), B16),
        compiler_params=vmem(56),
        cost_estimate=pl.CostEstimate(flops=10**9, bytes_accessed=10**7, transcendentals=0),
        name="maps",
    )(mixing, eval_weight.T)

    tiles = rows // TILE * pairs
    values = pl.pallas_call(
        functools.partial(butterfly_kernel, level_plan(levels, local_levels, rows_per), leaf, pairs),
        out_shape=jax.ShapeDtypeStruct((rows, 2 * LANES), B16),
        in_specs=[pl.BlockSpec(memory_space=pltpu.VMEM)] * 3
        + [in_hbm],
        scratch_shapes=[
            pltpu.VMEM((pairs, *square), B16),
            pltpu.VMEM((pairs, 2 * LANES, LANES), B16),
            pltpu.VMEM((count, *square), B16),
            pltpu.SemaphoreType.DMA((2,)),
            pltpu.VMEM((2, tiles, TILE, 2 * LANES), B16),
            pltpu.VMEM((levels, tiles, TILE, 2 * LANES), B16),
            pltpu.VMEM((rows // TILE // 2, TILE, 2 * LANES), B16),
        ],
        compiler_params=vmem(40),
        name="butterfly",
    )(packed, leaf_weight, jnp.asarray(split_nodes(width // 2)), weights)

    values = lax.all_to_all(
        values.reshape(devices, rows_per, 2 * LANES), AXES, 0, 0, tiled=True
    ).reshape(rows, 2 * LANES)

    out = pl.pallas_call(
        functools.partial(unpack_kernel, leaf),
        out_specs=in_hbm,
        out_shape=jax.ShapeDtypeStruct((2 * rows, LANES), F32),
        scratch_shapes=[pltpu.VMEM((2 * rows, LANES), F32), pltpu.SemaphoreType.DMA((STRIPS,))],
        compiler_params=vmem(8),
        name="unpack",
    )(values, target_order.reshape(rows, LANES))
    return out.reshape(rows, 2, LANES).transpose(1, 0, 2).reshape(2, rows * LANES)


def solution(mesh):
    mapped = jax.shard_map(
        on_device,
        mesh=mesh,
        in_specs=(
            P(None, AXES),
            P(AXES),
            P(AXES),
            P(),
            P(),
            P(),
            P(AXES),
        ),
        out_specs=P(None, AXES),
        check_vma=False,
    )

    def program(*arrays):
        with jax.sharding.use_abstract_mesh(mesh.abstract_mesh):
            return mapped(*arrays)

    return program
```

```python
import functools
import math

import jax
import jax.numpy as jnp
import numpy as np
from jax import lax
from jax.experimental import pallas as pl
from jax.experimental.pallas import tpu as pltpu
from jax.sharding import PartitionSpec as P

LANES = 128
HALF = LANES // 2
QUARTER = LANES // 4
TILE = 16
AXES = ("wide", "narrow")
F32, B16 = jnp.float32, jnp.bfloat16
UNITS = 32
ROOM = 200
def vmem(mebibytes):
    return pltpu.CompilerParams(vmem_limit_bytes=mebibytes * 2**20)


STRIPS = 2


def lane_index(shape):
    return lax.broadcasted_iota(jnp.int32, shape, len(shape) - 1)


def row_index(shape):
    return lax.broadcasted_iota(jnp.int32, shape, len(shape) - 2)


def swapped(x):
    return pltpu.roll(x, HALF, 1)


def repeated(x, group):
    while group < LANES:
        x = x + pltpu.roll(x, group, 1)
        group *= 2
    return x


def odd_bits(number):
    for shift in (16, 8, 4, 2, 1):
        number = number ^ lax.shift_right_logical(number, shift)
    return number & 1


def device_number():
    return lax.axis_index("wide") * lax.axis_size("narrow") + lax.axis_index("narrow")


def pack_kernel(
    leaf, charges_hbm, order_hbm, velocity_hbm, out_hbm,
    charges_ref, order_ref, velocity_ref, out_ref, arrived, gone,
):
    slabs = len(out_ref.shape) == 3
    rows = order_ref.shape[0]
    strip = rows // STRIPS
    group = LANES // leaf
    pairs = ((charges_hbm, charges_ref), (order_hbm, order_ref), (velocity_hbm, velocity_ref))

    def part(ref, number):
        height = ref.shape[0] // STRIPS
        return ref.at[number * height : (number + 1) * height]

    fetches = [
        [
            pltpu.make_async_copy(part(far, number), part(near, number), arrived.at[number, kind])
            for kind, (far, near) in enumerate(pairs)
        ]
        for number in range(STRIPS)
    ]
    stores = [
        pltpu.make_async_copy(part(out_ref, number), part(out_hbm, number), gone.at[number])
        for number in range(STRIPS)
    ]
    for fetch in sum(fetches, []):
        fetch.start()
    odd = odd_bits(device_number()) == 1
    lanes = lane_index((strip, LANES))
    own = lanes // group == row_index((strip, LANES)) % leaf
    speed_lanes = lane_index((strip // leaf, LANES)) ^ jnp.where(odd, group // 2, 0)
    for number in range(STRIPS):
        for fetch in fetches[number]:
            fetch.wait()
        here = slice(number * strip, (number + 1) * strip)
        index = order_ref[here, :] + lanes // leaf * leaf
        for half in range(2):
            values = charges_ref[pl.ds(2 * number * strip + half, strip, stride=2), :]
            values = jnp.take_along_axis(values, index, axis=1)
            values = jnp.where(odd, swapped(values), values).astype(B16)
            if slabs:
                for slab in range(strip // TILE):
                    out_ref[number * (strip // TILE) + slab, half * TILE : (half + 1) * TILE, :] = (
                        values[slab * TILE : (slab + 1) * TILE]
                    )
            else:
                out_ref[here, half * LANES : (half + 1) * LANES] = values
        top = number * strip // leaf
        speeds = velocity_ref[top : top + strip // leaf, :].astype(F32)
        speeds = jnp.take_along_axis(speeds, speed_lanes, axis=1)
        if slabs:
            for slab in range(strip // TILE):
                first = slab * TILE // leaf
                own_rows = speeds[first // 8 * 8 : first // 8 * 8 + 8]
                if first % 8:
                    own_rows = pltpu.roll(own_rows, 8 - first % 8, 0)
                out_ref[number * (strip // TILE) + slab, 2 * TILE :, :] = jnp.where(
                    row_index((8, LANES)) < TILE // leaf, own_rows, 0.0
                ).astype(B16)
        else:
            speeds = jnp.broadcast_to(speeds[:, None, :], (strip // leaf, leaf, LANES))
            speeds = jnp.where(own, speeds.reshape(strip, LANES), 0.0)
            out_ref[here, 2 * LANES :] = repeated(speeds, group).astype(B16)
        stores[number].start()
    for store in stores:
        store.wait()


def unpack_kernel(leaf, values_ref, order_ref, out_hbm, out_ref, gone):
    rows = order_ref.shape[0]
    strip = rows // STRIPS
    odd = odd_bits(device_number()) == 1
    base = lane_index((strip, LANES)) // leaf * leaf ^ jnp.where(odd, HALF, 0)
    stores = []
    for number in range(STRIPS):
        here = slice(number * strip, (number + 1) * strip)
        index = order_ref[here, :] + base
        for half in range(2):
            values = values_ref[here, half * LANES : (half + 1) * LANES].astype(F32)
            out_ref[pl.ds(2 * number * strip + half, strip, stride=2), :] = jnp.take_along_axis(
                values, index, axis=1
            )
        wide = slice(2 * number * strip, 2 * (number + 1) * strip)
        stores.append(pltpu.make_async_copy(out_ref.at[wide], out_hbm.at[wide], gone.at[number]))
        stores[-1].start()
    for store in stores:
        store.wait()


def odd_pair(pair):
    return bin(pair).count("1") % 2 == 1


def mirrored(index):
    place = index % HALF
    return index - place + jnp.where(place < QUARTER, place, HALF + QUARTER - 1 - place)


def sign_of(index):
    return jnp.where((index >= HALF) & (index % HALF >= QUARTER), -1.0, 1.0)


def boxes_of_pair(pair, pairs):
    return (pair + pairs, pair) if odd_pair(pair) else (pair, pair + pairs)


def maps_kernel(leaf, mixing_ref, eval_ref, weights):
    levels = mixing_ref.shape[0]
    pairs = LANES // leaf // 2
    low = lane_index((HALF, LANES)) < HALF
    shape = (LANES, LANES)
    mirror = jnp.where(
        row_index(shape) == mirrored(lane_index(shape)), sign_of(lane_index(shape)), 0.0
    ).astype(B16)
    mirror_back = jnp.where(
        lane_index(shape) == mirrored(row_index(shape)), sign_of(row_index(shape)), 0.0
    ).astype(B16)

    order_of_four = [(target, source) for target in range(2) for source in range(2)]

    @pl.loop(0, levels)
    def _(level):
        four = jnp.concatenate([mixing_ref[level, *place] for place in order_of_four], axis=0)
        four = jnp.dot(four, mirror, preferred_element_type=F32).astype(B16)
        four = jnp.concatenate(
            [four[number * LANES : (number + 1) * LANES] for number in range(4)], axis=1
        )
        four = jnp.dot(mirror_back, four, preferred_element_type=F32)
        for source in range(2):
            both = [
                four[:, (2 * target + source) * LANES : (2 * target + source + 1) * LANES]
                for target in range(2)
            ]
            for part in range(2):
                to_first, to_second = (
                    matrix[part * HALF : (part + 1) * HALF] for matrix in both
                )
                first_far, second_far = swapped(to_first), swapped(to_second)
                for order in range(2):
                    top = part * LANES + (source ^ order) * HALF
                    place = weights.at[2 * level + order, top : top + HALF]
                    if order == 0:
                        real = jnp.where(low, to_first, second_far)
                        imag = jnp.where(low, first_far, to_second)
                    else:
                        real = jnp.where(low, to_second, first_far)
                        imag = jnp.where(low, second_far, to_first)
                    place[:, :LANES] = real.astype(B16)
                    place[:, LANES:] = imag.astype(B16)

    box_of_lane = lane_index((HALF, LANES)) // leaf
    slot = lane_index((2 * leaf, 2 * LANES))
    spread = (slot // LANES * leaf + slot % leaf == row_index((2 * leaf, 2 * LANES))).astype(B16)
    eval_rows = lax.dot_general(
        eval_ref[...], spread, (((0,), (0,)), ((), ())), preferred_element_type=F32
    ).astype(B16)
    eval_rows = jnp.dot(mirror_back, eval_rows, preferred_element_type=F32)
    for pair in range(pairs):
        for number, box in enumerate(boxes_of_pair(pair, pairs)):
            for part in range(2):
                top = (2 * part + number) * HALF
                for side in range(2):
                    lanes = slice(side * LANES, (side + 1) * LANES)
                    block = eval_rows[part * HALF : (part + 1) * HALF, lanes]
                    weights[2 * levels + pair, top : top + HALF, lanes] = jnp.where(
                        box_of_lane == box, block, 0.0
                    ).astype(B16)


def first_maps(leaf, pairs, leaf_ref, nodes_ref, leaf_maps, node_maps):
    group = 2 * pairs
    leaf_rows = leaf_ref[...].astype(F32)
    lanes = lane_index(leaf_rows.shape)
    leaf_rows = jnp.take_along_axis(leaf_rows, mirrored(lanes), axis=1) * sign_of(lanes)
    shape = (LANES, LANES)
    in_left = lane_index(shape) % HALF < QUARTER
    low = lane_index(shape) < HALF
    box_of_row = row_index(shape) // leaf
    node_row = row_index(shape)
    nodes = jnp.zeros(shape, F32)
    for piece in range(3):
        nodes = jnp.where(node_row // group == piece, nodes_ref[piece : piece + 1, :], nodes)
    tiles = [
        jnp.broadcast_to(
            leaf_rows[part * leaf : (part + 1) * leaf][None], (group, leaf, LANES)
        ).reshape(shape)
        for part in range(2)
    ]

    @pl.loop(0, pairs)
    def _(pair):
        odd = odd_bits(pair) == 1
        left = pair + jnp.where(odd, pairs, 0)
        right = pair + jnp.where(odd, 0, pairs)
        mine = node_row % group == jnp.where(in_left, left, right)
        for part in range(2):
            tiled = tiles[part]
            far = swapped(tiled)
            here = slice(part * LANES, (part + 1) * LANES)
            first, second = box_of_row == left, box_of_row == right
            leaf_maps[pair, here, :LANES] = jnp.where(
                low, jnp.where(first, tiled, 0.0), jnp.where(second, far, 0.0)
            ).astype(B16)
            leaf_maps[pair, here, LANES:] = jnp.where(
                low, jnp.where(first, far, 0.0), jnp.where(second, tiled, 0.0)
            ).astype(B16)
            node_maps[pair, here, :] = jnp.where(
                mine & (lane_index(shape) // HALF == part), nodes, 0.0
            ).astype(B16)


def fitted(function, degree):
    domain = [0.0, 0.25]
    series = np.polynomial.Chebyshev.interpolate(function, degree, domain=domain)
    return [float(term) for term in series.convert(kind=np.polynomial.Polynomial).coef]


def sine_cosine(turns):
    u = turns - jnp.round(turns)
    w = u * u
    sin_terms = fitted(lambda x: math.pi * np.sinc(np.sqrt(x)), 4)
    cos_terms = fitted(lambda x: np.cos(np.pi * np.sqrt(x)), 4)
    half_sin = jnp.full_like(w, sin_terms[-1])
    for term in sin_terms[-2::-1]:
        half_sin = half_sin * w + term
    half_sin = half_sin * u
    half_cos = jnp.full_like(w, cos_terms[-1])
    for term in cos_terms[-2::-1]:
        half_cos = half_cos * w + term
    twice = half_sin + half_sin
    return twice * half_cos, 1.0 - twice * half_sin


def reversed_bits(number, bits):
    return sum((number >> bit & 1) << (bits - 1 - bit) for bit in range(bits))


def butterfly_kernel(
    plan, leaf, pairs, packed_ref, leaf_ref, nodes_ref, weights_ref, out_ref,
    leaf_maps, node_maps, weights, arrived, states_ref, tables, speeds_ref,
):
    slabs = len(packed_ref.shape) == 3
    rows = packed_ref.shape[0] * (TILE if slabs else 1)
    levels = len(plan)
    states = pltpu.annotate(states_ref, no_hazard_no_deps=True)
    rotations = [sum(kind == "tiles" for kind, _ in plan[:level]) for level in range(levels)]
    row_tiles = rows // TILE
    row_bits, pair_bits = row_tiles.bit_length() - 1, pairs.bit_length() - 1
    half_tiles = states_ref.shape[1] // 2
    units = min(UNITS, half_tiles)
    blocks = half_tiles // units
    index_bits = row_bits + pair_bits
    bounds = (0, 2 * levels, 2 * levels + pairs)
    fetches = [
        pltpu.make_async_copy(
            weights_ref.at[start:stop], weights.at[start:stop], arrived.at[number]
        )
        for number, (start, stop) in enumerate(zip(bounds, bounds[1:]))
    ]
    for fetch in fetches:
        fetch.start()
    first_maps(leaf, pairs, leaf_ref, nodes_ref, leaf_maps, node_maps)

    low = lax.broadcasted_iota(jnp.int16, (TILE, LANES), 1) < jnp.int16(HALF)
    lanes = lane_index((TILE // 2, LANES))
    upper_rows = lanes // HALF * QUARTER + lanes % QUARTER
    lower_rows = upper_rows + HALF

    def place_of(row_tile, pair):
        return reversed_bits(pair, pair_bits) << row_bits | reversed_bits(row_tile, row_bits)

    def merged(first, second):
        return jnp.concatenate(
            [
                jnp.where(low, first[:, :LANES], second[:, :LANES]),
                jnp.where(low, first[:, LANES:], second[:, LANES:]),
            ],
            axis=1,
        )

    def spread(table):
        return jnp.concatenate(
            [
                jnp.take_along_axis(table, upper_rows, axis=1),
                jnp.take_along_axis(table, lower_rows, axis=1),
            ],
            axis=0,
        )

    def moved(place, count):
        count = count % index_bits
        return (place << count | place >> (index_bits - count)) & (2 * half_tiles - 1)

    def turned(mixed, level, source, place):
        real, imag = mixed[:, :LANES], mixed[:, LANES:]
        cosine, sine = tables[level, source, :, :LANES], tables[level, source, :, LANES:]
        after = 1 - level % 2
        states[after, place, :, :LANES] = real * cosine - imag * sine
        states[after, place, :, LANES:] = real * sine + imag * cosine

    def run(*accumulators):
        few = min(2 * TILE, row_tiles)

        rounds = row_tiles // few

        def charges_of(row_tile):
            if slabs:
                halves = [packed_ref[row_tile, half * TILE : (half + 1) * TILE] for half in range(2)]
                return jnp.concatenate(halves, axis=1)
            return packed_ref[pl.ds(pl.multiple_of(row_tile * TILE, TILE), TILE), : 2 * LANES]

        def speeds_of(row_tile):
            if slabs:
                raw = packed_ref[row_tile, 2 * TILE :].astype(F32)
                group = 2 * pairs
                own = lanes // group == row_index(lanes.shape)
                return [
                    repeated(jnp.where(own, raw[half : half + 1], 0.0), group) for half in range(2)
                ]
            speeds = packed_ref[row_tile * TILE : (row_tile + 1) * TILE, 2 * LANES :].astype(F32)
            return [speeds[: TILE // 2], speeds[TILE // 2 :]]

        for i in range(0, row_tiles, 2):
            both = [speeds_of(i), speeds_of(i + 1)]
            speeds_ref[i // 2] = jnp.concatenate(
                [jnp.concatenate([both[0][half], both[1][half]], axis=0) for half in range(2)],
                axis=1,
            ).astype(B16)

        def push_nodes(item):
            for order in range(2):
                both = [node_maps[item // rounds * 2 + side] for side in range(2)]
                pltpu.matmul_push_rhs(jnp.concatenate(both, axis=1), 0, order)

        def send_speeds(item, i):
            pltpu.matmul_acc_lhs(
                accumulators[2 * few + i // 2],
                speeds_ref[(item % rounds * few + i) // 2],
                load_staged_rhs=0 if i < 4 else None,
            )

        items = pairs // 2 * rounds
        push_nodes(0)
        for i in range(0, few, 2):
            send_speeds(0, i)

        @pl.loop(0, items)
        def _(item):
            duo, start = item // rounds, item % rounds * few
            base = place_of(start, 2 * duo)
            coming = jnp.minimum(item + 1, items - 1)
            for order in range(2):
                pltpu.matmul_push_rhs(leaf_maps[2 * duo + order], 1, order)
            for i in range(few):
                charges = charges_of(start + i)
                for order in range(2):
                    pltpu.matmul_acc_lhs(
                        accumulators[2 * i + order],
                        charges,
                        load_staged_rhs=1 if i == 0 else None,
                    )
            push_nodes(coming)
            for i in range(0, few, 2):
                turns = pltpu.matmul_pop(accumulators[2 * few + i // 2])
                send_speeds(coming, i)
                for order in range(2):
                    sine, cosine = sine_cosine(turns[:, order * LANES : (order + 1) * LANES])
                    for side in range(2):
                        place = base + place_of(i + side, order)
                        states_ref[0, place] = pltpu.matmul_pop(
                            accumulators[2 * (i + side) + order]
                        ).astype(B16)
                        here = slice(side * TILE // 2, (side + 1) * TILE // 2)
                        cosines, sines = spread(cosine[here]), spread(sine[here])
                        twice = cosines + cosines
                        last_cosines, last_sines = 1.0, 0.0
                        for level in range(levels):
                            spot = moved(base, rotations[level]) + moved(
                                place_of(i + side, order), rotations[level]
                            )
                            tables[level, spot, :, :LANES] = cosines.astype(B16)
                            tables[level, spot, :, LANES:] = sines.astype(B16)
                            cosines, last_cosines = twice * cosines - last_cosines, cosines
                            sines, last_sines = twice * sines - last_sines, sines

        for i in range(0, few, 2):
            pltpu.matmul_pop(accumulators[2 * few + i // 2])

        def load_maps(level):
            for order in range(2):
                pltpu.matmul_push_rhs(weights[2 * level + order], 0, order)

        def send(level, block, unit, fresh):
            number = block * units + unit
            first = states[level % 2, number]
            second = states[level % 2, number + half_tiles]
            for order in range(2):
                pltpu.matmul_acc_lhs(
                    accumulators[2 * unit + order],
                    merged(second, first) if order else merged(first, second),
                    load_staged_rhs=0 if fresh and unit == 0 else None,
                )

        def received(unit):
            return [
                pltpu.matmul_pop(accumulators[2 * unit + order]).astype(B16) for order in range(2)
            ]

        def finish(level, block, unit):
            one, other = received(unit)
            number = block * units + unit
            turned(merged(one, other), level, number, 2 * number)
            turned(merged(other, one), level, number + half_tiles, 2 * number + 1)

        def across_tiles(first_level, count):
            load_maps(first_level)
            for unit in range(units):
                send(first_level, 0, unit, True)

            @pl.loop(first_level, first_level + count)
            def _(level):
                @pl.loop(0, blocks - 1)
                def _(block):
                    for unit in range(units):
                        finish(level, block, unit)
                        send(level, block + 1, unit, False)

                next_level = jnp.minimum(level + 1, levels - 1)
                load_maps(next_level)
                for unit in range(units):
                    finish(level, blocks - 1, unit)
                    send(next_level, 0, unit, True)

            for unit in range(units):
                received(unit)

        def within_tiles(level, stride):
            upper = row_index((TILE, 2 * LANES)) // stride % 2 == 1
            mask = (lane_index((TILE, 2 * LANES)) % LANES < HALF) != upper

            def one_tile(place, fresh):
                own = states_ref[level % 2, place].astype(F32)
                other = jnp.where(
                    upper, pltpu.roll(own, stride, 0), pltpu.roll(own, TILE - stride, 0)
                )
                pre = []
                for order in range(2):
                    lhs = jnp.where(mask, other, own) if order else jnp.where(mask, own, other)
                    pltpu.matmul_acc_lhs(
                        accumulators[order], lhs.astype(B16), load_staged_rhs=0 if fresh else None
                    )
                    pre.append(pltpu.matmul_pop(accumulators[order]))
                turned(jnp.where(mask, *pre).astype(B16), level, place, place)

            one_tile(0, True)

            @pl.loop(1, 2 * half_tiles)
            def _(place):
                one_tile(place, False)

        fetches[0].wait()
        level = 0
        while level < levels:
            kind, stride = plan[level]
            if kind == "rows":
                load_maps(level)
                within_tiles(level, stride)
                level += 1
                continue
            count = 1
            while blocks > 3 and level + count < levels and plan[level + count][0] == kind:
                count += 1
            across_tiles(level, count)
            level += count

        fetches[1].wait()
        final = states_ref.at[levels % 2]
        share = row_tiles // 2
        @pl.loop(0, pairs)
        def _(pair):
            base = place_of(0, pair)
            for order in range(2):
                pltpu.matmul_push_rhs(weights[2 * levels + pair], 0, order)
            for i in range(share):
                for order in range(2):
                    pltpu.matmul_acc_lhs(
                        accumulators[2 * i + order],
                        final[base + place_of(order * share + i, 0)],
                        load_staged_rhs=0 if i == 0 else None,
                    )

        for i in range(share):
            for order in range(2):
                top = (order * share + i) * TILE
                out_ref[top : top + TILE, :] = pltpu.matmul_pop(
                    accumulators[2 * i + order]
                ).astype(B16)

    pl.run_scoped(
        run, *[pltpu.ACC(order)((TILE, 2 * LANES), F32) for _ in range(2 * units) for order in range(2)]
    )


def split_nodes(rank):
    nodes = np.cos(np.pi * (np.arange(QUARTER) + 0.5) / rank) / 2
    pieces = []
    rest = np.tile(nodes, LANES // QUARTER)
    for _ in range(3):
        piece = rest.astype(B16)
        pieces.append(piece.astype(np.float32))
        rest = rest - piece.astype(np.float64)
    return np.stack(pieces)


def level_plan(levels, local_levels, rows_per):
    plan = [("tiles", level) for level in range(local_levels)]
    stride = rows_per
    for _ in range(levels - local_levels):
        if stride < TILE:
            plan.append(("rows", stride))
        else:
            plan.append(("tiles", local_levels + (stride // TILE).bit_length() - 1))
        stride *= 2
    return tuple(plan)


def on_device(charges, source_order, velocity, leaf_weight, mixing, eval_weight, target_order):
    leaf = leaf_weight.shape[0] // 2
    width = leaf_weight.shape[1]
    boxes = charges.shape[1] // leaf
    group = LANES // leaf
    pairs = group // 2
    rows = boxes // group
    devices = lax.axis_size("wide") * lax.axis_size("narrow")
    rows_per = rows // devices
    levels = mixing.shape[0]
    local_levels = levels - (devices.bit_length() - 1)
    assert width == LANES and 1 << local_levels == pairs

    charge_rows = charges.reshape(2, rows, LANES).transpose(1, 0, 2).reshape(2 * rows, LANES)
    in_hbm = pl.BlockSpec(memory_space=pltpu.HBM)
    if rows_per == TILE:
        packed_shape = (devices, 2 * TILE + 8, LANES)
    else:
        packed_shape = (rows, 3 * LANES)
    packed = pl.pallas_call(
        functools.partial(pack_kernel, leaf),
        in_specs=[in_hbm] * 3,
        out_specs=in_hbm,
        out_shape=jax.ShapeDtypeStruct(packed_shape, B16),
        scratch_shapes=[
            pltpu.VMEM((2 * rows, LANES), F32),
            pltpu.VMEM((rows, LANES), jnp.int32),
            pltpu.VMEM((boxes // LANES, LANES), B16),
            pltpu.VMEM(packed_shape, B16),
            pltpu.SemaphoreType.DMA((STRIPS, 3)),
            pltpu.SemaphoreType.DMA((STRIPS,)),
        ],
        compiler_params=vmem(56),
        name="pack",
    )(charge_rows, source_order.reshape(rows, LANES), velocity.reshape(boxes // LANES, LANES))

    packed = lax.all_to_all(
        packed.reshape(devices, -1, packed_shape[-1]), AXES, 0, 0, tiled=True
    ).reshape(packed_shape)

    square = (2 * LANES, 2 * LANES)
    count = 2 * levels + pairs
    weights = pl.pallas_call(
        functools.partial(maps_kernel, leaf),
        grid=(1,),
        out_specs=pl.BlockSpec((count, *square), lambda step: (0, 0, 0)),
        out_shape=jax.ShapeDtypeStruct((max(count, ROOM), *square), B16),
        compiler_params=vmem(56),
        cost_estimate=pl.CostEstimate(flops=10**9, bytes_accessed=10**7, transcendentals=0),
        name="maps",
    )(mixing, eval_weight.T)

    tiles = rows // TILE * pairs
    values = pl.pallas_call(
        functools.partial(butterfly_kernel, level_plan(levels, local_levels, rows_per), leaf, pairs),
        out_shape=jax.ShapeDtypeStruct((rows, 2 * LANES), B16),
        in_specs=[pl.BlockSpec(memory_space=pltpu.VMEM)] * 3
        + [in_hbm],
        scratch_shapes=[
            pltpu.VMEM((pairs, *square), B16),
            pltpu.VMEM((pairs, 2 * LANES, LANES), B16),
            pltpu.VMEM((count, *square), B16),
            pltpu.SemaphoreType.DMA((2,)),
            pltpu.VMEM((2, tiles, TILE, 2 * LANES), B16),
            pltpu.VMEM((levels, tiles, TILE, 2 * LANES), B16),
            pltpu.VMEM((rows // TILE // 2, TILE, 2 * LANES), B16),
        ],
        compiler_params=vmem(40),
        name="butterfly",
    )(packed, leaf_weight, jnp.asarray(split_nodes(width // 2)), weights)

    values = lax.all_to_all(
        values.reshape(devices, rows_per, 2 * LANES), AXES, 0, 0, tiled=True
    ).reshape(rows, 2 * LANES)

    out = pl.pallas_call(
        functools.partial(unpack_kernel, leaf),
        out_specs=in_hbm,
        out_shape=jax.ShapeDtypeStruct((2 * rows, LANES), F32),
        scratch_shapes=[pltpu.VMEM((2 * rows, LANES), F32), pltpu.SemaphoreType.DMA((STRIPS,))],
        compiler_params=vmem(8),
        name="unpack",
    )(values, target_order.reshape(rows, LANES))
    return out.reshape(rows, 2, LANES).transpose(1, 0, 2).reshape(2, rows * LANES)


def solution(mesh):
    mapped = jax.shard_map(
        on_device,
        mesh=mesh,
        in_specs=(
            P(None, AXES),
            P(AXES),
            P(AXES),
            P(),
            P(),
            P(),
            P(AXES),
        ),
        out_specs=P(None, AXES),
        check_vma=False,
    )

    def program(*arrays):
        with jax.sharding.use_abstract_mesh(mesh.abstract_mesh):
            return mapped(*arrays)

    return program
```
